128 devices in a mesh: alpha: 32 (over x, z, core), beta: 4 (over y).
Axes of the slice: x: 4, y: 4, z: 4, core: 2. Of those that a mesh axis runs over, the one named last changes fastest.
Arguments:
- coeffs: bfloat16 [16384, 16384], P('alpha', 'beta'), may hold values from -6 to 6
- local_coupling: bfloat16 [2, 64, 256, 256], P(None, 'alpha'), may hold values from -0.25 to 0.25
- remote_coupling: bfloat16 [2, 64, 1, 256, 256], P(None, 'alpha'), may hold values from -0.25 to 0.25
- beta_coupling: bfloat16 [2, 16, 1024, 1024], P(None, 'beta'), may hold values from -0.125 to 0.125
- exc_rows: int32 [64, 1, 256], P('alpha'), may hold values from 0 to 16383, as said below
Outputs:
- sigma: bfloat16 [16384, 16384], P('alpha', 'beta')
The draws below stay inside these ranges and needn't reach their ends.
Inputs may be any that keep to these rules, and one draw needn't show every extreme that they name: `exc_rows`: each entry names a global alpha string. Of the 512 entries that belong to the blocks of one alpha index, at most 32 lie in the rows of any one alpha index; in every draw some alpha index holds exactly 32 of the entries of every alpha index.
All inputs are finite; a program needn't handle non-finite values.
Results may differ from the reference program's by a relative error of at most 0.0059.
Values may be sent and summed in bfloat16 or wider, within the bound.
No kernel may reach another device: no remote copies, remote signals or barrier semaphores. Data moves between devices by JAX's collectives and lax.ppermute only.
A program may use at most 128 MiB of HBM per device.

```python
import jax
import jax.numpy as jnp
from jax import lax

N = 16384
ABLK = 256
BORD = 1024
CHANNELS = 2
SLOTS = 1
OWNERS = 32
ROWS = 512
CAP = 32


def draw_exc_rows(key, part):
    subkeys = jax.random.split(key, 3)
    favor = jax.random.randint(subkeys[0], (OWNERS,), 0, 1 << 14)
    favored = jax.random.randint(subkeys[1], (), 0, OWNERS)
    favor = jnp.where(jnp.arange(OWNERS) == favored, 1 << 16, favor)

    def one_device(device_id):
        device_key = jax.random.fold_in(subkeys[2], device_id)
        pieces = jax.random.split(device_key, 3)
        jitter = jax.random.randint(pieces[0], (OWNERS, CAP), 0, 1 << 13)
        scores = (jitter + favor[:, None]).reshape(-1)
        ranked = jnp.argsort(-scores, stable=True)
        chosen = ranked[:ROWS * SLOTS]
        owner_of = (chosen // CAP).astype(jnp.int32)
        shuffled = jax.random.permutation(pieces[1], owner_of)
        offset = jax.random.randint(pieces[2], (ROWS * SLOTS,), 0, ROWS)
        return (shuffled * ROWS + offset).astype(jnp.int32)
    requests = jax.vmap(one_device)(jnp.arange(OWNERS, dtype=jnp.int32))
    requests = requests.reshape(OWNERS, ROWS // ABLK, SLOTS, ABLK)
    return requests.reshape(N // ABLK, SLOTS, ABLK)


def block_levels(stream_key, shape, cuts, smallest, top_value):
    gain, own = 1.0, jax.random.fold_in(stream_key, 6)
    for axis_at, parts in cuts:
        heights = jnp.exp(jax.random.uniform(jax.random.fold_in(own, axis_at), (parts,), jnp.float32, smallest / len(cuts), top_value / len(cuts)))
        gain = gain * jnp.repeat(heights, shape[axis_at] // parts).reshape([-1 if axis == axis_at else 1 for axis in range(len(shape))])
    return gain


def normal_values(key, dims, scale, limit, cuts=(), kind=jnp.bfloat16):
    drawn = scale * jax.random.normal(key, dims, jnp.float32)
    if cuts:
        drawn = drawn * block_levels(key, dims, cuts, -0.22, 0.18)
    return jnp.clip(drawn, -limit, limit).astype(kind)


def setup_inputs(seed: int = 0) -> dict:
    seeds = jax.random.split(jax.random.key(seed), 6)
    coeffs = normal_values(seeds[0], (N, N), 1.0, 6.0, ((0, 32), (1, 4)))
    local_coupling = normal_values(seeds[1], (CHANNELS, N // ABLK, ABLK, ABLK), (ABLK * (SLOTS + 1)) ** -0.5, 0.25, ((1, 32),))
    remote_coupling = normal_values(seeds[2], (CHANNELS, N // ABLK, SLOTS, ABLK, ABLK), (ABLK * (SLOTS + 1)) ** -0.5, 0.25, ((1, 32),))
    beta_coupling = normal_values(seeds[3], (CHANNELS, N // BORD, BORD, BORD), (BORD * CHANNELS) ** -0.5, 0.125, ((1, 4),))
    exc_rows = draw_exc_rows(jax.random.fold_in(seeds[5], 71), 0)
    return dict(coeffs=coeffs, local_coupling=local_coupling, remote_coupling=remote_coupling, beta_coupling=beta_coupling, exc_rows=exc_rows)


def reference(coeffs, local_coupling, remote_coupling, beta_coupling, exc_rows):
    beta_blocks = N // BORD
    beta_wide = beta_coupling.astype(jnp.float32)

    def one_block(block_id):
        own_rows = lax.dynamic_slice_in_dim(coeffs, block_id * ABLK, ABLK, 0)
        sources = exc_rows[block_id].reshape(-1)
        fetched = jnp.take(coeffs, sources, axis=0)
        accumulated = jnp.zeros((ABLK, N), jnp.float32)
        for channel in range(CHANNELS):
            near_mix = jnp.dot(local_coupling[channel, block_id], own_rows, preferred_element_type=jnp.float32).astype(jnp.bfloat16)
            far_coupling = jnp.transpose(remote_coupling[channel, block_id], (1, 0, 2)).reshape(ABLK, SLOTS * ABLK)
            far_mix = jnp.dot(far_coupling, fetched, preferred_element_type=jnp.float32).astype(jnp.bfloat16)
            for mixed in (near_mix, far_mix):
                split_cols = mixed.astype(jnp.float32).reshape(ABLK, beta_blocks, BORD)
                product = jnp.einsum("rkj,kij->rki", split_cols, beta_wide[channel])
                accumulated = accumulated + product.reshape(ABLK, N)
        return accumulated.astype(jnp.bfloat16)

    sigma_half = lax.map(one_block, jnp.arange(N // ABLK, dtype=jnp.int32)).reshape(N, N)
    return (sigma_half.astype(jnp.float32) + sigma_half.T.astype(jnp.float32)).astype(jnp.bfloat16)
```

```python
import functools

import jax
import jax.numpy as jnp
from jax import lax
from jax.experimental import pallas as pl
from jax.experimental.pallas import tpu as pltpu
from jax.sharding import Mesh, PartitionSpec as P

ABLK = 256
CAP = 32
ALPHA = ("x", "z", "core")
DEVICES = ("x", "z", "core", "y")
F32 = jnp.float32
BF16 = jnp.bfloat16
VMEM_BYTES = 56 * 1024 * 1024
PARTS = 2
STRIPES = 4


def iota(shape, axis):
    return lax.broadcasted_iota(jnp.int32, shape, axis)


def product(a, b):
    return jnp.dot(a, b, preferred_element_type=F32)


def product_nt(a, b):
    return lax.dot_general(a, b, (((1,), (1,)), ((), ())), preferred_element_type=F32)


def slots(wanted, row_count, owners):
    entries = wanted.shape[1]
    owner = wanted // row_count
    source_row = wanted - owner * row_count
    owner_hot = (iota((owners, entries), 0) == owner).astype(F32)
    before = (iota((entries, entries), 0) < iota((entries, entries), 1)).astype(F32)
    earlier = product(owner_hot.astype(BF16), before.astype(BF16))
    slot = jnp.sum(owner_hot * earlier, axis=0, keepdims=True).astype(jnp.int32)
    return owner, owner_hot, slot, source_row


def request_kernel(row_count, owners, wanted_ref, table_ref):
    owner, owner_hot, slot, source_row = slots(wanted_ref[...], row_count, owners)
    slot_hot = (iota((CAP, slot.shape[1]), 0) == slot).astype(F32).astype(BF16)
    high = source_row // 32
    low = source_row - high * 32
    table = 32.0 * product_nt((owner_hot * high.astype(F32)).astype(BF16), slot_hot)
    table = table + product_nt((owner_hot * low.astype(F32)).astype(BF16), slot_hot)
    table_ref[...] = table.astype(jnp.int32)


def select_kernel(row_count, owners, wanted_ref, select_ref):
    owner, _, slot, _ = slots(wanted_ref[...], row_count, owners)
    entries = slot.shape[1]
    flat = (owner * CAP + slot).astype(F32)
    diagonal = iota((entries, entries), 0) == iota((entries, entries), 1)
    column = jnp.sum(jnp.where(diagonal, flat, 0.0), axis=1, keepdims=True).astype(jnp.int32)
    select_ref[...] = (iota((entries, owners * CAP), 1) == column).astype(F32).astype(BF16)


def outgoing_kernel(incoming_ref, coeffs_ref, out_ref, hot_ref):
    owners = incoming_ref.shape[0]
    row_count = coeffs_ref.shape[0]

    @pl.when(pl.program_id(0) == 0)
    def _():
        places = owners * CAP
        table = incoming_ref[...]
        high = table // 32
        low = table - high * 32
        place_owner = (iota((places, owners), 0) // CAP == iota((places, owners), 1)).astype(F32).astype(BF16)
        spread = 32.0 * product(place_owner, high.astype(F32).astype(BF16))
        spread = spread + product(place_owner, low.astype(F32).astype(BF16))
        mine = iota((places, CAP), 0) % CAP == iota((places, CAP), 1)
        column = jnp.sum(jnp.where(mine, spread, 0.0), axis=1, keepdims=True).astype(jnp.int32)
        hot_ref[...] = (iota((places, row_count), 1) == column).astype(F32).astype(BF16)

    rows = product(hot_ref[...], coeffs_ref[...]).astype(BF16)
    out_ref[...] = rows.reshape(out_ref.shape)


def half_kernel(select_ref, local_ref, remote_ref, coeffs_ref, replies_ref, beta_ref, *out_refs):
    replies = replies_ref[...]
    replies = replies.reshape(replies.shape[0] * replies.shape[1], replies.shape[2])
    far_rows = product(select_ref[...], replies).astype(BF16)
    own_rows = coeffs_ref[...]
    total = None
    for channel in range(local_ref.shape[0]):
        mix = product(local_ref[channel, 0], own_rows) + product(remote_ref[channel, 0, 0], far_rows)
        term = product_nt(mix.astype(BF16), beta_ref[channel, 0])
        total = term if total is None else total + term
    total = total.astype(BF16)
    stripe, width = out_refs[0].shape[1:]
    for index, out_ref in enumerate(out_refs):
        for piece in range(out_ref.shape[0]):
            out_ref[piece] = total[index * stripe:(index + 1) * stripe, piece * width:(piece + 1) * width]


def collect_kernel(order_ref, *refs):
    *in_refs, out_ref, sems = refs
    copies = []
    for index, in_ref in enumerate(in_refs):
        copies.append(pltpu.make_async_copy(in_ref, out_ref.at[order_ref[index]], sems.at[index]))
        copies[-1].start()
    for copy in copies:
        copy.wait()


def final_kernel(turn_ref, *refs):
    half_refs = refs[:PARTS * STRIPES]
    mirror_refs = refs[PARTS * STRIPES:PARTS * STRIPES + PARTS]
    out_ref = refs[-1]
    stripe = half_refs[0].shape[1]
    part_rows = stripe * STRIPES
    turned = []
    for part in range(PARTS):
        pieces = [mirror_refs[part][(turn_ref[0] + j) % STRIPES, 0] for j in range(STRIPES)]
        turned.append(jnp.concatenate(pieces, axis=0).T)
    mirror = jnp.concatenate(turned, axis=1)
    for part in range(PARTS):
        for j in range(STRIPES):
            low = part * part_rows + j * stripe
            own = half_refs[part * STRIPES + j][0]
            out_ref[low:low + stripe, :] = (own.astype(F32) + mirror[low:low + stripe].astype(F32)).astype(BF16)


def params(**more):
    return pltpu.CompilerParams(vmem_limit_bytes=VMEM_BYTES, **more)


def swap_pairs(sizes, j):
    nx, nz, nc, ny = sizes
    pairs = []
    for x in range(nx):
        for z in range(nz):
            for core in range(nc):
                for y in range(ny):
                    source = ((x * nz + z) * nc + core) * ny + y
                    target = ((((x + y + j) % nx) * nz + z) * nc + core) * ny + x
                    pairs.append((source, target))
    return pairs


def on_device(sizes, coeffs, local_coupling, remote_coupling, beta_coupling, exc_rows):
    nx, nz, nc, ny = sizes
    owners = nx * nz * nc
    row_count, col_count = coeffs.shape
    channels, beta_blocks, order, _ = beta_coupling.shape
    my_x, my_y = lax.axis_index("x"), lax.axis_index("y")
    wanted = exc_rows.reshape(1, row_count)
    places = owners * CAP

    table = pl.pallas_call(
        functools.partial(request_kernel, row_count, owners),
        out_shape=jax.ShapeDtypeStruct((owners, CAP), jnp.int32),
        name="requests",
    )(wanted)
    incoming = lax.all_to_all(table, ALPHA, split_axis=0, concat_axis=0, tiled=True)
    select = pl.pallas_call(
        functools.partial(select_kernel, row_count, owners),
        out_shape=jax.ShapeDtypeStruct((row_count, places), BF16),
        compiler_params=params(),
        name="select",
    )(wanted)
    width = 512
    outgoing = pl.pallas_call(
        outgoing_kernel,
        grid=(col_count // width,),
        in_specs=[
            pl.BlockSpec((owners, CAP), lambda i: (0, 0)),
            pl.BlockSpec((row_count, width), lambda i: (0, i)),
        ],
        out_specs=pl.BlockSpec((owners, CAP, width), lambda i: (0, 0, i)),
        out_shape=jax.ShapeDtypeStruct((owners, CAP, col_count), BF16),
        scratch_shapes=[pltpu.VMEM((places, row_count), BF16)],
        compiler_params=params(),
        name="outgoing",
    )(incoming, coeffs)
    replies = lax.all_to_all(outgoing, ALPHA, split_axis=0, concat_axis=0, tiled=True)

    part_rows = row_count // PARTS
    stripe = part_rows // STRIPES
    pieces = nz * nc
    piece = col_count // pieces
    halves, mirrors = [], []
    for part in range(PARTS):
        half = pl.pallas_call(
            half_kernel,
            grid=(beta_blocks,),
            in_specs=[
                pl.BlockSpec((ABLK, places), lambda k, part=part: (part, 0)),
                pl.BlockSpec((channels, 1, ABLK, ABLK), lambda k, part=part: (0, part, 0, 0)),
                pl.BlockSpec((channels, 1, 1, ABLK, ABLK), lambda k, part=part: (0, part, 0, 0, 0)),
                pl.BlockSpec((ABLK, order), lambda k, part=part: (part, k)),
                pl.BlockSpec((owners, CAP, order), lambda k: (0, 0, k)),
                pl.BlockSpec((channels, 1, order, order), lambda k: (0, k, 0, 0)),
            ],
            out_specs=[pl.BlockSpec((order // piece, stripe, piece), lambda k: (k, 0, 0))] * STRIPES,
            out_shape=[jax.ShapeDtypeStruct((pieces, stripe, piece), BF16)] * STRIPES,
            compiler_params=params(),
            cost_estimate=pl.CostEstimate(flops=9 * 10**9, bytes_accessed=30 * 2**20, transcendentals=0),
            name="half",
        )(select, local_coupling, remote_coupling, coeffs, replies, beta_coupling)
        halves.append(half)
    for part in range(PARTS):
        moved = [lax.ppermute(halves[part][j], DEVICES, swap_pairs(sizes, j)) for j in range(STRIPES)]
        target = (my_x - my_y - jnp.arange(STRIPES, dtype=jnp.int32)) % nx
        grouped = pl.pallas_call(
            collect_kernel,
            grid_spec=pltpu.PrefetchScalarGridSpec(
                num_scalar_prefetch=1,
                grid=(1,),
                in_specs=[pl.BlockSpec(memory_space=pl.ANY)] * STRIPES,
                out_specs=pl.BlockSpec(memory_space=pl.ANY),
                scratch_shapes=[pltpu.SemaphoreType.DMA((STRIPES,))],
            ),
            out_shape=jax.ShapeDtypeStruct((nx, pieces, stripe, piece), BF16),
            name="collect",
        )(target, *moved)
        grouped = grouped.reshape(owners, stripe, piece)
        mirrored = lax.all_to_all(grouped, ALPHA, split_axis=0, concat_axis=0, tiled=True)
        mirrors.append(mirrored.reshape(nx, pieces, stripe, piece))

    turn = ((my_x + my_y) % nx).astype(jnp.int32).reshape(1)
    return pl.pallas_call(
        final_kernel,
        grid_spec=pltpu.PrefetchScalarGridSpec(
            num_scalar_prefetch=1,
            grid=(pieces,),
            in_specs=[pl.BlockSpec((1, stripe, piece), lambda i, _: (i, 0, 0))] * (PARTS * STRIPES)
            + [pl.BlockSpec((nx, 1, stripe, piece), lambda i, _: (0, i, 0, 0))] * PARTS,
            out_specs=pl.BlockSpec((row_count, piece), lambda i, _: (0, i)),
        ),
        out_shape=jax.ShapeDtypeStruct((row_count, col_count), BF16),
        compiler_params=params(),
        name="final",
    )(turn, *halves[0], *halves[1], *mirrors)


def solution(mesh):
    sizes = (4, 4, 2, 4)
    cube = Mesh(mesh.devices.reshape(sizes), DEVICES)
    return jax.shard_map(
        functools.partial(on_device, sizes),
        mesh=cube,
        in_specs=(
            P(ALPHA, "y"),
            P(None, ALPHA, None, None),
            P(None, ALPHA, None, None, None),
            P(None, "y", None, None),
            P(ALPHA, None, None),
        ),
        out_specs=P(ALPHA, "y"),
        check_vma=False,
    )
```

```python
import functools

import jax
import jax.numpy as jnp
from jax import lax
from jax.experimental import pallas as pl
from jax.experimental.pallas import tpu as pltpu
from jax.sharding import Mesh, PartitionSpec as P

ABLK = 256
CAP = 32
ALPHA = ("x", "z", "core")
DEVICES = ("x", "z", "core", "y")
F32 = jnp.float32
BF16 = jnp.bfloat16
VMEM_BYTES = 56 * 1024 * 1024
STRIPES = 4


def iota(shape, axis):
    return lax.broadcasted_iota(jnp.int32, shape, axis)


def product(a, b):
    return jnp.dot(a, b, preferred_element_type=F32)


def product_nt(a, b):
    return lax.dot_general(a, b, (((1,), (1,)), ((), ())), preferred_element_type=F32)


def slots(wanted, row_count, owners):
    entries = wanted.shape[1]
    owner = wanted // row_count
    source_row = wanted - owner * row_count
    owner_hot = (iota((owners, entries), 0) == owner).astype(F32)
    before = (iota((entries, entries), 0) < iota((entries, entries), 1)).astype(F32)
    earlier = product(owner_hot.astype(BF16), before.astype(BF16))
    slot = jnp.sum(owner_hot * earlier, axis=0, keepdims=True).astype(jnp.int32)
    return owner, owner_hot, slot, source_row


def request_kernel(row_count, owners, wanted_ref, table_ref):
    owner, owner_hot, slot, source_row = slots(wanted_ref[...], row_count, owners)
    slot_hot = (iota((CAP, slot.shape[1]), 0) == slot).astype(F32).astype(BF16)
    high = source_row // 32
    low = source_row - high * 32
    table = 32.0 * product_nt((owner_hot * high.astype(F32)).astype(BF16), slot_hot)
    table = table + product_nt((owner_hot * low.astype(F32)).astype(BF16), slot_hot)
    table_ref[...] = table.astype(jnp.int32)


def select_kernel(row_count, owners, wanted_ref, select_ref):
    owner, _, slot, _ = slots(wanted_ref[...], row_count, owners)
    entries = slot.shape[1]
    flat = (owner * CAP + slot).astype(F32)
    diagonal = iota((entries, entries), 0) == iota((entries, entries), 1)
    column = jnp.sum(jnp.where(diagonal, flat, 0.0), axis=1, keepdims=True).astype(jnp.int32)
    select_ref[...] = (iota((entries, owners * CAP), 1) == column).astype(F32).astype(BF16)


def outgoing_kernel(sizes, incoming_ref, coeffs_ref, out_ref, hot_ref):
    nx, nz, nc, _ = sizes
    owners = nx * nz * nc
    row_count = coeffs_ref.shape[0]
    group = nx * nc * CAP

    @pl.when((pl.program_id(0) == 0) & (pl.program_id(1) == 0))
    def _():
        places = owners * CAP
        table = incoming_ref[...]
        high = table // 32
        low = table - high * 32
        place = iota((places, owners), 0)
        owner = (place % group // (nc * CAP)) * (nz * nc) + place // group * nc + place % (nc * CAP) // CAP
        place_owner = (owner == iota((places, owners), 1)).astype(F32).astype(BF16)
        spread = 32.0 * product(place_owner, high.astype(F32).astype(BF16))
        spread = spread + product(place_owner, low.astype(F32).astype(BF16))
        mine = iota((places, CAP), 0) % CAP == iota((places, CAP), 1)
        column = jnp.sum(jnp.where(mine, spread, 0.0), axis=1, keepdims=True).astype(jnp.int32)
        hot_ref[...] = (iota((places, row_count), 1) == column).astype(F32).astype(BF16)

    start = pl.multiple_of(pl.program_id(0) * group, group)
    rows = product(hot_ref[pl.ds(start, group), :], coeffs_ref[...]).astype(BF16)
    out_ref[...] = rows.reshape(out_ref.shape)


def half_kernel(_, select_ref, local_ref, remote_ref, coeffs_ref, replies_ref, beta_ref, *refs):
    *out_refs, mix_ref = refs
    channels, blocks = local_ref.shape[:2]

    @pl.when(pl.program_id(0) == 0)
    def _():
        replies = replies_ref[...]
        replies = replies.reshape(replies.shape[0] * replies.shape[1], replies.shape[2])
        far_rows = product(select_ref[...], replies).astype(BF16)
        for block in range(blocks):
            low, high = block * ABLK, (block + 1) * ABLK
            own_rows = coeffs_ref[low:high, :]
            for channel in range(channels):
                mix = product(local_ref[channel, block], own_rows)
                mix = mix + product(remote_ref[channel, block, 0], far_rows[low:high])
                mix_ref[channel, low:high, :] = mix.astype(BF16)

    total = None
    for channel in range(channels):
        term = product_nt(beta_ref[channel, 0], mix_ref[channel])
        total = term if total is None else total + term
    total = total.astype(BF16)
    stripe = out_refs[0].shape[2]
    for index, out_ref in enumerate(out_refs):
        out_ref[0] = total[:, index * stripe:(index + 1) * stripe]


def own_kernel(*refs):
    *in_refs, out_ref = refs
    stripe = in_refs[0].shape[2]
    for index, in_ref in enumerate(in_refs):
        out_ref[index * stripe:(index + 1) * stripe, :] = in_ref[0].T


def collect_kernel(order_ref, *refs):
    *in_refs, out_ref = refs
    for index, in_ref in enumerate(in_refs):
        out_ref[order_ref[index % STRIPES], 0, index // STRIPES] = in_ref[0]


def final_kernel(turn_ref, *refs):
    own_refs, mirror_refs, out_ref = refs[:4], refs[4:6], refs[6]
    stripe = mirror_refs[0].shape[4]
    for distance, own_ref in enumerate(own_refs):
        back = -distance % len(own_refs)

        @pl.when(pl.program_id(0) == distance)
        def _(own_ref=own_ref, mirror_ref=mirror_refs[back // 2]):
            for j in range(STRIPES):
                cols = slice(j * stripe, (j + 1) * stripe)
                mirror = mirror_ref[(turn_ref[4] + j) % STRIPES, 0, 0]
                out_ref[:, cols] = (own_ref[:, cols].astype(F32) + mirror.astype(F32)).astype(BF16)


def params(**more):
    return pltpu.CompilerParams(vmem_limit_bytes=VMEM_BYTES, **more)


def estimate(flops, mebibytes):
    return pl.CostEstimate(flops=flops, bytes_accessed=mebibytes * 2**20, transcendentals=0)


def swap_pairs(sizes, j, distance):
    nx, nz, nc, ny = sizes
    pairs = []
    for x in range(nx):
        for z in range(nz):
            for core in range(nc):
                for y in range(ny):
                    source = ((x * nz + z) * nc + core) * ny + y
                    target = ((((x + y + j) % nx) * nz + (z + distance) % nz) * nc + core) * ny + x
                    pairs.append((source, target))
    return pairs


def on_device(sizes, coeffs, local_coupling, remote_coupling, beta_coupling, exc_rows):
    nx, nz, nc, ny = sizes
    owners = nx * nz * nc
    row_count, col_count = coeffs.shape
    channels, beta_blocks, order, _ = beta_coupling.shape
    blocks = row_count // ABLK
    my_x, my_y, my_z = lax.axis_index("x"), lax.axis_index("y"), lax.axis_index("z")
    wanted = exc_rows.reshape(1, row_count)
    places = owners * CAP
    chunks = 2
    per_chunk = beta_blocks // chunks
    piece = order // nc
    stripe = row_count // STRIPES

    table = pl.pallas_call(
        functools.partial(request_kernel, row_count, owners),
        out_shape=jax.ShapeDtypeStruct((owners, CAP), jnp.int32),
        name="requests",
    )(wanted)
    incoming = lax.all_to_all(table, ALPHA, split_axis=0, concat_axis=0, tiled=True)
    select = pl.pallas_call(
        functools.partial(select_kernel, row_count, owners),
        out_shape=jax.ShapeDtypeStruct((row_count, places), BF16),
        compiler_params=params(),
        name="select",
    )(wanted)
    column = (my_z + jnp.arange(nz, dtype=jnp.int32)) % nz
    turn = jnp.concatenate([column, ((my_x + my_y) % nx).reshape(1)]).astype(jnp.int32)
    target = (my_x - my_y - jnp.arange(STRIPES, dtype=jnp.int32)) % nx

    replies = []
    for chunk in range(chunks):
        outgoing = pl.pallas_call(
            functools.partial(outgoing_kernel, sizes),
            grid=(nz, per_chunk),
            in_specs=[
                pl.BlockSpec((owners, CAP), lambda z, i: (0, 0)),
                pl.BlockSpec((row_count, order), lambda z, i, chunk=chunk: (0, (z + chunk * per_chunk + i) % nz)),
            ],
            out_specs=pl.BlockSpec((nx, 1, nc, CAP, order), lambda z, i: (0, z, 0, 0, i)),
            out_shape=jax.ShapeDtypeStruct((nx, nz, nc, CAP, per_chunk * order), BF16),
            scratch_shapes=[pltpu.VMEM((places, row_count), BF16)],
            compiler_params=params(),
            cost_estimate=estimate(2 * 10**9, 10),
            name="outgoing",
        )(incoming, coeffs)
        outgoing = outgoing.reshape(owners, CAP, per_chunk * order)
        replies.append(lax.all_to_all(outgoing, ALPHA, split_axis=0, concat_axis=0, tiled=True))

    owns, mirrors = [], []
    for chunk in range(chunks):
        moved = []
        for i in range(per_chunk):
            distance = chunk * per_chunk + i
            half = pl.pallas_call(
                half_kernel,
                grid_spec=pltpu.PrefetchScalarGridSpec(
                    num_scalar_prefetch=1,
                    grid=(nc,),
                    in_specs=[
                        pl.BlockSpec((row_count, places), lambda n, s: (0, 0)),
                        pl.BlockSpec((channels, blocks, ABLK, ABLK), lambda n, s: (0, 0, 0, 0)),
                        pl.BlockSpec((channels, blocks, 1, ABLK, ABLK), lambda n, s: (0, 0, 0, 0, 0)),
                        pl.BlockSpec((row_count, order), lambda n, s, d=distance: (0, s[d])),
                        pl.BlockSpec((owners, CAP, order), lambda n, s, i=i: (0, 0, i)),
                        pl.BlockSpec((channels, 1, piece, order), lambda n, s, d=distance: (0, s[d], n, 0)),
                    ],
                    out_specs=[pl.BlockSpec((1, piece, stripe), lambda n, s: (n, 0, 0))] * STRIPES,
                    scratch_shapes=[pltpu.VMEM((channels, row_count, order), BF16)],
                ),
                out_shape=[jax.ShapeDtypeStruct((nc, piece, stripe), BF16)] * STRIPES,
                compiler_params=params(),
                cost_estimate=estimate(4 * 10**9, 12),
                name="half",
            )(turn, select, local_coupling, remote_coupling, coeffs, replies[chunk], beta_coupling)
            owns.append(
                pl.pallas_call(
                    own_kernel,
                    grid=(nc,),
                    in_specs=[pl.BlockSpec((1, piece, stripe), lambda n: (n, 0, 0))] * STRIPES,
                    out_specs=pl.BlockSpec((row_count, piece), lambda n: (0, n)),
                    out_shape=jax.ShapeDtypeStruct((row_count, order), BF16),
                    compiler_params=params(),
                    cost_estimate=estimate(10**9, 2),
                    name="own",
                )(*half)
            )
            moved += [
                lax.ppermute(half[j], DEVICES, swap_pairs(sizes, j, distance)) for j in range(STRIPES)
            ]
        grouped = pl.pallas_call(
            collect_kernel,
            grid_spec=pltpu.PrefetchScalarGridSpec(
                num_scalar_prefetch=1,
                grid=(nc,),
                in_specs=[pl.BlockSpec((1, piece, stripe), lambda n, s: (n, 0, 0))] * (STRIPES * per_chunk),
                out_specs=pl.BlockSpec((nx, 1, per_chunk, piece, stripe), lambda n, s: (0, n, 0, 0, 0)),
            ),
            out_shape=jax.ShapeDtypeStruct((nx, nc, per_chunk, piece, stripe), BF16),
            compiler_params=params(),
            name="collect",
        )(target, *moved)
        grouped = grouped.reshape(nx * nc, per_chunk * piece, stripe)
        mirrored = lax.all_to_all(grouped, ("x", "core"), split_axis=0, concat_axis=0, tiled=True)
        mirrors.append(mirrored.reshape(nx, nc, per_chunk, piece, stripe))

    def mirror_index(chunk):
        def index(d, n, s):
            back = -d % nz
            return (0, n, jnp.where(back // per_chunk == chunk, back % per_chunk, 0), 0, 0)
        return index

    return pl.pallas_call(
        final_kernel,
        grid_spec=pltpu.PrefetchScalarGridSpec(
            num_scalar_prefetch=1,
            grid=(nz, nc),
            in_specs=[
                pl.BlockSpec((row_count, piece), lambda d, n, s, at=at: (0, jnp.where(d == at, n, 0)))
                for at in range(nz)
            ]
            + [
                pl.BlockSpec((nx, 1, 1, piece, stripe), mirror_index(chunk))
                for chunk in range(chunks)
            ],
            out_specs=pl.BlockSpec((row_count, piece), lambda d, n, s: (0, s[d] * nc + n)),
        ),
        out_shape=jax.ShapeDtypeStruct((row_count, col_count), BF16),
        compiler_params=params(),
        name="final",
    )(turn, *owns, *mirrors)


def solution(mesh):
    sizes = (4, 4, 2, 4)
    cube = Mesh(mesh.devices.reshape(sizes), DEVICES)
    return jax.shard_map(
        functools.partial(on_device, sizes),
        mesh=cube,
        in_specs=(
            P(ALPHA, "y"),
            P(None, ALPHA, None, None),
            P(None, ALPHA, None, None, None),
            P(None, "y", None, None),
            P(ALPHA, None, None),
        ),
        out_specs=P(ALPHA, "y"),
        check_vma=False,
    )
```

```python
import functools

import jax
import jax.numpy as jnp
from jax import lax
from jax.experimental import pallas as pl
from jax.experimental.pallas import tpu as pltpu
from jax.sharding import Mesh, PartitionSpec as P

ABLK = 256
CAP = 32
ALPHA = ("x", "z", "core")
DEVICES = ("x", "z", "core", "y")
F32 = jnp.float32
BF16 = jnp.bfloat16
STRIPES = 4


def iota(shape, axis):
    return lax.broadcasted_iota(jnp.int32, shape, axis)


def split(value, size):
    return lax.shift_right_logical(value, jnp.int32(size.bit_length() - 1))


def product(a, b):
    return jnp.dot(a, b, preferred_element_type=F32)


def product_nt(a, b):
    return lax.dot_general(a, b, (((1,), (1,)), ((), ())), preferred_element_type=F32)


def slots(wanted, row_count, owners):
    entries = wanted.shape[1]
    owner = split(wanted, row_count)
    source_row = wanted & (row_count - 1)
    owner_hot = (iota((owners, entries), 0) == owner).astype(F32)
    before = (iota((entries, entries), 0) < iota((entries, entries), 1)).astype(F32)
    earlier = product(owner_hot.astype(BF16), before.astype(BF16))
    slot = jnp.sum(owner_hot * earlier, axis=0, keepdims=True).astype(jnp.int32)
    return owner, owner_hot, slot, source_row


def request_kernel(row_count, owners, wanted_ref, table_ref):
    owner, owner_hot, slot, source_row = slots(wanted_ref[...], row_count, owners)
    slot_hot = (iota((CAP, slot.shape[1]), 0) == slot).astype(F32).astype(BF16)
    high, low = split(source_row, 32), source_row & 31
    table = 32.0 * product_nt((owner_hot * high.astype(F32)).astype(BF16), slot_hot)
    table = table + product_nt((owner_hot * low.astype(F32)).astype(BF16), slot_hot)
    table_ref[...] = table.astype(jnp.int32)


def select_kernel(row_count, owners, wanted_ref, select_ref):
    owner, _, slot, _ = slots(wanted_ref[...], row_count, owners)
    entries = slot.shape[1]
    flat = (owner * CAP + slot).astype(F32)
    diagonal = iota((entries, entries), 0) == iota((entries, entries), 1)
    column = jnp.sum(jnp.where(diagonal, flat, 0.0), axis=1, keepdims=True).astype(jnp.int32)
    select_ref[...] = (iota((entries, owners * CAP), 1) == column).astype(F32).astype(BF16)


def outgoing_kernel(sizes, first, incoming_ref, coeffs_ref, out_ref, hot_ref):
    nx, nz, nc, _ = sizes
    owners = nx * nz * nc
    row_count = coeffs_ref.shape[0]
    group = nx * nc * CAP

    @pl.when((pl.program_id(0) == 0) & (pl.program_id(1) == 0))
    def _():
        places = owners * CAP
        table = incoming_ref[...]
        high, low = split(table, 32), table & 31
        place = iota((places, owners), 0)
        by_z, by_x, by_core = split(place, group), split(place & (group - 1), nc * CAP), split(place & (nc * CAP - 1), CAP)
        owner = by_x * (nz * nc) + by_z * nc + by_core
        place_owner = (owner == iota((places, owners), 1)).astype(F32).astype(BF16)
        spread = 32.0 * product(place_owner, high.astype(F32).astype(BF16))
        spread = spread + product(place_owner, low.astype(F32).astype(BF16))
        mine = (iota((places, CAP), 0) & (CAP - 1)) == iota((places, CAP), 1)
        column = jnp.sum(jnp.where(mine, spread, 0.0), axis=1, keepdims=True).astype(jnp.int32)
        hot_ref[...] = (iota((places, row_count), 1) == column).astype(F32).astype(BF16)

    z = (nz + pl.program_id(0) - first - pl.program_id(1)) & (nz - 1)
    start = pl.multiple_of(z * group, group)
    rows = product(hot_ref[pl.ds(start, group), :], coeffs_ref[...]).astype(BF16)
    out_ref[...] = rows.reshape(out_ref.shape)


def half_kernel(_, select_ref, local_ref, remote_ref, coeffs_ref, replies_ref, beta_ref, *refs):
    *out_refs, mix_ref = refs
    channels, blocks = local_ref.shape[:2]
    order = coeffs_ref.shape[1]

    @pl.when(pl.program_id(1) == 0)
    def _():
        replies = replies_ref[...]
        replies = replies.reshape(replies.shape[0] * replies.shape[1], order)
        far_rows = product(select_ref[...], replies).astype(BF16)
        for block in range(blocks):
            low, high = block * ABLK, (block + 1) * ABLK
            rows = jnp.concatenate([coeffs_ref[low:high, :], far_rows[low:high]], axis=0)
            for channel in range(channels):
                coupling = jnp.concatenate([local_ref[channel, block], remote_ref[channel, block, 0]], axis=1)
                mix_ref[low:high, channel * order:(channel + 1) * order] = product(coupling, rows).astype(BF16)

    beta = jnp.concatenate([beta_ref[channel, 0] for channel in range(channels)], axis=1)
    total = product_nt(beta, mix_ref[...]).astype(BF16)
    stripe = out_refs[0].shape[2]
    for n in range(len(out_refs) // STRIPES):

        @pl.when(pl.program_id(1) == n)
        def _(n=n):
            for index in range(STRIPES):
                out_refs[n * STRIPES + index][0] = total[:, index * stripe:(index + 1) * stripe]


def own_kernel(*refs):
    *in_refs, out_ref = refs
    _, piece, stripe = in_refs[0].shape
    for place, in_ref in enumerate(in_refs):
        n, index = place // STRIPES, place % STRIPES
        out_ref[index * stripe:(index + 1) * stripe, n * piece:(n + 1) * piece] = in_ref[0].T


def regroup_kernel(per_chunk, turn_ref, *refs):
    count = len(refs) // 2
    in_refs, out_refs = refs[:count], refs[count:]
    for my_x in range(STRIPES):

        @pl.when(turn_ref[4] == my_x)
        def _(my_x=my_x):
            for j in range(STRIPES):
                index = (-my_x - j) % STRIPES
                for i in range(per_chunk):
                    for n in range(count // STRIPES):
                        out_refs[i * STRIPES + j][n] = in_refs[n * STRIPES + index][i]


def final_kernel(per_chunk, nz, turn_ref, *refs):
    *in_refs, out_ref = refs
    chunks = nz // per_chunk
    stripe = out_ref.shape[1] // STRIPES
    for distance in range(nz):
        back = -distance % nz

        @pl.when(pl.program_id(0) == distance)
        def _(own_ref=in_refs[distance // per_chunk], mirror_refs=in_refs[chunks + back * STRIPES:]):
            for j in range(STRIPES):
                index = (2 * STRIPES - turn_ref[5] - j) & (STRIPES - 1)
                cols = pl.ds(pl.multiple_of(index * stripe, stripe), stripe)
                out_ref[:, cols] = (own_ref[:, cols].astype(F32) + mirror_refs[j][0].astype(F32)).astype(BF16)


def params(mebibytes):
    return pltpu.CompilerParams(vmem_limit_bytes=mebibytes * 2**20)


def estimate(flops, mebibytes):
    return pl.CostEstimate(flops=flops, bytes_accessed=mebibytes * 2**20, transcendentals=0)


def device_pairs(sizes, move):
    nx, nz, nc, ny = sizes

    def at(x, z, core, y):
        return ((x % nx * nz + z % nz) * nc + core % nc) * ny + y % ny

    places = [(x, z, c, y) for x in range(nx) for z in range(nz) for c in range(nc) for y in range(ny)]
    return [(at(*place), at(*move(*place))) for place in places]


def on_device(sizes, coeffs, local_coupling, remote_coupling, beta_coupling, exc_rows):
    nx, nz, nc, ny = sizes
    owners = nx * nz * nc
    row_count, col_count = coeffs.shape
    channels, beta_blocks, order, _ = beta_coupling.shape
    blocks = row_count // ABLK
    my_x, my_y, my_z = lax.axis_index("x"), lax.axis_index("y"), lax.axis_index("z")
    wanted = exc_rows.reshape(1, row_count)
    places = owners * CAP
    chunks = 2
    per_chunk = beta_blocks // chunks
    piece = order // nc
    stripe = row_count // STRIPES

    table = pl.pallas_call(
        functools.partial(request_kernel, row_count, owners),
        out_shape=jax.ShapeDtypeStruct((owners, CAP), jnp.int32),
        name="requests",
    )(wanted)
    incoming = lax.all_to_all(table, ALPHA, split_axis=0, concat_axis=0, tiled=True)
    select = pl.pallas_call(
        functools.partial(select_kernel, row_count, owners),
        out_shape=jax.ShapeDtypeStruct((row_count, places), BF16),
        compiler_params=params(10),
        name="select",
    )(wanted)
    my_core = lax.axis_index("core")
    column = (my_z + jnp.arange(nz, dtype=jnp.int32)) % nz
    turn = jnp.stack([*(column[d] for d in range(nz)), my_x, my_y, my_core, 1 - my_core]).astype(jnp.int32)

    replies = []
    for chunk in range(chunks):
        outgoing = pl.pallas_call(
            functools.partial(outgoing_kernel, sizes, chunk * per_chunk),
            grid=(nz, per_chunk),
            in_specs=[
                pl.BlockSpec((owners, CAP), lambda k, i: (0, 0)),
                pl.BlockSpec((row_count, order), lambda k, i: (0, k)),
            ],
            out_specs=pl.BlockSpec(
                (nx, 1, nc, CAP, order), lambda k, i, first=chunk * per_chunk: (0, (nz + k - first - i) % nz, 0, 0, i)
            ),
            out_shape=jax.ShapeDtypeStruct((nx, nz, nc, CAP, per_chunk * order), BF16),
            scratch_shapes=[pltpu.VMEM((places, row_count), BF16)],
            compiler_params=params(14),
            cost_estimate=estimate(2 * 10**9, 10),
            name="outgoing",
        )(incoming, coeffs)
        outgoing = outgoing.reshape(owners, CAP, per_chunk * order)
        replies.append(lax.all_to_all(outgoing, ALPHA, split_axis=0, concat_axis=0, tiled=True))

    owns, mirrors = [], []
    block_shape = jax.ShapeDtypeStruct((per_chunk, piece, stripe), BF16)
    for chunk in range(chunks):
        half = pl.pallas_call(
            half_kernel,
            grid_spec=pltpu.PrefetchScalarGridSpec(
                num_scalar_prefetch=1,
                grid=(per_chunk, nc),
                in_specs=[
                    pl.BlockSpec((row_count, places), lambda i, n, s: (0, 0)),
                    pl.BlockSpec((channels, blocks, ABLK, ABLK), lambda i, n, s: (0, 0, 0, 0)),
                    pl.BlockSpec((channels, blocks, 1, ABLK, ABLK), lambda i, n, s: (0, 0, 0, 0, 0)),
                    pl.BlockSpec((row_count, order), lambda i, n, s, d=chunk * per_chunk: (0, s[d + i])),
                    pl.BlockSpec((owners, CAP, order), lambda i, n, s: (0, 0, i)),
                    pl.BlockSpec((channels, 1, piece, order), lambda i, n, s, d=chunk * per_chunk: (0, s[d + i], s[6 + n], 0)),
                ],
                out_specs=[pl.BlockSpec((1, piece, stripe), lambda i, n, s: (i, 0, 0))] * (nc * STRIPES),
                scratch_shapes=[pltpu.VMEM((row_count, channels * order), BF16)],
            ),
            out_shape=[block_shape] * (nc * STRIPES),
            compiler_params=params(30),
            cost_estimate=estimate(8 * 10**9, 24),
            name="half",
        )(turn, select, local_coupling, remote_coupling, coeffs, replies[chunk], beta_coupling)
        owns.append(
            pl.pallas_call(
                own_kernel,
                grid=(per_chunk,),
                in_specs=[pl.BlockSpec((1, piece, stripe), lambda i: (i, 0, 0))] * (nc * STRIPES),
                out_specs=pl.BlockSpec((row_count, order), lambda i: (0, i)),
                out_shape=jax.ShapeDtypeStruct((row_count, per_chunk * order), BF16),
                compiler_params=params(10),
                cost_estimate=estimate(10**9, 4),
                name="own",
            )(*half)
        )
        spread = []
        for n in range(nc):
            for j in range(STRIPES):
                block = half[n * STRIPES + j]
                if n or j:
                    pairs = device_pairs(sizes, lambda x, z, c, y: (x, z, c + n, y + j))
                    block = lax.ppermute(block, DEVICES, pairs)
                spread.append(block)
        grouped = pl.pallas_call(
            functools.partial(regroup_kernel, per_chunk),
            grid_spec=pltpu.PrefetchScalarGridSpec(
                num_scalar_prefetch=1,
                grid=(4,),
                in_specs=[pl.BlockSpec((per_chunk, piece // 4, stripe), lambda g, s: (0, g, 0))] * (nc * STRIPES),
                out_specs=[pl.BlockSpec((nc, piece // 4, stripe), lambda g, s: (0, g, 0))] * (per_chunk * STRIPES),
            ),
            out_shape=[jax.ShapeDtypeStruct((nc, piece, stripe), BF16)] * (per_chunk * STRIPES),
            compiler_params=params(10),
            name="regroup",
        )(turn, *spread)
        if chunk + 1 < chunks:
            replies[chunk + 1], grouped = lax.optimization_barrier((replies[chunk + 1], grouped))
        for i in range(per_chunk):
            distance = chunk * per_chunk + i
            for j in range(STRIPES):
                pairs = device_pairs(sizes, lambda x, z, c, y: (x + y + j, z + distance, c, x))
                mirrors.append(lax.ppermute(grouped[i * STRIPES + j], DEVICES, pairs))

    def own_index(chunk):
        return lambda d, n, s: (0, jnp.clip((d - chunk * per_chunk) * nc + n, 0, per_chunk * nc - 1))

    def mirror_index(distance):
        return lambda d, n, s: (jnp.clip((d + distance - (nz if distance else 0)) * nc + n, 0, nc - 1), 0, 0)

    return pl.pallas_call(
        functools.partial(final_kernel, per_chunk, nz),
        grid_spec=pltpu.PrefetchScalarGridSpec(
            num_scalar_prefetch=1,
            grid=(nz, nc),
            in_specs=[pl.BlockSpec((row_count, piece), own_index(chunk)) for chunk in range(chunks)]
            + [pl.BlockSpec((1, piece, stripe), mirror_index(at // STRIPES)) for at in range(nz * STRIPES)],
            out_specs=pl.BlockSpec((row_count, piece), lambda d, n, s: (0, s[d] * nc + s[6 + n])),
        ),
        out_shape=jax.ShapeDtypeStruct((row_count, col_count), BF16),
        compiler_params=params(14),
        name="final",
    )(turn, *owns, *mirrors)


def solution(mesh):
    sizes = (4, 4, 2, 4)
    cube = Mesh(mesh.devices.reshape(sizes), DEVICES)
    return jax.shard_map(
        functools.partial(on_device, sizes),
        mesh=cube,
        in_specs=(
            P(ALPHA, "y"),
            P(None, ALPHA, None, None),
            P(None, ALPHA, None, None, None),
            P(None, "y", None, None),
            P(ALPHA, None, None),
        ),
        out_specs=P(ALPHA, "y"),
        check_vma=False,
    )
```

```python
import functools

import jax
import jax.numpy as jnp
from jax import lax
from jax.experimental import pallas as pl
from jax.experimental.pallas import tpu as pltpu
from jax.sharding import Mesh, PartitionSpec as P

ABLK = 256
CAP = 32
ALPHA = ("x", "z", "core")
DEVICES = ("x", "z", "core", "y")
F32 = jnp.float32
BF16 = jnp.bfloat16
STRIPES = 4


def iota(shape, axis):
    return lax.broadcasted_iota(jnp.int32, shape, axis)


def split(value, size):
    return lax.shift_right_logical(value, jnp.int32(size.bit_length() - 1))


def product(a, b):
    return jnp.dot(a, b, preferred_element_type=F32)


def product_nt(a, b):
    return lax.dot_general(a, b, (((1,), (1,)), ((), ())), preferred_element_type=F32)


def slots(wanted, row_count, owners):
    entries = wanted.shape[1]
    owner = split(wanted, row_count)
    source_row = wanted & (row_count - 1)
    owner_hot = (iota((owners, entries), 0) == owner).astype(F32)
    before = (iota((entries, entries), 0) < iota((entries, entries), 1)).astype(F32)
    earlier = product(owner_hot.astype(BF16), before.astype(BF16))
    slot = jnp.sum(owner_hot * earlier, axis=0, keepdims=True).astype(jnp.int32)
    return owner, owner_hot, slot, source_row


def request_kernel(row_count, owners, wanted_ref, table_ref):
    owner, owner_hot, slot, source_row = slots(wanted_ref[...], row_count, owners)
    slot_hot = (iota((CAP, slot.shape[1]), 0) == slot).astype(F32).astype(BF16)
    high, low = split(source_row, 32), source_row & 31
    table = 32.0 * product_nt((owner_hot * high.astype(F32)).astype(BF16), slot_hot)
    table = table + product_nt((owner_hot * low.astype(F32)).astype(BF16), slot_hot)
    table_ref[...] = table.astype(jnp.int32)


def select_kernel(row_count, owners, wanted_ref, select_ref):
    owner, _, slot, _ = slots(wanted_ref[...], row_count, owners)
    entries = slot.shape[1]
    flat = (owner * CAP + slot).astype(F32)
    diagonal = iota((entries, entries), 0) == iota((entries, entries), 1)
    column = jnp.sum(jnp.where(diagonal, flat, 0.0), axis=1, keepdims=True).astype(jnp.int32)
    select_ref[...] = (iota((entries, owners * CAP), 1) == column).astype(F32).astype(BF16)


def outgoing_kernel(sizes, first, incoming_ref, coeffs_ref, out_ref, hot_ref):
    nx, nz, nc, _ = sizes
    owners = nx * nz * nc
    row_count = coeffs_ref.shape[0]
    group = nx * nc * CAP

    @pl.when((pl.program_id(0) == 0) & (pl.program_id(1) == 0))
    def _():
        places = owners * CAP
        table = incoming_ref[...]
        high, low = split(table, 32), table & 31
        place = iota((places, owners), 0)
        by_z, by_x, by_core = split(place, group), split(place & (group - 1), nc * CAP), split(place & (nc * CAP - 1), CAP)
        owner = by_x * (nz * nc) + by_z * nc + by_core
        place_owner = (owner == iota((places, owners), 1)).astype(F32).astype(BF16)
        spread = 32.0 * product(place_owner, high.astype(F32).astype(BF16))
        spread = spread + product(place_owner, low.astype(F32).astype(BF16))
        mine = (iota((places, CAP), 0) & (CAP - 1)) == iota((places, CAP), 1)
        column = jnp.sum(jnp.where(mine, spread, 0.0), axis=1, keepdims=True).astype(jnp.int32)
        hot_ref[...] = (iota((places, row_count), 1) == column).astype(F32).astype(BF16)

    z = (nz + pl.program_id(0) - first - pl.program_id(1)) & (nz - 1)
    start = pl.multiple_of(z * group, group)
    rows = product(hot_ref[pl.ds(start, group), :], coeffs_ref[...]).astype(BF16)
    out_ref[...] = rows.reshape(out_ref.shape)


def half_kernel(_, select_ref, local_ref, remote_ref, coeffs_ref, replies_ref, beta_ref, *refs):
    *out_refs, mix_ref = refs
    channels, blocks = local_ref.shape[:2]
    order = coeffs_ref.shape[1]

    @pl.when(pl.program_id(1) == 0)
    def _():
        replies = replies_ref[...]
        replies = replies.reshape(replies.shape[0] * replies.shape[1], order)
        far_rows = product(select_ref[...], replies).astype(BF16)
        for block in range(blocks):
            low, high = block * ABLK, (block + 1) * ABLK
            rows = jnp.concatenate([coeffs_ref[low:high, :], far_rows[low:high]], axis=0)
            for channel in range(channels):
                coupling = jnp.concatenate([local_ref[channel, block], remote_ref[channel, block, 0]], axis=1)
                mix_ref[low:high, channel * order:(channel + 1) * order] = product(coupling, rows).astype(BF16)

    beta = jnp.concatenate([beta_ref[channel, 0] for channel in range(channels)], axis=1)
    total = product_nt(beta, mix_ref[...]).astype(BF16)
    stripe = out_refs[0].shape[3]
    for index, out_ref in enumerate(out_refs):
        out_ref[0, 0] = total[:, index * stripe:(index + 1) * stripe]


def own_kernel(*refs):
    *in_refs, out_ref = refs
    stripe = in_refs[0].shape[3]
    for index, in_ref in enumerate(in_refs):
        out_ref[index * stripe:(index + 1) * stripe, :] = in_ref[0, 0].T


def collect_kernel(turn_ref, *refs):
    *in_refs, out_ref = refs
    per_array = in_refs[0].shape[0]
    for place, in_ref in enumerate(in_refs):
        index = place % STRIPES
        target = (2 * STRIPES + turn_ref[4] - index) & (STRIPES - 1)
        for i in range(per_array):
            out_ref[target, 0, place // STRIPES * per_array + i] = in_ref[i, 0]


def pick_kernel(turn_ref, in_ref, *out_refs):
    for place, out_ref in enumerate(out_refs):
        source = (turn_ref[5] + place % STRIPES) & (STRIPES - 1)
        out_ref[0] = in_ref[source, 0, place // STRIPES]


def final_kernel(nz, turn_ref, *refs):
    own_refs, first_refs, second_ref, out_ref = refs[:nz], refs[nz:-2], refs[-2], refs[-1]
    per_chunk = nz // 2
    stripe = out_ref.shape[1] // STRIPES
    for distance, own_ref in enumerate(own_refs):
        back = -distance % nz

        @pl.when(pl.program_id(0) == distance)
        def _(own_ref=own_ref, back=back):
            for j in range(STRIPES):
                if back < per_chunk:
                    place = (2 * STRIPES + turn_ref[6] - j) & (STRIPES - 1)
                    cols = pl.ds(pl.multiple_of(place * stripe, stripe), stripe)
                    mirror = first_refs[back * STRIPES + j][0]
                else:
                    cols = slice(j * stripe, (j + 1) * stripe)
                    mirror = second_ref[(turn_ref[7] + j) & (STRIPES - 1), 0, 0]
                out_ref[:, cols] = (own_ref[:, cols].astype(F32) + mirror.astype(F32)).astype(BF16)


def params(mebibytes):
    return pltpu.CompilerParams(vmem_limit_bytes=mebibytes * 2**20)


def estimate(flops, mebibytes):
    return pl.CostEstimate(flops=flops, bytes_accessed=mebibytes * 2**20, transcendentals=0)


def device_pairs(sizes, move):
    nx, nz, nc, ny = sizes

    def at(x, z, core, y):
        return ((x % nx * nz + z % nz) * nc + core % nc) * ny + y % ny

    places = [(x, z, c, y) for x in range(nx) for z in range(nz) for c in range(nc) for y in range(ny)]
    return [(at(*place), at(*move(*place))) for place in places]


def on_device(sizes, coeffs, local_coupling, remote_coupling, beta_coupling, exc_rows):
    nx, nz, nc, ny = sizes
    owners = nx * nz * nc
    row_count, col_count = coeffs.shape
    channels, beta_blocks, order, _ = beta_coupling.shape
    blocks = row_count // ABLK
    my_x, my_y, my_z = lax.axis_index("x"), lax.axis_index("y"), lax.axis_index("z")
    wanted = exc_rows.reshape(1, row_count)
    places = owners * CAP
    chunks = 2
    per_chunk = beta_blocks // chunks
    piece = order // nc
    stripe = row_count // STRIPES

    table = pl.pallas_call(
        functools.partial(request_kernel, row_count, owners),
        out_shape=jax.ShapeDtypeStruct((owners, CAP), jnp.int32),
        name="requests",
    )(wanted)
    incoming = lax.all_to_all(table, ALPHA, split_axis=0, concat_axis=0, tiled=True)
    select = pl.pallas_call(
        functools.partial(select_kernel, row_count, owners),
        out_shape=jax.ShapeDtypeStruct((row_count, places), BF16),
        compiler_params=params(10),
        name="select",
    )(wanted)
    column = (my_z + jnp.arange(nz, dtype=jnp.int32)) % nz
    places_of = [*(column[d] for d in range(nz)), my_y, my_y, (my_y - my_x) % STRIPES, (my_x + my_y) % STRIPES]
    turn = jnp.stack(places_of).astype(jnp.int32)
    turn_second = turn.at[4].set((my_x - my_y) % STRIPES)

    replies = []
    for chunk in range(chunks):
        outgoing = pl.pallas_call(
            functools.partial(outgoing_kernel, sizes, chunk * per_chunk),
            grid=(nz, per_chunk),
            in_specs=[
                pl.BlockSpec((owners, CAP), lambda k, i: (0, 0)),
                pl.BlockSpec((row_count, order), lambda k, i: (0, k)),
            ],
            out_specs=pl.BlockSpec(
                (nx, 1, nc, CAP, order), lambda k, i, first=chunk * per_chunk: (0, (nz + k - first - i) % nz, 0, 0, i)
            ),
            out_shape=jax.ShapeDtypeStruct((nx, nz, nc, CAP, per_chunk * order), BF16),
            scratch_shapes=[pltpu.VMEM((places, row_count), BF16)],
            compiler_params=params(56),
            cost_estimate=estimate(2 * 10**9, 10),
            name="outgoing",
        )(incoming, coeffs)
        outgoing = outgoing.reshape(owners, CAP, per_chunk * order)
        replies.append(lax.all_to_all(outgoing, ALPHA, split_axis=0, concat_axis=0, tiled=True))

    def half(chunk, start, count):
        first = chunk * per_chunk + start
        return pl.pallas_call(
            half_kernel,
            grid_spec=pltpu.PrefetchScalarGridSpec(
                num_scalar_prefetch=1,
                grid=(count, nc),
                in_specs=[
                    pl.BlockSpec((row_count, places), lambda i, n, s: (0, 0)),
                    pl.BlockSpec((channels, blocks, ABLK, ABLK), lambda i, n, s: (0, 0, 0, 0)),
                    pl.BlockSpec((channels, blocks, 1, ABLK, ABLK), lambda i, n, s: (0, 0, 0, 0, 0)),
                    pl.BlockSpec((row_count, order), lambda i, n, s: (0, s[first + i])),
                    pl.BlockSpec((owners, CAP, order), lambda i, n, s: (0, 0, start + i)),
                    pl.BlockSpec((channels, 1, piece, order), lambda i, n, s: (0, s[first + i], n, 0)),
                ],
                out_specs=[pl.BlockSpec((1, 1, piece, stripe), lambda i, n, s: (i, n, 0, 0))] * STRIPES,
                scratch_shapes=[pltpu.VMEM((row_count, channels * order), BF16)],
            ),
            out_shape=[jax.ShapeDtypeStruct((count, nc, piece, stripe), BF16)] * STRIPES,
            compiler_params=params(30),
            cost_estimate=estimate(count * 4 * 10**9, 12 * count),
            name="half",
        )(turn, select, local_coupling, remote_coupling, coeffs, replies[chunk], beta_coupling)

    def own(blocks_of, start):
        return pl.pallas_call(
            own_kernel,
            grid=(nc,),
            in_specs=[pl.BlockSpec((1, 1, piece, stripe), lambda n: (start, n, 0, 0))] * STRIPES,
            out_specs=pl.BlockSpec((row_count, piece), lambda n: (0, n)),
            out_shape=jax.ShapeDtypeStruct((row_count, order), BF16),
            compiler_params=params(8),
            cost_estimate=estimate(10**9, 2),
            name="own",
        )(*blocks_of)

    def collect(arrays, which):
        per_array = arrays[0].shape[0]
        grouped = pl.pallas_call(
            collect_kernel,
            grid_spec=pltpu.PrefetchScalarGridSpec(
                num_scalar_prefetch=1,
                grid=(nc, 2),
                in_specs=[pl.BlockSpec((per_array, 1, piece // 2, stripe), lambda n, g, s: (0, n, g, 0))] * len(arrays),
                out_specs=pl.BlockSpec((nx, 1, per_chunk, piece // 2, stripe), lambda n, g, s: (0, n, 0, g, 0)),
            ),
            out_shape=jax.ShapeDtypeStruct((nx, nc, per_chunk, piece, stripe), BF16),
            compiler_params=params(10),
            name="collect",
        )(which, *arrays)
        return grouped.reshape(nx * nc, per_chunk * piece, stripe)

    def exchange(grouped):
        mirrored = lax.all_to_all(grouped, ("x", "core"), split_axis=0, concat_axis=0, tiled=True)
        return mirrored.reshape(nx, nc, per_chunk, piece, stripe)

    def permute(block, move):
        return lax.ppermute(block, DEVICES, device_pairs(sizes, move))

    first = half(0, 0, per_chunk)
    spread = [first[0]] + [permute(first[j], lambda x, z, c, y: (x, z, c, y + j)) for j in range(1, STRIPES)]
    first_grouped = collect(spread, turn)
    replies[1], first_grouped = lax.optimization_barrier((replies[1], first_grouped))
    owns = [own(first, i) for i in range(per_chunk)]
    first_mirror = exchange(first_grouped)

    swapped = []
    for i in range(per_chunk):
        second = half(1, i, 1)
        owns.append(own(second, 0))
        for j in range(STRIPES):
            swapped.append(permute(second[j], lambda x, z, c, y: (x + y + j, z + per_chunk + i, c, x)))
    second_mirror = exchange(collect(swapped, turn_second))

    picked = pl.pallas_call(
        pick_kernel,
        grid_spec=pltpu.PrefetchScalarGridSpec(
            num_scalar_prefetch=1,
            grid=(nc, 2),
            in_specs=[pl.BlockSpec((nx, 1, per_chunk, piece // 2, stripe), lambda n, g, s: (0, n, 0, g, 0))],
            out_specs=[pl.BlockSpec((1, piece // 2, stripe), lambda n, g, s: (n, g, 0))] * (per_chunk * STRIPES),
        ),
        out_shape=[jax.ShapeDtypeStruct((nc, piece, stripe), BF16)] * (per_chunk * STRIPES),
        compiler_params=params(10),
        name="pick",
    )(turn, first_mirror)
    arrived = [picked[0]]
    for place in range(1, per_chunk * STRIPES):
        i, j = place // STRIPES, place % STRIPES
        arrived.append(permute(picked[place], lambda x, z, c, y: (x, z + i, c, y + j)))

    def when_index(at):
        return lambda d, n, s: jnp.clip((d - at) * nc + n, 0, nc - 1)

    def own_spec(distance):
        at = when_index(distance)
        return pl.BlockSpec((row_count, piece), lambda d, n, s: (0, at(d, n, s)))

    def first_spec(i):
        at = when_index(-i % nz)
        return pl.BlockSpec((1, piece, stripe), lambda d, n, s: (at(d, n, s), 0, 0))

    def second_index(d, n, s):
        inside = (d >= 1) & (d <= per_chunk)
        return (0, jnp.where(inside, n, jnp.where(d < 1, 0, nc - 1)), jnp.clip(per_chunk - d, 0, per_chunk - 1), 0, 0)

    return pl.pallas_call(
        functools.partial(final_kernel, nz),
        grid_spec=pltpu.PrefetchScalarGridSpec(
            num_scalar_prefetch=1,
            grid=(nz, nc),
            in_specs=[own_spec(distance) for distance in range(nz)]
            + [first_spec(place // STRIPES) for place in range(per_chunk * STRIPES)]
            + [pl.BlockSpec((nx, 1, 1, piece, stripe), second_index)],
            out_specs=pl.BlockSpec((row_count, piece), lambda d, n, s: (0, s[d] * nc + n)),
        ),
        out_shape=jax.ShapeDtypeStruct((row_count, col_count), BF16),
        compiler_params=params(14),
        name="final",
    )(turn, *owns, *arrived, second_mirror)


def solution(mesh):
    sizes = (4, 4, 2, 4)
    cube = Mesh(mesh.devices.reshape(sizes), DEVICES)
    return jax.shard_map(
        functools.partial(on_device, sizes),
        mesh=cube,
        in_specs=(
            P(ALPHA, "y"),
            P(None, ALPHA, None, None),
            P(None, ALPHA, None, None, None),
            P(None, "y", None, None),
            P(ALPHA, None, None),
        ),
        out_specs=P(ALPHA, "y"),
        check_vma=False,
    )
```

```python
import functools

import jax
import jax.numpy as jnp
from jax import lax
from jax.experimental import pallas as pl
from jax.experimental.pallas import tpu as pltpu
from jax.sharding import Mesh, PartitionSpec as P

ABLK = 256
CAP = 32
ALPHA = ("x", "z", "core")
DEVICES = ("x", "z", "core", "y")
F32 = jnp.float32
BF16 = jnp.bfloat16
STRIPES = 4


def iota(shape, axis):
    return lax.broadcasted_iota(jnp.int32, shape, axis)


def split(value, size):
    return lax.shift_right_logical(value, jnp.int32(size.bit_length() - 1))


def product(a, b):
    return jnp.dot(a, b, preferred_element_type=F32)


def product_nt(a, b):
    return lax.dot_general(a, b, (((1,), (1,)), ((), ())), preferred_element_type=F32)


def slots(wanted, row_count, owners):
    entries = wanted.shape[1]
    owner = split(wanted, row_count)
    source_row = wanted & (row_count - 1)
    owner_hot = (iota((owners, entries), 0) == owner).astype(F32)
    before = (iota((entries, entries), 0) < iota((entries, entries), 1)).astype(F32)
    earlier = product(owner_hot.astype(BF16), before.astype(BF16))
    slot = jnp.sum(owner_hot * earlier, axis=0, keepdims=True).astype(jnp.int32)
    return owner, owner_hot, slot, source_row


def request_kernel(row_count, owners, wanted_ref, table_ref):
    owner, owner_hot, slot, source_row = slots(wanted_ref[...], row_count, owners)
    slot_hot = (iota((CAP, slot.shape[1]), 0) == slot).astype(F32).astype(BF16)
    high, low = split(source_row, 32), source_row & 31
    table = 32.0 * product_nt((owner_hot * high.astype(F32)).astype(BF16), slot_hot)
    table = table + product_nt((owner_hot * low.astype(F32)).astype(BF16), slot_hot)
    table_ref[...] = table.astype(jnp.int32)


def select_kernel(row_count, owners, wanted_ref, select_ref):
    owner, _, slot, _ = slots(wanted_ref[...], row_count, owners)
    entries = slot.shape[1]
    flat = (owner * CAP + slot).astype(F32)
    diagonal = iota((entries, entries), 0) == iota((entries, entries), 1)
    column = jnp.sum(jnp.where(diagonal, flat, 0.0), axis=1, keepdims=True).astype(jnp.int32)
    select_ref[...] = (iota((entries, owners * CAP), 1) == column).astype(F32).astype(BF16)


def outgoing_kernel(sizes, first, per_chunk, incoming_ref, coeffs_ref, out_ref, hot_ref, coeffs_buf, out_buf, in_sems, out_sems):
    nx, nz, nc, _ = sizes
    owners = nx * nz * nc
    row_count = coeffs_ref.shape[0]
    group = nx * nc * CAP
    order = coeffs_buf.shape[2]
    loads = []
    for k in range(nz):
        loads.append(pltpu.make_async_copy(coeffs_ref.at[:, k * order:(k + 1) * order], coeffs_buf.at[k], in_sems.at[k]))
        loads[-1].start()

    places = owners * CAP
    table = incoming_ref[...]
    high, low = split(table, 32), table & 31
    place = iota((places, owners), 0)
    by_z, by_x, by_core = split(place, group), split(place & (group - 1), nc * CAP), split(place & (nc * CAP - 1), CAP)
    owner = by_x * (nz * nc) + by_z * nc + by_core
    place_owner = (owner == iota((places, owners), 1)).astype(F32).astype(BF16)
    spread = 32.0 * product(place_owner, high.astype(F32).astype(BF16))
    spread = spread + product(place_owner, low.astype(F32).astype(BF16))
    mine = (iota((places, CAP), 0) & (CAP - 1)) == iota((places, CAP), 1)
    column = jnp.sum(jnp.where(mine, spread, 0.0), axis=1, keepdims=True).astype(jnp.int32)
    hot_ref[...] = (iota((places, row_count), 1) == column).astype(F32).astype(BF16)

    stores = []
    for k in range(nz):
        loads[k].wait()
        for i in range(per_chunk):
            z = (k - first - i) % nz
            rows = product(hot_ref[z * group:(z + 1) * group, :], coeffs_buf[k]).astype(BF16)
            slot = k * per_chunk + i
            out_buf[slot] = rows.reshape(out_buf.shape[1:])
            target = out_ref.at[:, z, :, :, i * order:(i + 1) * order]
            stores.append(pltpu.make_async_copy(out_buf.at[slot], target, out_sems.at[slot]))
            stores[-1].start()
    for store in stores:
        store.wait()


def half_kernel(_, select_ref, local_ref, remote_ref, coeffs_ref, replies_ref, beta_ref, *refs):
    *out_refs, mix_ref = refs
    channels, blocks = local_ref.shape[:2]
    order = coeffs_ref.shape[1]

    @pl.when(pl.program_id(1) == 0)
    def _():
        replies = replies_ref[...]
        replies = replies.reshape(replies.shape[0] * replies.shape[1], order)
        far_rows = product(select_ref[...], replies).astype(BF16)
        for block in range(blocks):
            low, high = block * ABLK, (block + 1) * ABLK
            rows = jnp.concatenate([coeffs_ref[low:high, :], far_rows[low:high]], axis=0)
            for channel in range(channels):
                coupling = jnp.concatenate([local_ref[channel, block], remote_ref[channel, block, 0]], axis=1)
                mix_ref[low:high, channel * order:(channel + 1) * order] = product(coupling, rows).astype(BF16)

    beta = jnp.concatenate([beta_ref[channel, 0] for channel in range(channels)], axis=1)
    total = product_nt(beta, mix_ref[...]).astype(BF16)
    stripe = out_refs[0].shape[3]
    for index, out_ref in enumerate(out_refs):
        out_ref[0, 0] = total[:, index * stripe:(index + 1) * stripe]


def second_half_kernel(place, distance, turn_ref, select_ref, local_ref, remote_ref, coeffs_ref, replies_ref, beta_ref, *refs):
    out_refs = refs[:STRIPES]
    select, local, remote, coeffs, replies, beta, mix, out_buf, in_sems, beta_sems, out_sems = refs[STRIPES:]
    channels, blocks = local.shape[:2]
    order = coeffs.shape[1]
    pieces = out_buf.shape[0]
    piece = order // pieces
    column = turn_ref[distance]
    sources = [
        (select_ref, select),
        (replies_ref.at[:, :, place * order:(place + 1) * order], replies),
        (coeffs_ref.at[:, pl.ds(pl.multiple_of(column * order, order), order)], coeffs),
        (local_ref, local),
        (remote_ref, remote),
    ]
    loads = [pltpu.make_async_copy(source, target, in_sems.at[at]) for at, (source, target) in enumerate(sources)]
    beta_loads = {}
    for n in range(pieces):
        for channel in range(channels):
            source = beta_ref.at[channel, column, n * piece:(n + 1) * piece]
            target = beta.at[n, :, channel * order:(channel + 1) * order]
            beta_loads[n, channel] = pltpu.make_async_copy(source, target, beta_sems.at[n * channels + channel])
    for load in [*loads, *beta_loads.values()]:
        load.start()

    loads[0].wait()
    loads[1].wait()
    far_rows = product(select[...], replies[...].reshape(-1, order)).astype(BF16)
    for load in loads[2:]:
        load.wait()
    for block in range(blocks):
        low, high = block * ABLK, (block + 1) * ABLK
        rows = jnp.concatenate([coeffs[low:high, :], far_rows[low:high]], axis=0)
        for channel in range(channels):
            coupling = jnp.concatenate([local[channel, block], remote[channel, block, 0]], axis=1)
            mix[low:high, channel * order:(channel + 1) * order] = product(coupling, rows).astype(BF16)
    stores = []
    for n in range(pieces):
        for channel in range(channels):
            beta_loads[n, channel].wait()
        total = product_nt(beta[n], mix[...]).astype(BF16)
        stripe = out_buf.shape[3]
        for index in range(STRIPES):
            out_buf[n, index] = total[:, index * stripe:(index + 1) * stripe]
            store = pltpu.make_async_copy(out_buf.at[n, index], out_refs[index].at[0, n], out_sems.at[n * STRIPES + index])
            store.start()
            stores.append(store)
    for store in stores:
        store.wait()


def own_kernel(*refs):
    *in_refs, out_ref = refs
    stripe = in_refs[0].shape[3]
    for index, in_ref in enumerate(in_refs):
        out_ref[index * stripe:(index + 1) * stripe, :] = in_ref[0, 0].T


def collect_kernel(turn_ref, *refs):
    *in_refs, out_ref = refs
    per_array = in_refs[0].shape[0]
    for place, in_ref in enumerate(in_refs):
        index = place % STRIPES
        target = (2 * STRIPES + turn_ref[4] - index) & (STRIPES - 1)
        for i in range(per_array):
            out_ref[target, 0, place // STRIPES * per_array + i] = in_ref[i, 0]


def pick_kernel(turn_ref, in_ref, *out_refs):
    for place, out_ref in enumerate(out_refs):
        source = (turn_ref[5] + place % STRIPES) & (STRIPES - 1)
        out_ref[0] = in_ref[source, 0, place // STRIPES]


def final_kernel(turn_ref, *refs):
    own_buf, mirror_buf, out_buf, own_sems, mirror_sems, out_sems = refs[-6:]
    out_ref = refs[-7]
    nz, row_count, order = own_buf.shape
    nc, piece, stripe = mirror_buf.shape[2:]
    per_chunk = nz // 2
    own_refs, first_refs, second_ref = refs[:nz], refs[nz:nz + per_chunk * STRIPES], refs[nz + per_chunk * STRIPES]
    loads = []
    for distance in range(nz):
        back = -distance % nz
        group = [pltpu.make_async_copy(own_refs[distance], own_buf.at[distance], own_sems.at[distance])]
        for j in range(STRIPES):
            if back < per_chunk:
                source = first_refs[back * STRIPES + j]
            else:
                source = second_ref.at[j, :, back - per_chunk]
            group.append(pltpu.make_async_copy(source, mirror_buf.at[back, j], mirror_sems.at[back * STRIPES + j]))
        for load in group:
            load.start()
        loads.append(group)
    stores = []
    for distance in range(nz):
        back = -distance % nz
        for load in loads[distance]:
            load.wait()
        for n in range(nc):
            slot = distance * nc + n
            for j in range(STRIPES):
                if back < per_chunk:
                    at, source = (2 * STRIPES + turn_ref[6] - j) & (STRIPES - 1), j
                else:
                    at, source = j, (turn_ref[7] + j) & (STRIPES - 1)
                own_cols = pl.ds(pl.multiple_of(n * piece + at * stripe, stripe), stripe)
                cols = pl.ds(pl.multiple_of(at * stripe, stripe), stripe)
                mirror = mirror_buf[back, source, n].astype(F32)
                out_buf[slot, :, cols] = (own_buf[distance, :, own_cols].astype(F32) + mirror).astype(BF16)
            start = pl.multiple_of((turn_ref[distance] * nc + n) * piece, piece)
            store = pltpu.make_async_copy(out_buf.at[slot], out_ref.at[:, pl.ds(start, piece)], out_sems.at[slot])
            store.start()
            stores.append(store)
    for store in stores:
        store.wait()


def params(mebibytes):
    return pltpu.CompilerParams(vmem_limit_bytes=mebibytes * 2**20)


def estimate(flops, mebibytes):
    return pl.CostEstimate(flops=flops, bytes_accessed=mebibytes * 2**20, transcendentals=0)


def device_pairs(sizes, move):
    nx, nz, nc, ny = sizes

    def at(x, z, core, y):
        return ((x % nx * nz + z % nz) * nc + core % nc) * ny + y % ny

    places = [(x, z, c, y) for x in range(nx) for z in range(nz) for c in range(nc) for y in range(ny)]
    return [(at(*place), at(*move(*place))) for place in places]


def on_device(sizes, coeffs, local_coupling, remote_coupling, beta_coupling, exc_rows):
    nx, nz, nc, ny = sizes
    owners = nx * nz * nc
    row_count, col_count = coeffs.shape
    channels, beta_blocks, order, _ = beta_coupling.shape
    blocks = row_count // ABLK
    my_x, my_y, my_z = lax.axis_index("x"), lax.axis_index("y"), lax.axis_index("z")
    wanted = exc_rows.reshape(1, row_count)
    places = owners * CAP
    chunks = 2
    per_chunk = beta_blocks // chunks
    piece = order // nc
    stripe = row_count // STRIPES

    table = pl.pallas_call(
        functools.partial(request_kernel, row_count, owners),
        out_shape=jax.ShapeDtypeStruct((owners, CAP), jnp.int32),
        name="requests",
    )(wanted)
    incoming = lax.all_to_all(table, ALPHA, split_axis=0, concat_axis=0, tiled=True)
    select = pl.pallas_call(
        functools.partial(select_kernel, row_count, owners),
        out_shape=jax.ShapeDtypeStruct((row_count, places), BF16),
        compiler_params=params(56),
        name="select",
    )(wanted)
    column = (my_z + jnp.arange(nz, dtype=jnp.int32)) % nz
    places_of = [*(column[d] for d in range(nz)), my_y, my_y, (my_y - my_x) % STRIPES, (my_x + my_y) % STRIPES]
    turn = jnp.stack(places_of).astype(jnp.int32)
    turn_second = turn.at[4].set((my_x - my_y) % STRIPES)

    replies = []
    for chunk in range(chunks):
        outgoing = pl.pallas_call(
            functools.partial(outgoing_kernel, sizes, chunk * per_chunk, per_chunk),
            in_specs=[pl.BlockSpec(memory_space=pltpu.VMEM), pl.BlockSpec(memory_space=pl.ANY)],
            out_specs=pl.BlockSpec(memory_space=pl.ANY),
            out_shape=jax.ShapeDtypeStruct((nx, nz, nc, CAP, per_chunk * order), BF16),
            scratch_shapes=[
                pltpu.VMEM((places, row_count), BF16),
                pltpu.VMEM((nz, row_count, order), BF16),
                pltpu.VMEM((nz * per_chunk, nx, nc, CAP, order), BF16),
                pltpu.SemaphoreType.DMA((nz,)),
                pltpu.SemaphoreType.DMA((nz * per_chunk,)),
            ],
            compiler_params=params(56),
            cost_estimate=estimate(2 * 10**9, 10),
            name="outgoing",
        )(incoming, coeffs)
        outgoing = outgoing.reshape(owners, CAP, per_chunk * order)
        replies.append(lax.all_to_all(outgoing, ALPHA, split_axis=0, concat_axis=0, tiled=True))

    def half(chunk, start, count):
        first = chunk * per_chunk + start
        return pl.pallas_call(
            half_kernel,
            grid_spec=pltpu.PrefetchScalarGridSpec(
                num_scalar_prefetch=1,
                grid=(count, nc),
                in_specs=[
                    pl.BlockSpec((row_count, places), lambda i, n, s: (0, 0)),
                    pl.BlockSpec((channels, blocks, ABLK, ABLK), lambda i, n, s: (0, 0, 0, 0)),
                    pl.BlockSpec((channels, blocks, 1, ABLK, ABLK), lambda i, n, s: (0, 0, 0, 0, 0)),
                    pl.BlockSpec((row_count, order), lambda i, n, s: (0, s[first + i])),
                    pl.BlockSpec((owners, CAP, order), lambda i, n, s: (0, 0, start + i)),
                    pl.BlockSpec((channels, 1, piece, order), lambda i, n, s: (0, s[first + i], n, 0)),
                ],
                out_specs=[pl.BlockSpec((1, 1, piece, stripe), lambda i, n, s: (i, n, 0, 0))] * STRIPES,
                scratch_shapes=[pltpu.VMEM((row_count, channels * order), BF16)],
            ),
            out_shape=[jax.ShapeDtypeStruct((count, nc, piece, stripe), BF16)] * STRIPES,
            compiler_params=params(56),
            cost_estimate=estimate(count * 4 * 10**9, 12 * count),
            name="half",
        )(turn, select, local_coupling, remote_coupling, coeffs, replies[chunk], beta_coupling)

    def second_half(place):
        return pl.pallas_call(
            functools.partial(second_half_kernel, place, per_chunk + place),
            grid_spec=pltpu.PrefetchScalarGridSpec(
                num_scalar_prefetch=1,
                grid=(1,),
                in_specs=[pl.BlockSpec(memory_space=pl.ANY)] * 6,
                out_specs=[pl.BlockSpec(memory_space=pl.ANY)] * STRIPES,
                scratch_shapes=[
                    pltpu.VMEM((row_count, places), BF16),
                    pltpu.VMEM(local_coupling.shape, BF16),
                    pltpu.VMEM(remote_coupling.shape, BF16),
                    pltpu.VMEM((row_count, order), BF16),
                    pltpu.VMEM((owners, CAP, order), BF16),
                    pltpu.VMEM((nc, piece, channels * order), BF16),
                    pltpu.VMEM((row_count, channels * order), BF16),
                    pltpu.VMEM((nc, STRIPES, piece, stripe), BF16),
                    pltpu.SemaphoreType.DMA((5,)),
                    pltpu.SemaphoreType.DMA((nc * channels,)),
                    pltpu.SemaphoreType.DMA((nc * STRIPES,)),
                ],
            ),
            out_shape=[jax.ShapeDtypeStruct((1, nc, piece, stripe), BF16)] * STRIPES,
            compiler_params=params(56),
            cost_estimate=estimate(4 * 10**9, 12),
            name="half",
        )(turn, select, local_coupling, remote_coupling, coeffs, replies[1], beta_coupling)

    def own(blocks_of, start):
        return pl.pallas_call(
            own_kernel,
            grid=(nc,),
            in_specs=[pl.BlockSpec((1, 1, piece, stripe), lambda n: (start, n, 0, 0))] * STRIPES,
            out_specs=pl.BlockSpec((row_count, piece), lambda n: (0, n)),
            out_shape=jax.ShapeDtypeStruct((row_count, order), BF16),
            compiler_params=params(56),
            cost_estimate=estimate(10**9, 2),
            name="own",
        )(*blocks_of)

    def collect(arrays, which):
        per_array = arrays[0].shape[0]
        grouped = pl.pallas_call(
            collect_kernel,
            grid_spec=pltpu.PrefetchScalarGridSpec(
                num_scalar_prefetch=1,
                grid=(nc, 2),
                in_specs=[pl.BlockSpec((per_array, 1, piece // 2, stripe), lambda n, g, s: (0, n, g, 0))] * len(arrays),
                out_specs=pl.BlockSpec((nx, 1, per_chunk, piece // 2, stripe), lambda n, g, s: (0, n, 0, g, 0)),
            ),
            out_shape=jax.ShapeDtypeStruct((nx, nc, per_chunk, piece, stripe), BF16),
            compiler_params=params(56),
            name="collect",
        )(which, *arrays)
        return grouped.reshape(nx * nc, per_chunk * piece, stripe)

    def exchange(grouped):
        mirrored = lax.all_to_all(grouped, ("x", "core"), split_axis=0, concat_axis=0, tiled=True)
        return mirrored.reshape(nx, nc, per_chunk, piece, stripe)

    def permute(block, move):
        return lax.ppermute(block, DEVICES, device_pairs(sizes, move))

    first = half(0, 0, per_chunk)
    spread = [first[0]] + [permute(first[j], lambda x, z, c, y: (x, z, c, y + j)) for j in range(1, STRIPES)]
    first_grouped = collect(spread, turn)
    replies[1], first_grouped = lax.optimization_barrier((replies[1], first_grouped))
    owns = [own(first, i) for i in range(per_chunk)]
    first_mirror = exchange(first_grouped)

    swapped = []
    for i in range(per_chunk):
        second = second_half(i)
        owns.append(own(second, 0))
        for j in range(STRIPES):
            swapped.append(permute(second[j], lambda x, z, c, y: (x + y + j, z + per_chunk + i, c, x)))
    second_mirror = exchange(collect(swapped, turn_second))

    picked = pl.pallas_call(
        pick_kernel,
        grid_spec=pltpu.PrefetchScalarGridSpec(
            num_scalar_prefetch=1,
            grid=(nc, 2),
            in_specs=[pl.BlockSpec((nx, 1, per_chunk, piece // 2, stripe), lambda n, g, s: (0, n, 0, g, 0))],
            out_specs=[pl.BlockSpec((1, piece // 2, stripe), lambda n, g, s: (n, g, 0))] * (per_chunk * STRIPES),
        ),
        out_shape=[jax.ShapeDtypeStruct((nc, piece, stripe), BF16)] * (per_chunk * STRIPES),
        compiler_params=params(56),
        name="pick",
    )(turn, first_mirror)
    arrived = [picked[0]]
    for place in range(1, per_chunk * STRIPES):
        i, j = place // STRIPES, place % STRIPES
        arrived.append(permute(picked[place], lambda x, z, c, y: (x, z + i, c, y + j)))

    return pl.pallas_call(
        final_kernel,
        grid_spec=pltpu.PrefetchScalarGridSpec(
            num_scalar_prefetch=1,
            grid=(1,),
            in_specs=[pl.BlockSpec(memory_space=pl.ANY)] * (nz + per_chunk * STRIPES + 1),
            out_specs=pl.BlockSpec(memory_space=pl.ANY),
            scratch_shapes=[
                pltpu.VMEM((nz, row_count, order), BF16),
                pltpu.VMEM((nz, STRIPES, nc, piece, stripe), BF16),
                pltpu.VMEM((nz * nc, row_count, piece), BF16),
                pltpu.SemaphoreType.DMA((nz,)),
                pltpu.SemaphoreType.DMA((nz * STRIPES,)),
                pltpu.SemaphoreType.DMA((nz * nc,)),
            ],
        ),
        out_shape=jax.ShapeDtypeStruct((row_count, col_count), BF16),
        compiler_params=params(56),
        name="final",
    )(turn, *owns, *arrived, second_mirror)


def solution(mesh):
    sizes = (4, 4, 2, 4)
    cube = Mesh(mesh.devices.reshape(sizes), DEVICES)
    return jax.shard_map(
        functools.partial(on_device, sizes),
        mesh=cube,
        in_specs=(
            P(ALPHA, "y"),
            P(None, ALPHA, None, None),
            P(None, ALPHA, None, None, None),
            P(None, "y", None, None),
            P(ALPHA, None, None),
        ),
        out_specs=P(ALPHA, "y"),
        check_vma=False,
    )
```

```python
import functools

import jax
import jax.numpy as jnp
from jax import lax
from jax.experimental import pallas as pl
from jax.experimental.pallas import tpu as pltpu
from jax.sharding import Mesh, PartitionSpec as P

ABLK = 256
CAP = 32
ALPHA = ("x", "zh", "zl", "core")
NEAR = ("x", "zl", "core")
DEVICES = ("x", "zh", "zl", "core", "y")
F32 = jnp.float32
BF16 = jnp.bfloat16
STRIPES = 4


def iota(shape, axis):
    return lax.broadcasted_iota(jnp.int32, shape, axis)


def split(value, size):
    return lax.shift_right_logical(value, jnp.int32(size.bit_length() - 1))


def product(a, b):
    return jnp.dot(a, b, preferred_element_type=F32)


def product_nt(a, b):
    return lax.dot_general(a, b, (((1,), (1,)), ((), ())), preferred_element_type=F32)


def slots(wanted, row_count, owners):
    entries = wanted.shape[1]
    owner = split(wanted, row_count)
    source_row = wanted & (row_count - 1)
    owner_hot = (iota((owners, entries), 0) == owner).astype(F32)
    before = (iota((entries, entries), 0) < iota((entries, entries), 1)).astype(F32)
    earlier = product(owner_hot.astype(BF16), before.astype(BF16))
    slot = jnp.sum(owner_hot * earlier, axis=0, keepdims=True).astype(jnp.int32)
    return owner, owner_hot, slot, source_row


def request_kernel(row_count, owners, wanted_ref, table_ref):
    owner, owner_hot, slot, source_row = slots(wanted_ref[...], row_count, owners)
    slot_hot = (iota((CAP, slot.shape[1]), 0) == slot).astype(F32).astype(BF16)
    high, low = split(source_row, 32), source_row & 31
    table = 32.0 * product_nt((owner_hot * high.astype(F32)).astype(BF16), slot_hot)
    table = table + product_nt((owner_hot * low.astype(F32)).astype(BF16), slot_hot)
    table_ref[...] = table.astype(jnp.int32)


def select_kernel(row_count, owners, wanted_ref, select_ref):
    owner, _, slot, _ = slots(wanted_ref[...], row_count, owners)
    entries = slot.shape[1]
    flat = (owner * CAP + slot).astype(F32)
    diagonal = iota((entries, entries), 0) == iota((entries, entries), 1)
    column = jnp.sum(jnp.where(diagonal, flat, 0.0), axis=1, keepdims=True).astype(jnp.int32)
    select_ref[...] = (iota((entries, owners * CAP), 1) == column).astype(F32).astype(BF16)


def outgoing_kernel(sizes, chunk, incoming_ref, coeffs_ref, out_ref, hot_ref, coeffs_buf, out_buf, in_sems, out_sems):
    nx, nz, nc, _ = sizes
    owners = nx * nz * nc
    row_count = coeffs_ref.shape[0]
    group = nx * nc * CAP
    order = coeffs_buf.shape[2]
    loads = []
    for k in range(nz):
        loads.append(pltpu.make_async_copy(coeffs_ref.at[:, k * order:(k + 1) * order], coeffs_buf.at[k], in_sems.at[k]))
        loads[-1].start()

    places = owners * CAP
    table = incoming_ref[...]
    high, low = split(table, 32), table & 31
    place = iota((places, owners), 0)
    by_z, by_x, by_core = split(place, group), split(place & (group - 1), nc * CAP), split(place & (nc * CAP - 1), CAP)
    owner = by_x * (nz * nc) + by_z * nc + by_core
    place_owner = (owner == iota((places, owners), 1)).astype(F32).astype(BF16)
    spread = 32.0 * product(place_owner, high.astype(F32).astype(BF16))
    spread = spread + product(place_owner, low.astype(F32).astype(BF16))
    mine = (iota((places, CAP), 0) & (CAP - 1)) == iota((places, CAP), 1)
    column = jnp.sum(jnp.where(mine, spread, 0.0), axis=1, keepdims=True).astype(jnp.int32)
    hot_ref[...] = (iota((places, row_count), 1) == column).astype(F32).astype(BF16)

    stores = []
    for k in range(nz):
        loads[k].wait()
        z = (k // 2 ^ chunk) * 2
        rows = product(hot_ref[z * group:(z + 2) * group, :], coeffs_buf[k]).astype(BF16)
        out_buf[k] = rows.reshape(out_buf.shape[1:])
        for near in range(2):
            slot = k * 2 + near
            target = out_ref.at[:, z + near, :, :, k % 2 * order:(k % 2 + 1) * order]
            stores.append(pltpu.make_async_copy(out_buf.at[k, near], target, out_sems.at[slot]))
            stores[-1].start()
    for store in stores:
        store.wait()


def half_kernel(chunk, turn_ref, select_ref, local_ref, remote_ref, coeffs_ref, replies_ref, beta_ref, *refs):
    out_refs = refs[:STRIPES]
    select, local, remote, coeffs, replies, beta, mix, out_buf, base_sems, in_sems, beta_sems, out_sems = refs[STRIPES:]
    channels, blocks = local.shape[:2]
    count, _, order = coeffs.shape
    pieces = out_buf.shape[1]
    piece = order // pieces

    base = [
        pltpu.make_async_copy(source, target, base_sems.at[at])
        for at, (source, target) in enumerate([(select_ref, select), (local_ref, local), (remote_ref, remote)])
    ]
    rows_loads, reply_loads, beta_loads = [], [], []
    for i in range(count):
        column = turn_ref[chunk * count + i]
        source = replies_ref.at[:, :, i * order:(i + 1) * order]
        reply_loads.append(pltpu.make_async_copy(source, replies.at[i], in_sems.at[i]))
        source = coeffs_ref.at[:, pl.ds(pl.multiple_of(column * order, order), order)]
        rows_loads.append(pltpu.make_async_copy(source, coeffs.at[i], in_sems.at[count + i]))
        group = []
        for n in range(pieces):
            for channel in range(channels):
                source = beta_ref.at[channel, column, n * piece:(n + 1) * piece]
                target = beta.at[i, n, :, channel * order:(channel + 1) * order]
                group.append(pltpu.make_async_copy(source, target, beta_sems.at[i, n * channels + channel]))
        beta_loads.append(group)
    base[0].start()
    for i in range(count):
        reply_loads[i].start()
        rows_loads[i].start()
        if i == 0:
            base[1].start()
            base[2].start()
        for load in beta_loads[i]:
            load.start()

    base[0].wait()
    stores = []
    for i in range(count):
        reply_loads[i].wait()
        far_rows = product(select[...], replies[i].reshape(-1, order)).astype(BF16)
        rows_loads[i].wait()
        if i == 0:
            base[1].wait()
            base[2].wait()
        for block in range(blocks):
            low, high = block * ABLK, (block + 1) * ABLK
            rows = jnp.concatenate([coeffs[i, low:high, :], far_rows[low:high]], axis=0)
            for channel in range(channels):
                coupling = jnp.concatenate([local[channel, block], remote[channel, block, 0]], axis=1)
                mix[low:high, channel * order:(channel + 1) * order] = product(coupling, rows).astype(BF16)
        for n in range(pieces):
            for load in beta_loads[i][n * channels:(n + 1) * channels]:
                load.wait()
            total = product_nt(beta[i, n], mix[...]).astype(BF16)
            stripe = out_buf.shape[4]
            for index in range(STRIPES):
                out_buf[i, n, index] = total[:, index * stripe:(index + 1) * stripe]
                target = out_refs[index].at[i, n]
                slot = (i * pieces + n) * STRIPES + index
                stores.append(pltpu.make_async_copy(out_buf.at[i, n, index], target, out_sems.at[slot]))
                stores[-1].start()
    for store in stores:
        store.wait()


def own_kernel(*refs):
    *in_refs, out_ref = refs
    stripe = in_refs[0].shape[3]
    for index, in_ref in enumerate(in_refs):
        out_ref[index * stripe:(index + 1) * stripe, :] = in_ref[0, 0].T


def collect_kernel(order_ref, *refs):
    *in_refs, out_ref, buf, in_sems, out_sems = refs
    loads = [pltpu.make_async_copy(ref, buf.at[at], in_sems.at[at]) for at, ref in enumerate(in_refs)]
    for load in loads:
        load.start()
    stores = []
    for at in range(len(in_refs)):
        loads[at].wait()
        stores.append(pltpu.make_async_copy(buf.at[at], out_ref.at[order_ref[at]], out_sems.at[at]))
        stores[-1].start()
    for store in stores:
        store.wait()


def pick_kernel(order_ref, in_ref, *refs):
    *out_refs, buf, in_sems, out_sems = refs
    count = len(out_refs)
    loads = [pltpu.make_async_copy(in_ref.at[order_ref[at]], buf.at[at], in_sems.at[at]) for at in range(count)]
    for load in loads:
        load.start()
    stores = []
    for at in range(count):
        loads[at].wait()
        stores.append(pltpu.make_async_copy(buf.at[at], out_refs[at], out_sems.at[at]))
        stores[-1].start()
    for store in stores:
        store.wait()


def final_kernel(turn_ref, *refs):
    own_buf, mirror_buf, out_buf, own_sems, mirror_sems, out_sems = refs[-6:]
    out_ref = refs[-7]
    chunks, row_count, width = own_buf.shape
    _, _, per_chunk, nc, piece, stripe = mirror_buf.shape
    own_refs, first_refs, second_ref = refs[:chunks], refs[chunks:chunks + STRIPES], refs[chunks + STRIPES]
    loads = []
    for chunk in (1, 0):
        for i in range(per_chunk):
            cols = slice(i * nc * piece, (i + 1) * nc * piece)
            source, target = own_refs[chunk].at[:, cols], own_buf.at[chunk, :, cols]
            group = [pltpu.make_async_copy(source, target, own_sems.at[chunk * per_chunk + i])]
            for j in range(STRIPES):
                source = second_ref.at[j, i] if chunk else first_refs[j].at[i]
                slot = (chunk * per_chunk + i) * STRIPES + j
                group.append(pltpu.make_async_copy(source, mirror_buf.at[chunk, j, i], mirror_sems.at[slot]))
            for load in group:
                load.start()
            loads.append((chunk, i, group))
    stores = []
    for chunk, i, group in loads:
        for load in group:
            load.wait()
        for n in range(nc):
            slot = (chunk * per_chunk + i) * nc + n
            base = (i * nc + n) * piece
            for j in range(STRIPES):
                if chunk:
                    at, source = j, (turn_ref[5] + j) & (STRIPES - 1)
                else:
                    at, source = (2 * STRIPES + turn_ref[4] - j) & (STRIPES - 1), j
                own_cols = pl.ds(pl.multiple_of(base + at * stripe, stripe), stripe)
                cols = pl.ds(pl.multiple_of(at * stripe, stripe), stripe)
                mirror = mirror_buf[chunk, source, i, n].astype(F32)
                out_buf[slot, :, cols] = (own_buf[chunk, :, own_cols].astype(F32) + mirror).astype(BF16)
            start = pl.multiple_of((turn_ref[chunk * per_chunk + i] * nc + n) * piece, piece)
            store = pltpu.make_async_copy(out_buf.at[slot], out_ref.at[:, pl.ds(start, piece)], out_sems.at[slot])
            store.start()
            stores.append(store)
    for store in stores:
        store.wait()


def params(mebibytes):
    return pltpu.CompilerParams(vmem_limit_bytes=mebibytes * 2**20)


def estimate(flops, mebibytes):
    return pl.CostEstimate(flops=flops, bytes_accessed=mebibytes * 2**20, transcendentals=0)


def device_pairs(sizes, move):
    nx, nz, nc, ny = sizes

    def at(x, z, core, y):
        return ((x % nx * nz + z % nz) * nc + core % nc) * ny + y % ny

    places = [(x, z, c, y) for x in range(nx) for z in range(nz) for c in range(nc) for y in range(ny)]
    return [(at(*place), at(*move(*place))) for place in places]


def prefetched(kernel, name, inputs, out_shape, scratch, flops, mebibytes):
    return pl.pallas_call(
        kernel,
        grid_spec=pltpu.PrefetchScalarGridSpec(
            num_scalar_prefetch=1,
            grid=(1,),
            in_specs=[pl.BlockSpec(memory_space=pl.ANY)] * inputs,
            out_specs=jax.tree.map(lambda _: pl.BlockSpec(memory_space=pl.ANY), out_shape),
            scratch_shapes=scratch,
        ),
        out_shape=out_shape,
        compiler_params=params(56),
        cost_estimate=estimate(flops, mebibytes),
        name=name,
    )


def on_device(sizes, coeffs, local_coupling, remote_coupling, beta_coupling, exc_rows):
    nx, nz, nc, ny = sizes
    owners = nx * nz * nc
    row_count, col_count = coeffs.shape
    channels, _, order, _ = beta_coupling.shape
    my_x, my_y, my_half = lax.axis_index("x"), lax.axis_index("y"), lax.axis_index("zh")
    wanted = exc_rows.reshape(1, row_count)
    places = owners * CAP
    chunks, per_chunk = 2, nz // 2
    piece = order // nc
    stripe = row_count // STRIPES
    dma = pltpu.SemaphoreType.DMA

    table = pl.pallas_call(
        functools.partial(request_kernel, row_count, owners),
        out_shape=jax.ShapeDtypeStruct((owners, CAP), jnp.int32),
        name="requests",
    )(wanted)
    incoming = lax.all_to_all(table, ALPHA, split_axis=0, concat_axis=0, tiled=True)
    select = pl.pallas_call(
        functools.partial(select_kernel, row_count, owners),
        out_shape=jax.ShapeDtypeStruct((row_count, places), BF16),
        compiler_params=params(56),
        name="select",
    )(wanted)
    near, far = 2 * my_half, 2 - 2 * my_half
    stripes = jnp.arange(STRIPES, dtype=jnp.int32)
    scalars = [near, near + 1, far, far + 1, (my_y - my_x) % STRIPES, (my_x + my_y) % STRIPES]
    turn = jnp.stack(scalars).astype(jnp.int32)
    first_order = (my_y - stripes) % STRIPES
    second_order = (my_x - my_y - stripes) % STRIPES
    pick_order = (my_y + stripes) % STRIPES

    replies = []
    for chunk in range(chunks):
        outgoing = pl.pallas_call(
            functools.partial(outgoing_kernel, sizes, chunk),
            in_specs=[pl.BlockSpec(memory_space=pltpu.VMEM), pl.BlockSpec(memory_space=pl.ANY)],
            out_specs=pl.BlockSpec(memory_space=pl.ANY),
            out_shape=jax.ShapeDtypeStruct((nx, nz, nc, CAP, per_chunk * order), BF16),
            scratch_shapes=[
                pltpu.VMEM((places, row_count), BF16),
                pltpu.VMEM((nz, row_count, order), BF16),
                pltpu.VMEM((nz, 2, nx, nc, CAP, order), BF16),
                dma((nz,)),
                dma((nz * 2,)),
            ],
            compiler_params=params(56),
            cost_estimate=estimate(2 * 10**9, 10),
            name="outgoing",
        )(incoming, coeffs)
        outgoing = outgoing.reshape(owners, CAP, per_chunk * order)
        replies.append(lax.all_to_all(outgoing, ALPHA, split_axis=0, concat_axis=0, tiled=True))

    blocks_shape = jax.ShapeDtypeStruct((per_chunk, nc, piece, stripe), BF16)
    group_shape = jax.ShapeDtypeStruct((STRIPES, per_chunk, nc, piece, stripe), BF16)

    def half(chunk):
        scratch = [
            pltpu.VMEM((row_count, places), BF16),
            pltpu.VMEM(local_coupling.shape, BF16),
            pltpu.VMEM(remote_coupling.shape, BF16),
            pltpu.VMEM((per_chunk, row_count, order), BF16),
            pltpu.VMEM((per_chunk, owners, CAP, order), BF16),
            pltpu.VMEM((per_chunk, nc, piece, channels * order), BF16),
            pltpu.VMEM((row_count, channels * order), BF16),
            pltpu.VMEM((per_chunk, nc, STRIPES, piece, stripe), BF16),
            dma((3,)),
            dma((2 * per_chunk,)),
            dma((per_chunk, nc * channels)),
            dma((per_chunk * nc * STRIPES,)),
        ]
        call = prefetched(functools.partial(half_kernel, chunk), "half", 6, [blocks_shape] * STRIPES, scratch, 8 * 10**9, 18)
        return call(turn, select, local_coupling, remote_coupling, coeffs, replies[chunk], beta_coupling)

    def own(blocks_of):
        return pl.pallas_call(
            own_kernel,
            grid=(per_chunk, nc),
            in_specs=[pl.BlockSpec((1, 1, piece, stripe), lambda i, n: (i, n, 0, 0))] * STRIPES,
            out_specs=pl.BlockSpec((row_count, piece), lambda i, n: (0, i * nc + n)),
            out_shape=jax.ShapeDtypeStruct((row_count, per_chunk * order), BF16),
            compiler_params=params(56),
            cost_estimate=estimate(10**9, 4),
            name="own",
        )(*blocks_of)

    moving = [pltpu.VMEM(group_shape.shape, BF16), dma((STRIPES,)), dma((STRIPES,))]

    def exchange(arrays, to):
        grouped = prefetched(collect_kernel, "collect", STRIPES, group_shape, moving, 0, 4)(to, *arrays)
        return grouped

    def all_near(grouped):
        grouped = grouped.reshape(nx * per_chunk * nc, piece, stripe)
        return lax.all_to_all(grouped, NEAR, split_axis=0, concat_axis=0, tiled=True).reshape(group_shape.shape)

    def permute(block, move):
        return lax.ppermute(block, DEVICES, device_pairs(sizes, move))

    first = half(0)
    spread = [first[0]] + [permute(first[j], lambda x, z, c, y: (x, z, c, y + j)) for j in range(1, STRIPES)]
    first_grouped = exchange(spread, first_order)
    replies[1], first_grouped = lax.optimization_barrier((replies[1], first_grouped))
    first_mirror = all_near(first_grouped)
    second = half(1)
    swapped = {j: permute(second[j], lambda x, z, c, y: (x + y + j, z ^ 2, c, x)) for j in (0, 2, 1, 3)}
    second_grouped = exchange([swapped[j] for j in range(STRIPES)], second_order)
    second_mirror = all_near(second_grouped)

    picked = prefetched(pick_kernel, "pick", 1, [blocks_shape] * STRIPES, moving, 0, 4)(pick_order, first_mirror)
    arrived = [picked[0]] + [permute(picked[j], lambda x, z, c, y: (x, z, c, y + j)) for j in range(1, STRIPES)]

    scratch = [
        pltpu.VMEM((chunks, row_count, per_chunk * order), BF16),
        pltpu.VMEM((chunks, STRIPES, per_chunk, nc, piece, stripe), BF16),
        pltpu.VMEM((nz * nc, row_count, piece), BF16),
        dma((nz,)),
        dma((nz * STRIPES,)),
        dma((nz * nc,)),
    ]
    out_shape = jax.ShapeDtypeStruct((row_count, col_count), BF16)
    final = prefetched(final_kernel, "final", chunks + STRIPES + 1, out_shape, scratch, 10**7, 12)
    return final(turn, own(first), own(second), *arrived, second_mirror)


def solution(mesh):
    sizes = (4, 4, 2, 4)
    cube = Mesh(mesh.devices.reshape(4, 2, 2, 2, 4), DEVICES)
    return jax.shard_map(
        functools.partial(on_device, sizes),
        mesh=cube,
        in_specs=(
            P(ALPHA, "y"),
            P(None, ALPHA, None, None),
            P(None, ALPHA, None, None, None),
            P(None, "y", None, None),
            P(ALPHA, None, None),
        ),
        out_specs=P(ALPHA, "y"),
        check_vma=False,
    )
```

```python
import functools

import jax
import jax.numpy as jnp
from jax import lax
from jax.experimental import pallas as pl
from jax.experimental.pallas import tpu as pltpu
from jax.sharding import Mesh, PartitionSpec as P

ABLK = 256
CAP = 32
ALPHA = ("x", "zh", "zl", "core")
NEAR = ("x", "zh", "core")
DEVICES = ("x", "zh", "zl", "core", "y")
F32 = jnp.float32
BF16 = jnp.bfloat16
STRIPES = 4


def iota(shape, axis):
    return lax.broadcasted_iota(jnp.int32, shape, axis)


def split(value, size):
    return lax.shift_right_logical(value, jnp.int32(size.bit_length() - 1))


def product(a, b):
    return jnp.dot(a, b, preferred_element_type=F32)


def product_nt(a, b):
    return lax.dot_general(a, b, (((1,), (1,)), ((), ())), preferred_element_type=F32)


def slots(wanted, row_count, owners):
    entries = wanted.shape[1]
    owner = split(wanted, row_count)
    source_row = wanted & (row_count - 1)
    owner_hot = (iota((owners, entries), 0) == owner).astype(F32)
    before = (iota((entries, entries), 0) < iota((entries, entries), 1)).astype(F32)
    earlier = product(owner_hot.astype(BF16), before.astype(BF16))
    slot = jnp.sum(owner_hot * earlier, axis=0, keepdims=True).astype(jnp.int32)
    return owner, owner_hot, slot, source_row


def request_kernel(row_count, owners, wanted_ref, table_ref):
    owner, owner_hot, slot, source_row = slots(wanted_ref[...], row_count, owners)
    slot_hot = (iota((CAP, slot.shape[1]), 0) == slot).astype(F32).astype(BF16)
    high, low = split(source_row, 32), source_row & 31
    table = 32.0 * product_nt((owner_hot * high.astype(F32)).astype(BF16), slot_hot)
    table = table + product_nt((owner_hot * low.astype(F32)).astype(BF16), slot_hot)
    table_ref[...] = table.astype(jnp.int32)


def select_kernel(row_count, owners, wanted_ref, select_ref):
    owner, _, slot, _ = slots(wanted_ref[...], row_count, owners)
    entries = slot.shape[1]
    flat = (owner * CAP + slot).astype(F32)
    diagonal = iota((entries, entries), 0) == iota((entries, entries), 1)
    column = jnp.sum(jnp.where(diagonal, flat, 0.0), axis=1, keepdims=True).astype(jnp.int32)
    select_ref[...] = (iota((entries, owners * CAP), 1) == column).astype(F32).astype(BF16)


def outgoing_kernel(sizes, chunk, incoming_ref, coeffs_ref, out_ref, hot_ref, coeffs_buf, out_buf, in_sems, out_sems):
    nx, nz, nc, _ = sizes
    owners = nx * nz * nc
    row_count = coeffs_ref.shape[0]
    group = nx * nc * CAP
    order = coeffs_buf.shape[2]
    loads = []
    for k in range(nz):
        loads.append(pltpu.make_async_copy(coeffs_ref.at[:, k * order:(k + 1) * order], coeffs_buf.at[k], in_sems.at[k]))
        loads[-1].start()

    places = owners * CAP
    table = incoming_ref[...]
    high, low = split(table, 32), table & 31
    place = iota((places, owners), 0)
    by_z, by_x, by_core = split(place, group), split(place & (group - 1), nc * CAP), split(place & (nc * CAP - 1), CAP)
    owner = by_x * (nz * nc) + ((by_z & 1) * 2 + split(by_z, 2)) * nc + by_core
    place_owner = (owner == iota((places, owners), 1)).astype(F32).astype(BF16)
    spread = 32.0 * product(place_owner, high.astype(F32).astype(BF16))
    spread = spread + product(place_owner, low.astype(F32).astype(BF16))
    mine = (iota((places, CAP), 0) & (CAP - 1)) == iota((places, CAP), 1)
    column = jnp.sum(jnp.where(mine, spread, 0.0), axis=1, keepdims=True).astype(jnp.int32)
    hot_ref[...] = (iota((places, row_count), 1) == column).astype(F32).astype(BF16)

    stores = []
    for k in range(nz):
        loads[k].wait()
        parity = k % 2 ^ chunk
        rows = product(hot_ref[parity * 2 * group:(parity + 1) * 2 * group, :], coeffs_buf[k]).astype(BF16)
        out_buf[k] = rows.reshape(out_buf.shape[1:])
        for near in range(2):
            slot = k * 2 + near
            target = out_ref.at[:, near * 2 + parity, :, :, k // 2 * order:(k // 2 + 1) * order]
            stores.append(pltpu.make_async_copy(out_buf.at[k, near], target, out_sems.at[slot]))
            stores[-1].start()
    for store in stores:
        store.wait()


def half_kernel(chunk, turn_ref, select_ref, local_ref, remote_ref, coeffs_ref, replies_ref, beta_ref, *refs):
    out_refs = refs[:STRIPES]
    select, local, remote, coeffs, replies, beta, mix, out_buf, base_sems, in_sems, beta_sems, out_sems = refs[STRIPES:]
    channels, blocks = local.shape[:2]
    count, _, order = coeffs.shape
    pieces = out_buf.shape[1]
    piece = order // pieces

    base = [
        pltpu.make_async_copy(source, target, base_sems.at[at])
        for at, (source, target) in enumerate([(select_ref, select), (local_ref, local), (remote_ref, remote)])
    ]
    rows_loads, reply_loads, beta_loads = [], [], []
    for i in range(count):
        column = turn_ref[chunk * count + i]
        source = replies_ref.at[:, :, i * order:(i + 1) * order]
        reply_loads.append(pltpu.make_async_copy(source, replies.at[i], in_sems.at[i]))
        source = coeffs_ref.at[:, pl.ds(pl.multiple_of(column * order, order), order)]
        rows_loads.append(pltpu.make_async_copy(source, coeffs.at[i], in_sems.at[count + i]))
        group = []
        for n in range(pieces):
            for channel in range(channels):
                source = beta_ref.at[channel, column, n * piece:(n + 1) * piece]
                target = beta.at[i, n, :, channel * order:(channel + 1) * order]
                group.append(pltpu.make_async_copy(source, target, beta_sems.at[i, n * channels + channel]))
        beta_loads.append(group)
    base[0].start()
    for i in range(count):
        reply_loads[i].start()
        rows_loads[i].start()
        if i == 0:
            base[1].start()
            base[2].start()
        for load in beta_loads[i]:
            load.start()

    base[0].wait()
    stores = []
    for i in range(count):
        reply_loads[i].wait()
        far_rows = product(select[...], replies[i].reshape(-1, order)).astype(BF16)
        rows_loads[i].wait()
        if i == 0:
            base[1].wait()
            base[2].wait()
        for block in range(blocks):
            low, high = block * ABLK, (block + 1) * ABLK
            rows = jnp.concatenate([coeffs[i, low:high, :], far_rows[low:high]], axis=0)
            for channel in range(channels):
                coupling = jnp.concatenate([local[channel, block], remote[channel, block, 0]], axis=1)
                mix[low:high, channel * order:(channel + 1) * order] = product(coupling, rows).astype(BF16)
        for n in range(pieces):
            for load in beta_loads[i][n * channels:(n + 1) * channels]:
                load.wait()
            total = product_nt(beta[i, n], mix[...]).astype(BF16)
            stripe = out_buf.shape[4]
            for index in range(STRIPES):
                out_buf[i, n, index] = total[:, index * stripe:(index + 1) * stripe]
                target = out_refs[index].at[i, n]
                slot = (i * pieces + n) * STRIPES + index
                stores.append(pltpu.make_async_copy(out_buf.at[i, n, index], target, out_sems.at[slot]))
                stores[-1].start()
    for store in stores:
        store.wait()


def own_kernel(*refs):
    *in_refs, out_ref = refs
    stripe = in_refs[0].shape[3]
    for index, in_ref in enumerate(in_refs):
        out_ref[index * stripe:(index + 1) * stripe, :] = in_ref[0, 0].T


def collect_kernel(order_ref, *refs):
    *in_refs, out_ref, buf, in_sems, out_sems = refs
    loads = [pltpu.make_async_copy(ref, buf.at[at], in_sems.at[at]) for at, ref in enumerate(in_refs)]
    for load in loads:
        load.start()
    stores = []
    for at in range(len(in_refs)):
        loads[at].wait()
        stores.append(pltpu.make_async_copy(buf.at[at], out_ref.at[order_ref[at]], out_sems.at[at]))
        stores[-1].start()
    for store in stores:
        store.wait()


def pick_kernel(order_ref, in_ref, *refs):
    *out_refs, buf, in_sems, out_sems = refs
    count = len(out_refs)
    loads = [pltpu.make_async_copy(in_ref.at[order_ref[at]], buf.at[at], in_sems.at[at]) for at in range(count)]
    for load in loads:
        load.start()
    stores = []
    for at in range(count):
        loads[at].wait()
        stores.append(pltpu.make_async_copy(buf.at[at], out_refs[at], out_sems.at[at]))
        stores[-1].start()
    for store in stores:
        store.wait()


def final_kernel(turn_ref, *refs):
    own_buf, mirror_buf, out_buf, own_sems, mirror_sems, out_sems = refs[-6:]
    out_ref = refs[-7]
    chunks, row_count, width = own_buf.shape
    _, _, per_chunk, nc, piece, stripe = mirror_buf.shape
    own_refs, first_refs, second_ref = refs[:chunks], refs[chunks:chunks + STRIPES], refs[chunks + STRIPES]
    loads = []
    for chunk in (1, 0):
        for i in range(per_chunk):
            cols = slice(i * nc * piece, (i + 1) * nc * piece)
            source, target = own_refs[chunk].at[:, cols], own_buf.at[chunk, :, cols]
            group = [pltpu.make_async_copy(source, target, own_sems.at[chunk * per_chunk + i])]
            for j in range(STRIPES):
                if chunk:
                    z_flip = (turn_ref[6] + 1 + j // 2) & 1
                    source = second_ref.at[(turn_ref[5] + j) & (STRIPES - 1), (i + z_flip) & 1]
                else:
                    source = first_refs[j].at[i]
                slot = (chunk * per_chunk + i) * STRIPES + j
                group.append(pltpu.make_async_copy(source, mirror_buf.at[chunk, j, i], mirror_sems.at[slot]))
            for load in group:
                load.start()
            loads.append((chunk, i, group))
    stores = []
    for chunk, i, group in loads:
        for load in group:
            load.wait()
        for n in range(nc):
            slot = (chunk * per_chunk + i) * nc + n
            base = (i * nc + n) * piece
            for j in range(STRIPES):
                at = j if chunk else (2 * STRIPES + turn_ref[4] - j) & (STRIPES - 1)
                own_cols = pl.ds(pl.multiple_of(base + at * stripe, stripe), stripe)
                cols = pl.ds(pl.multiple_of(at * stripe, stripe), stripe)
                mirror = mirror_buf[chunk, j, i, n].astype(F32)
                out_buf[slot, :, cols] = (own_buf[chunk, :, own_cols].astype(F32) + mirror).astype(BF16)
            start = pl.multiple_of((turn_ref[chunk * per_chunk + i] * nc + n) * piece, piece)
            store = pltpu.make_async_copy(out_buf.at[slot], out_ref.at[:, pl.ds(start, piece)], out_sems.at[slot])
            store.start()
            stores.append(store)
    for store in stores:
        store.wait()


def params(mebibytes):
    return pltpu.CompilerParams(vmem_limit_bytes=mebibytes * 2**20)


def estimate(flops, mebibytes):
    return pl.CostEstimate(flops=flops, bytes_accessed=mebibytes * 2**20, transcendentals=0)


def device_pairs(sizes, move):
    nx, nz, nc, ny = sizes

    def at(x, z, core, y):
        return ((x % nx * nz + z % nz) * nc + core % nc) * ny + y % ny

    places = [(x, z, c, y) for x in range(nx) for z in range(nz) for c in range(nc) for y in range(ny)]
    return [(at(*place), at(*move(*place))) for place in places]


def prefetched(kernel, name, inputs, out_shape, scratch, flops, mebibytes):
    return pl.pallas_call(
        kernel,
        grid_spec=pltpu.PrefetchScalarGridSpec(
            num_scalar_prefetch=1,
            grid=(1,),
            in_specs=[pl.BlockSpec(memory_space=pl.ANY)] * inputs,
            out_specs=jax.tree.map(lambda _: pl.BlockSpec(memory_space=pl.ANY), out_shape),
            scratch_shapes=scratch,
        ),
        out_shape=out_shape,
        compiler_params=params(56),
        cost_estimate=estimate(flops, mebibytes),
        name=name,
    )


def on_device(sizes, coeffs, local_coupling, remote_coupling, beta_coupling, exc_rows):
    nx, nz, nc, ny = sizes
    owners = nx * nz * nc
    row_count, col_count = coeffs.shape
    channels, _, order, _ = beta_coupling.shape
    my_x, my_y, parity = lax.axis_index("x"), lax.axis_index("y"), lax.axis_index("zl")
    wanted = exc_rows.reshape(1, row_count)
    places = owners * CAP
    chunks, per_chunk = 2, nz // 2
    piece = order // nc
    stripe = row_count // STRIPES
    dma = pltpu.SemaphoreType.DMA

    table = pl.pallas_call(
        functools.partial(request_kernel, row_count, owners),
        out_shape=jax.ShapeDtypeStruct((owners, CAP), jnp.int32),
        name="requests",
    )(wanted)
    incoming = lax.all_to_all(table, ALPHA, split_axis=0, concat_axis=0, tiled=True)
    select = pl.pallas_call(
        functools.partial(select_kernel, row_count, owners),
        out_shape=jax.ShapeDtypeStruct((row_count, places), BF16),
        compiler_params=params(56),
        name="select",
    )(wanted)
    stripes = jnp.arange(STRIPES, dtype=jnp.int32)
    columns = [parity, 2 + parity, 1 - parity, 3 - parity]
    scalars = [*columns, (my_y - my_x) % STRIPES, (my_x + my_y) % STRIPES, parity]
    turn = jnp.stack(scalars).astype(jnp.int32)
    first_order = (my_y - stripes) % STRIPES
    second_order = (my_x - my_y - stripes) % STRIPES
    pick_order = (my_y + stripes) % STRIPES

    replies = []
    for chunk in range(chunks):
        outgoing = pl.pallas_call(
            functools.partial(outgoing_kernel, sizes, chunk),
            in_specs=[pl.BlockSpec(memory_space=pltpu.VMEM), pl.BlockSpec(memory_space=pl.ANY)],
            out_specs=pl.BlockSpec(memory_space=pl.ANY),
            out_shape=jax.ShapeDtypeStruct((nx, nz, nc, CAP, per_chunk * order), BF16),
            scratch_shapes=[
                pltpu.VMEM((places, row_count), BF16),
                pltpu.VMEM((nz, row_count, order), BF16),
                pltpu.VMEM((nz, 2, nx, nc, CAP, order), BF16),
                dma((nz,)),
                dma((nz * 2,)),
            ],
            compiler_params=params(56),
            cost_estimate=estimate(2 * 10**9, 10),
            name="outgoing",
        )(incoming, coeffs)
        outgoing = outgoing.reshape(owners, CAP, per_chunk * order)
        replies.append(lax.all_to_all(outgoing, ALPHA, split_axis=0, concat_axis=0, tiled=True))

    blocks_shape = jax.ShapeDtypeStruct((per_chunk, nc, piece, stripe), BF16)
    group_shape = jax.ShapeDtypeStruct((STRIPES, per_chunk, nc, piece, stripe), BF16)

    def half(chunk):
        scratch = [
            pltpu.VMEM((row_count, places), BF16),
            pltpu.VMEM(local_coupling.shape, BF16),
            pltpu.VMEM(remote_coupling.shape, BF16),
            pltpu.VMEM((per_chunk, row_count, order), BF16),
            pltpu.VMEM((per_chunk, owners, CAP, order), BF16),
            pltpu.VMEM((per_chunk, nc, piece, channels * order), BF16),
            pltpu.VMEM((row_count, channels * order), BF16),
            pltpu.VMEM((per_chunk, nc, STRIPES, piece, stripe), BF16),
            dma((3,)),
            dma((2 * per_chunk,)),
            dma((per_chunk, nc * channels)),
            dma((per_chunk * nc * STRIPES,)),
        ]
        call = prefetched(functools.partial(half_kernel, chunk), "half", 6, [blocks_shape] * STRIPES, scratch, 8 * 10**9, 18)
        return call(turn, select, local_coupling, remote_coupling, coeffs, replies[chunk], beta_coupling)

    def own(blocks_of):
        return pl.pallas_call(
            own_kernel,
            grid=(per_chunk, nc),
            in_specs=[pl.BlockSpec((1, 1, piece, stripe), lambda i, n: (i, n, 0, 0))] * STRIPES,
            out_specs=pl.BlockSpec((row_count, piece), lambda i, n: (0, i * nc + n)),
            out_shape=jax.ShapeDtypeStruct((row_count, per_chunk * order), BF16),
            compiler_params=params(56),
            cost_estimate=estimate(10**9, 4),
            name="own",
        )(*blocks_of)

    moving = [pltpu.VMEM(group_shape.shape, BF16), dma((STRIPES,)), dma((STRIPES,))]

    def exchange(arrays, to):
        grouped = prefetched(collect_kernel, "collect", STRIPES, group_shape, moving, 0, 4)(to, *arrays)
        return grouped

    def all_near(grouped):
        grouped = grouped.reshape(nx * per_chunk * nc, piece, stripe)
        return lax.all_to_all(grouped, NEAR, split_axis=0, concat_axis=0, tiled=True).reshape(group_shape.shape)

    def permute(block, move):
        return lax.ppermute(block, DEVICES, device_pairs(sizes, move))

    first = half(0)
    spread = [first[0]] + [permute(first[j], lambda x, z, c, y: (x, z, c, y + j)) for j in range(1, STRIPES)]
    first_grouped = exchange(spread, first_order)
    replies[1], first_grouped = lax.optimization_barrier((replies[1], first_grouped))
    first_mirror = all_near(first_grouped)
    second = half(1)
    swapped = {}
    for j in (0, 2, 1, 3):
        step = 1 if j < 2 else -1
        swapped[j] = permute(second[j], lambda x, z, c, y: (x + y + j, z + step, c, x))
    picked = prefetched(pick_kernel, "pick", 1, [blocks_shape] * STRIPES, moving, 0, 4)(pick_order, first_mirror)
    swapped, picked = lax.optimization_barrier(([swapped[j] for j in range(STRIPES)], picked))
    second_mirror = all_near(exchange(swapped, second_order))

    arrived = [picked[0]] + [permute(picked[j], lambda x, z, c, y: (x, z, c, y + j)) for j in range(1, STRIPES)]

    scratch = [
        pltpu.VMEM((chunks, row_count, per_chunk * order), BF16),
        pltpu.VMEM((chunks, STRIPES, per_chunk, nc, piece, stripe), BF16),
        pltpu.VMEM((nz * nc, row_count, piece), BF16),
        dma((nz,)),
        dma((nz * STRIPES,)),
        dma((nz * nc,)),
    ]
    out_shape = jax.ShapeDtypeStruct((row_count, col_count), BF16)
    final = prefetched(final_kernel, "final", chunks + STRIPES + 1, out_shape, scratch, 10**7, 12)
    return final(turn, own(first), own(second), *arrived, second_mirror)


def solution(mesh):
    sizes = (4, 4, 2, 4)
    cube = Mesh(mesh.devices.reshape(4, 2, 2, 2, 4), DEVICES)
    return jax.shard_map(
        functools.partial(on_device, sizes),
        mesh=cube,
        in_specs=(
            P(ALPHA, "y"),
            P(None, ALPHA, None, None),
            P(None, ALPHA, None, None, None),
            P(None, "y", None, None),
            P(ALPHA, None, None),
        ),
        out_specs=P(ALPHA, "y"),
        check_vma=False,
    )
```

```python
import functools

import jax
import jax.numpy as jnp
from jax import lax
from jax.experimental import pallas as pl
from jax.experimental.pallas import tpu as pltpu
from jax.sharding import Mesh, PartitionSpec as P

ABLK = 256
CAP = 32
ALPHA = ("x", "zh", "zl", "core")
NEAR = ("x", "zh", "core")
DEVICES = ("x", "zh", "zl", "core", "y")
F32 = jnp.float32
BF16 = jnp.bfloat16
STRIPES = 4


def iota(shape, axis):
    return lax.broadcasted_iota(jnp.int32, shape, axis)


def split(value, size):
    return lax.shift_right_logical(value, jnp.int32(size.bit_length() - 1))


def product(a, b):
    return jnp.dot(a, b, preferred_element_type=F32)


def product_nt(a, b):
    return lax.dot_general(a, b, (((1,), (1,)), ((), ())), preferred_element_type=F32)


def slots(wanted, row_count, owners):
    entries = wanted.shape[1]
    owner = split(wanted, row_count)
    source_row = wanted & (row_count - 1)
    owner_hot = (iota((owners, entries), 0) == owner).astype(F32)
    before = (iota((entries, entries), 0) < iota((entries, entries), 1)).astype(F32)
    earlier = product(owner_hot.astype(BF16), before.astype(BF16))
    slot = jnp.sum(owner_hot * earlier, axis=0, keepdims=True).astype(jnp.int32)
    return owner, owner_hot, slot, source_row


def request_kernel(row_count, owners, wanted_ref, table_ref):
    owner, owner_hot, slot, source_row = slots(wanted_ref[...], row_count, owners)
    slot_hot = (iota((CAP, slot.shape[1]), 0) == slot).astype(F32).astype(BF16)
    high, low = split(source_row, 32), source_row & 31
    table = 32.0 * product_nt((owner_hot * high.astype(F32)).astype(BF16), slot_hot)
    table = table + product_nt((owner_hot * low.astype(F32)).astype(BF16), slot_hot)
    table_ref[...] = table.astype(jnp.int32)


def select_kernel(row_count, owners, wanted_ref, select_ref):
    owner, _, slot, _ = slots(wanted_ref[...], row_count, owners)
    entries = slot.shape[1]
    flat = (owner * CAP + slot).astype(F32)
    diagonal = iota((entries, entries), 0) == iota((entries, entries), 1)
    column = jnp.sum(jnp.where(diagonal, flat, 0.0), axis=1, keepdims=True).astype(jnp.int32)
    select_ref[...] = (iota((entries, owners * CAP), 1) == column).astype(F32).astype(BF16)


def outgoing_kernel(sizes, chunk, incoming_ref, coeffs_ref, out_ref, hot_ref, coeffs_buf, out_buf, in_sems, out_sems):
    nx, nz, nc, _ = sizes
    owners = nx * nz * nc
    row_count = coeffs_ref.shape[0]
    group = nx * nc * CAP
    order = coeffs_buf.shape[2]
    loads = []
    for k in range(nz):
        loads.append(pltpu.make_async_copy(coeffs_ref.at[:, k * order:(k + 1) * order], coeffs_buf.at[k], in_sems.at[k]))
        loads[-1].start()

    places = owners * CAP
    table = incoming_ref[...]
    high, low = split(table, 32), table & 31
    place = iota((places, owners), 0)
    by_z, by_x, by_core = split(place, group), split(place & (group - 1), nc * CAP), split(place & (nc * CAP - 1), CAP)
    owner = by_x * (nz * nc) + ((by_z & 1) * 2 + split(by_z, 2)) * nc + by_core
    place_owner = (owner == iota((places, owners), 1)).astype(F32).astype(BF16)
    spread = 32.0 * product(place_owner, high.astype(F32).astype(BF16))
    spread = spread + product(place_owner, low.astype(F32).astype(BF16))
    mine = (iota((places, CAP), 0) & (CAP - 1)) == iota((places, CAP), 1)
    column = jnp.sum(jnp.where(mine, spread, 0.0), axis=1, keepdims=True).astype(jnp.int32)
    hot_ref[...] = (iota((places, row_count), 1) == column).astype(F32).astype(BF16)

    stores = []
    for k in range(nz):
        loads[k].wait()
        parity = k % 2 ^ chunk
        rows = product(hot_ref[parity * 2 * group:(parity + 1) * 2 * group, :], coeffs_buf[k]).astype(BF16)
        out_buf[k] = rows.reshape(out_buf.shape[1:])
        for near in range(2):
            slot = k * 2 + near
            target = out_ref.at[:, near * 2 + parity, :, :, k // 2 * order:(k // 2 + 1) * order]
            stores.append(pltpu.make_async_copy(out_buf.at[k, near], target, out_sems.at[slot]))
            stores[-1].start()
    for store in stores:
        store.wait()


def half_kernel(chunk, turn_ref, select_ref, local_ref, remote_ref, coeffs_ref, replies_ref, beta_ref, *refs):
    out_refs = refs[:STRIPES]
    select, local, remote, coeffs, replies, beta, mix, out_buf, base_sems, in_sems, beta_sems, out_sems = refs[STRIPES:]
    channels, blocks = local.shape[:2]
    count, _, order = coeffs.shape
    pieces = out_buf.shape[1]
    piece = order // pieces

    base = [
        pltpu.make_async_copy(source, target, base_sems.at[at])
        for at, (source, target) in enumerate([(select_ref, select), (local_ref, local), (remote_ref, remote)])
    ]
    rows_loads, reply_loads, beta_loads = [], [], []
    for i in range(count):
        column = turn_ref[chunk * count + i]
        source = replies_ref.at[:, :, i * order:(i + 1) * order]
        reply_loads.append(pltpu.make_async_copy(source, replies.at[i], in_sems.at[i]))
        source = coeffs_ref.at[:, pl.ds(pl.multiple_of(column * order, order), order)]
        rows_loads.append(pltpu.make_async_copy(source, coeffs.at[i], in_sems.at[count + i]))
        group = []
        for n in range(pieces):
            for channel in range(channels):
                source = beta_ref.at[channel, column, n * piece:(n + 1) * piece]
                target = beta.at[i, n, :, channel * order:(channel + 1) * order]
                group.append(pltpu.make_async_copy(source, target, beta_sems.at[i, n * channels + channel]))
        beta_loads.append(group)
    base[0].start()
    for i in range(count):
        reply_loads[i].start()
        rows_loads[i].start()
        if i == 0:
            base[1].start()
            base[2].start()
        for load in beta_loads[i]:
            load.start()

    base[0].wait()
    stores = []
    for i in range(count):
        reply_loads[i].wait()
        far_rows = product(select[...], replies[i].reshape(-1, order)).astype(BF16)
        rows_loads[i].wait()
        if i == 0:
            base[1].wait()
            base[2].wait()
        for block in range(blocks):
            low, high = block * ABLK, (block + 1) * ABLK
            rows = jnp.concatenate([coeffs[i, low:high, :], far_rows[low:high]], axis=0)
            for channel in range(channels):
                coupling = jnp.concatenate([local[channel, block], remote[channel, block, 0]], axis=1)
                mix[low:high, channel * order:(channel + 1) * order] = product(coupling, rows).astype(BF16)
        for n in range(pieces):
            for load in beta_loads[i][n * channels:(n + 1) * channels]:
                load.wait()
            total = product_nt(beta[i, n], mix[...]).astype(BF16)
            stripe = out_buf.shape[4]
            for index in range(STRIPES):
                out_buf[i, n, index] = total[:, index * stripe:(index + 1) * stripe]
                target = out_refs[index].at[i, n]
                slot = (i * pieces + n) * STRIPES + index
                stores.append(pltpu.make_async_copy(out_buf.at[i, n, index], target, out_sems.at[slot]))
                stores[-1].start()
    for store in stores:
        store.wait()


def own_kernel(*refs):
    *in_refs, out_ref = refs
    stripe = in_refs[0].shape[3]
    for index, in_ref in enumerate(in_refs):
        out_ref[index * stripe:(index + 1) * stripe, :] = in_ref[0, 0].T


def collect_kernel(order_ref, *refs):
    *in_refs, out_ref, buf, in_sems, out_sems = refs
    loads = [pltpu.make_async_copy(ref, buf.at[at], in_sems.at[at]) for at, ref in enumerate(in_refs)]
    for load in loads:
        load.start()
    stores = []
    for at in range(len(in_refs)):
        loads[at].wait()
        stores.append(pltpu.make_async_copy(buf.at[at], out_ref.at[order_ref[at]], out_sems.at[at]))
        stores[-1].start()
    for store in stores:
        store.wait()


def pick_kernel(order_ref, in_ref, *refs):
    *out_refs, buf, in_sems, out_sems = refs
    count = len(out_refs)
    loads = [pltpu.make_async_copy(in_ref.at[order_ref[at]], buf.at[at], in_sems.at[at]) for at in range(count)]
    for load in loads:
        load.start()
    stores = []
    for at in range(count):
        loads[at].wait()
        stores.append(pltpu.make_async_copy(buf.at[at], out_refs[at], out_sems.at[at]))
        stores[-1].start()
    for store in stores:
        store.wait()


def final_kernel(chunk, turn_ref, own_ref, *refs):
    own_buf, mirror_buf, out_buf, own_sems, mirror_sems, out_sems = refs[-6:]
    out_ref, mirror_refs = refs[-7], refs[:-7]
    _, per_chunk, nc, piece, stripe = mirror_buf.shape
    loads = []
    for i in range(per_chunk):
        cols = slice(i * nc * piece, (i + 1) * nc * piece)
        group = [pltpu.make_async_copy(own_ref.at[:, cols], own_buf.at[:, cols], own_sems.at[i])]
        for j in range(STRIPES):
            if chunk:
                z_flip = (turn_ref[6] + 1 + j // 2) & 1
                source = mirror_refs[0].at[(turn_ref[5] + j) & (STRIPES - 1), (i + z_flip) & 1]
            else:
                source = mirror_refs[j].at[i]
            group.append(pltpu.make_async_copy(source, mirror_buf.at[j, i], mirror_sems.at[i * STRIPES + j]))
        for load in group:
            load.start()
        loads.append(group)
    stores = []
    for i, group in enumerate(loads):
        for load in group:
            load.wait()
        for n in range(nc):
            slot = i * nc + n
            for j in range(STRIPES):
                at = j if chunk else (2 * STRIPES + turn_ref[4] - j) & (STRIPES - 1)
                own_cols = pl.ds(pl.multiple_of(slot * piece + at * stripe, stripe), stripe)
                cols = pl.ds(pl.multiple_of(at * stripe, stripe), stripe)
                mirror = mirror_buf[j, i, n].astype(F32)
                out_buf[slot, :, cols] = (own_buf[:, own_cols].astype(F32) + mirror).astype(BF16)
            start = pl.multiple_of((turn_ref[chunk * per_chunk + i] * nc + n) * piece, piece)
            store = pltpu.make_async_copy(out_buf.at[slot], out_ref.at[:, pl.ds(start, piece)], out_sems.at[slot])
            store.start()
            stores.append(store)
    for store in stores:
        store.wait()


def params(mebibytes):
    return pltpu.CompilerParams(vmem_limit_bytes=mebibytes * 2**20)


def estimate(flops, mebibytes):
    return pl.CostEstimate(flops=flops, bytes_accessed=mebibytes * 2**20, transcendentals=0)


def device_pairs(sizes, move):
    nx, nz, nc, ny = sizes

    def at(x, z, core, y):
        return ((x % nx * nz + z % nz) * nc + core % nc) * ny + y % ny

    places = [(x, z, c, y) for x in range(nx) for z in range(nz) for c in range(nc) for y in range(ny)]
    return [(at(*place), at(*move(*place))) for place in places]


def prefetched(kernel, name, inputs, out_shape, scratch, flops, mebibytes, aliases={}):
    return pl.pallas_call(
        kernel,
        grid_spec=pltpu.PrefetchScalarGridSpec(
            num_scalar_prefetch=1,
            grid=(1,),
            in_specs=[pl.BlockSpec(memory_space=pl.ANY)] * inputs,
            out_specs=jax.tree.map(lambda _: pl.BlockSpec(memory_space=pl.ANY), out_shape),
            scratch_shapes=scratch,
        ),
        out_shape=out_shape,
        compiler_params=params(56),
        cost_estimate=estimate(flops, mebibytes),
        input_output_aliases=aliases,
        name=name,
    )


def on_device(sizes, coeffs, local_coupling, remote_coupling, beta_coupling, exc_rows):
    nx, nz, nc, ny = sizes
    owners = nx * nz * nc
    row_count, col_count = coeffs.shape
    channels, _, order, _ = beta_coupling.shape
    my_x, my_y, parity = lax.axis_index("x"), lax.axis_index("y"), lax.axis_index("zl")
    wanted = exc_rows.reshape(1, row_count)
    places = owners * CAP
    chunks, per_chunk = 2, nz // 2
    piece = order // nc
    stripe = row_count // STRIPES
    dma = pltpu.SemaphoreType.DMA

    table = pl.pallas_call(
        functools.partial(request_kernel, row_count, owners),
        out_shape=jax.ShapeDtypeStruct((owners, CAP), jnp.int32),
        name="requests",
    )(wanted)
    incoming = lax.all_to_all(table, ALPHA, split_axis=0, concat_axis=0, tiled=True)
    select = pl.pallas_call(
        functools.partial(select_kernel, row_count, owners),
        out_shape=jax.ShapeDtypeStruct((row_count, places), BF16),
        compiler_params=params(56),
        name="select",
    )(wanted)
    stripes = jnp.arange(STRIPES, dtype=jnp.int32)
    columns = [parity, 2 + parity, 1 - parity, 3 - parity]
    scalars = [*columns, (my_y - my_x) % STRIPES, (my_x + my_y) % STRIPES, parity]
    turn = jnp.stack(scalars).astype(jnp.int32)
    first_order = (my_y - stripes) % STRIPES
    second_order = (my_x - my_y - stripes) % STRIPES
    pick_order = (my_y + stripes) % STRIPES

    replies = []
    for chunk in range(chunks):
        outgoing = pl.pallas_call(
            functools.partial(outgoing_kernel, sizes, chunk),
            in_specs=[pl.BlockSpec(memory_space=pltpu.VMEM), pl.BlockSpec(memory_space=pl.ANY)],
            out_specs=pl.BlockSpec(memory_space=pl.ANY),
            out_shape=jax.ShapeDtypeStruct((nx, nz, nc, CAP, per_chunk * order), BF16),
            scratch_shapes=[
                pltpu.VMEM((places, row_count), BF16),
                pltpu.VMEM((nz, row_count, order), BF16),
                pltpu.VMEM((nz, 2, nx, nc, CAP, order), BF16),
                dma((nz,)),
                dma((nz * 2,)),
            ],
            compiler_params=params(56),
            cost_estimate=estimate(2 * 10**9, 10),
            name="outgoing",
        )(incoming, coeffs)
        outgoing = outgoing.reshape(owners, CAP, per_chunk * order)
        replies.append(lax.all_to_all(outgoing, ALPHA, split_axis=0, concat_axis=0, tiled=True))

    blocks_shape = jax.ShapeDtypeStruct((per_chunk, nc, piece, stripe), BF16)
    group_shape = jax.ShapeDtypeStruct((STRIPES, per_chunk, nc, piece, stripe), BF16)

    def half(chunk):
        scratch = [
            pltpu.VMEM((row_count, places), BF16),
            pltpu.VMEM(local_coupling.shape, BF16),
            pltpu.VMEM(remote_coupling.shape, BF16),
            pltpu.VMEM((per_chunk, row_count, order), BF16),
            pltpu.VMEM((per_chunk, owners, CAP, order), BF16),
            pltpu.VMEM((per_chunk, nc, piece, channels * order), BF16),
            pltpu.VMEM((row_count, channels * order), BF16),
            pltpu.VMEM((per_chunk, nc, STRIPES, piece, stripe), BF16),
            dma((3,)),
            dma((2 * per_chunk,)),
            dma((per_chunk, nc * channels)),
            dma((per_chunk * nc * STRIPES,)),
        ]
        call = prefetched(functools.partial(half_kernel, chunk), "half", 6, [blocks_shape] * STRIPES, scratch, 8 * 10**9, 18)
        return call(turn, select, local_coupling, remote_coupling, coeffs, replies[chunk], beta_coupling)

    def own(blocks_of):
        return pl.pallas_call(
            own_kernel,
            grid=(per_chunk, nc),
            in_specs=[pl.BlockSpec((1, 1, piece, stripe), lambda i, n: (i, n, 0, 0))] * STRIPES,
            out_specs=pl.BlockSpec((row_count, piece), lambda i, n: (0, i * nc + n)),
            out_shape=jax.ShapeDtypeStruct((row_count, per_chunk * order), BF16),
            compiler_params=params(56),
            cost_estimate=estimate(10**9, 4),
            name="own",
        )(*blocks_of)

    moving = [pltpu.VMEM(group_shape.shape, BF16), dma((STRIPES,)), dma((STRIPES,))]

    def exchange(arrays, to):
        grouped = prefetched(collect_kernel, "collect", STRIPES, group_shape, moving, 0, 4)(to, *arrays)
        return grouped

    def all_near(grouped):
        grouped = grouped.reshape(nx * per_chunk * nc, piece, stripe)
        return lax.all_to_all(grouped, NEAR, split_axis=0, concat_axis=0, tiled=True).reshape(group_shape.shape)

    def permute(block, move):
        return lax.ppermute(block, DEVICES, device_pairs(sizes, move))

    first = half(0)
    spread = [first[0]] + [permute(first[j], lambda x, z, c, y: (x, z, c, y + j)) for j in range(1, STRIPES)]
    first_grouped = exchange(spread, first_order)
    replies[1], first_grouped = lax.optimization_barrier((replies[1], first_grouped))
    first_mirror = all_near(first_grouped)
    second = half(1)
    swapped = {}
    for j in (0, 2, 1, 3):
        step = 1 if j < 2 else -1
        swapped[j] = permute(second[j], lambda x, z, c, y: (x + y + j, z + step, c, x))
    picked = prefetched(pick_kernel, "pick", 1, [blocks_shape] * STRIPES, moving, 0, 4)(pick_order, first_mirror)
    early = lax.optimization_barrier((swapped[0], swapped[2], *picked))
    swapped[0], swapped[2], picked = early[0], early[1], early[2:]
    second_mirror = all_near(exchange([swapped[j] for j in range(STRIPES)], second_order))

    arrived = [picked[0]] + [permute(picked[j], lambda x, z, c, y: (x, z, c, y + j)) for j in range(1, STRIPES)]

    scratch = [
        pltpu.VMEM((row_count, per_chunk * order), BF16),
        pltpu.VMEM((STRIPES, per_chunk, nc, piece, stripe), BF16),
        pltpu.VMEM((per_chunk * nc, row_count, piece), BF16),
        dma((per_chunk,)),
        dma((per_chunk * STRIPES,)),
        dma((per_chunk * nc,)),
    ]
    out_shape = jax.ShapeDtypeStruct((row_count, col_count), BF16)
    final = prefetched(functools.partial(final_kernel, 0), "final", 1 + STRIPES, out_shape, scratch, 10**7, 6)
    sigma = final(turn, own(first), *arrived)
    final = prefetched(functools.partial(final_kernel, 1), "final", 3, out_shape, scratch, 10**7, 6, {3: 0})
    return final(turn, own(second), second_mirror, sigma)


def solution(mesh):
    sizes = (4, 4, 2, 4)
    cube = Mesh(mesh.devices.reshape(4, 2, 2, 2, 4), DEVICES)
    return jax.shard_map(
        functools.partial(on_device, sizes),
        mesh=cube,
        in_specs=(
            P(ALPHA, "y"),
            P(None, ALPHA, None, None),
            P(None, ALPHA, None, None, None),
            P(None, "y", None, None),
            P(ALPHA, None, None),
        ),
        out_specs=P(ALPHA, "y"),
        check_vma=False,
    )
```

```python
import functools

import jax
import jax.numpy as jnp
from jax import lax
from jax.experimental import pallas as pl
from jax.experimental.pallas import tpu as pltpu
from jax.sharding import Mesh, PartitionSpec as P

ABLK = 256
CAP = 32
ALPHA = ("x", "zh", "zl", "core")
NEAR = ("x", "zh", "core")
DEVICES = ("x", "zh", "zl", "core", "y")
F32 = jnp.float32
BF16 = jnp.bfloat16
STRIPES = 4


def iota(shape, axis):
    return lax.broadcasted_iota(jnp.int32, shape, axis)


def split(value, size):
    return lax.shift_right_logical(value, jnp.int32(size.bit_length() - 1))


def product(a, b):
    return jnp.dot(a, b, preferred_element_type=F32)


def product_nt(a, b):
    return lax.dot_general(a, b, (((1,), (1,)), ((), ())), preferred_element_type=F32)


def slots(wanted, row_count, owners):
    entries = wanted.shape[1]
    owner = split(wanted, row_count)
    source_row = wanted & (row_count - 1)
    owner_hot = (iota((owners, entries), 0) == owner).astype(F32)
    before = (iota((entries, entries), 0) < iota((entries, entries), 1)).astype(F32)
    earlier = product(owner_hot.astype(BF16), before.astype(BF16))
    slot = jnp.sum(owner_hot * earlier, axis=0, keepdims=True).astype(jnp.int32)
    return owner, owner_hot, slot, source_row


def request_kernel(row_count, owners, wanted_ref, table_ref):
    owner, owner_hot, slot, source_row = slots(wanted_ref[...], row_count, owners)
    slot_hot = (iota((CAP, slot.shape[1]), 0) == slot).astype(F32).astype(BF16)
    high, low = split(source_row, 32), source_row & 31
    table = 32.0 * product_nt((owner_hot * high.astype(F32)).astype(BF16), slot_hot)
    table = table + product_nt((owner_hot * low.astype(F32)).astype(BF16), slot_hot)
    table_ref[...] = table.astype(jnp.int32)


def select_kernel(row_count, owners, wanted_ref, select_ref):
    owner, _, slot, _ = slots(wanted_ref[...], row_count, owners)
    entries = slot.shape[1]
    flat = (owner * CAP + slot).astype(F32)
    diagonal = iota((entries, entries), 0) == iota((entries, entries), 1)
    column = jnp.sum(jnp.where(diagonal, flat, 0.0), axis=1, keepdims=True).astype(jnp.int32)
    select_ref[...] = (iota((entries, owners * CAP), 1) == column).astype(F32).astype(BF16)


def outgoing_kernel(sizes, chunk, incoming_ref, coeffs_ref, out_ref, hot_ref, coeffs_buf, out_buf, in_sems, out_sems):
    nx, nz, nc, _ = sizes
    owners = nx * nz * nc
    row_count = coeffs_ref.shape[0]
    group = nx * nc * CAP
    order = coeffs_buf.shape[2]
    loads = []
    for k in range(nz):
        loads.append(pltpu.make_async_copy(coeffs_ref.at[:, k * order:(k + 1) * order], coeffs_buf.at[k], in_sems.at[k]))
        loads[-1].start()

    places = owners * CAP
    table = incoming_ref[...]
    high, low = split(table, 32), table & 31
    place = iota((places, owners), 0)
    by_z, by_x, by_core = split(place, group), split(place & (group - 1), nc * CAP), split(place & (nc * CAP - 1), CAP)
    owner = by_x * (nz * nc) + ((by_z & 1) * 2 + split(by_z, 2)) * nc + by_core
    place_owner = (owner == iota((places, owners), 1)).astype(F32).astype(BF16)
    spread = 32.0 * product(place_owner, high.astype(F32).astype(BF16))
    spread = spread + product(place_owner, low.astype(F32).astype(BF16))
    mine = (iota((places, CAP), 0) & (CAP - 1)) == iota((places, CAP), 1)
    column = jnp.sum(jnp.where(mine, spread, 0.0), axis=1, keepdims=True).astype(jnp.int32)
    hot_ref[...] = (iota((places, row_count), 1) == column).astype(F32).astype(BF16)

    stores = []
    for k in range(nz):
        loads[k].wait()
        parity = k % 2 ^ chunk
        rows = product(hot_ref[parity * 2 * group:(parity + 1) * 2 * group, :], coeffs_buf[k]).astype(BF16)
        out_buf[k] = rows.reshape(out_buf.shape[1:])
        for near in range(2):
            slot = k * 2 + near
            target = out_ref.at[:, near * 2 + parity, :, :, k // 2 * order:(k // 2 + 1) * order]
            stores.append(pltpu.make_async_copy(out_buf.at[k, near], target, out_sems.at[slot]))
            stores[-1].start()
    for store in stores:
        store.wait()


def half_kernel(chunk, turn_ref, select_ref, local_ref, remote_ref, coeffs_ref, replies_ref, beta_ref, *refs):
    out_refs = refs[:STRIPES]
    select, local, remote, coeffs, replies, beta, mix, out_buf, base_sems, in_sems, beta_sems, out_sems = refs[STRIPES:]
    channels, blocks = local.shape[:2]
    count, _, order = coeffs.shape
    pieces = out_buf.shape[1]
    piece = order // pieces

    base = [
        pltpu.make_async_copy(source, target, base_sems.at[at])
        for at, (source, target) in enumerate([(select_ref, select), (local_ref, local), (remote_ref, remote)])
    ]
    rows_loads, reply_loads, beta_loads = [], [], []
    for i in range(count):
        column = turn_ref[chunk * count + i]
        source = replies_ref.at[:, :, i * order:(i + 1) * order]
        reply_loads.append(pltpu.make_async_copy(source, replies.at[i], in_sems.at[i]))
        source = coeffs_ref.at[:, pl.ds(pl.multiple_of(column * order, order), order)]
        rows_loads.append(pltpu.make_async_copy(source, coeffs.at[i], in_sems.at[count + i]))
        group = []
        for n in range(pieces):
            for channel in range(channels):
                source = beta_ref.at[channel, column, n * piece:(n + 1) * piece]
                target = beta.at[i, n, :, channel * order:(channel + 1) * order]
                group.append(pltpu.make_async_copy(source, target, beta_sems.at[i, n * channels + channel]))
        beta_loads.append(group)
    waves = [[base[0], reply_loads[0]], [rows_loads[0], *base[1:]]]
    for i in range(count):
        if i:
            waves.append([reply_loads[i], rows_loads[i]])
        waves += [beta_loads[i][n * channels:(n + 1) * channels] for n in range(pieces)]

    def start_next():
        for load in waves.pop(0) if waves else []:
            load.start()

    for _ in range(3):
        start_next()
    base[0].wait()
    stores = []
    for i in range(count):
        reply_loads[i].wait()
        start_next()
        far_rows = product(select[...], replies[i].reshape(-1, order)).astype(BF16)
        rows_loads[i].wait()
        if i == 0:
            base[1].wait()
            base[2].wait()
            start_next()
        for block in range(blocks):
            low, high = block * ABLK, (block + 1) * ABLK
            rows = jnp.concatenate([coeffs[i, low:high, :], far_rows[low:high]], axis=0)
            for channel in range(channels):
                coupling = jnp.concatenate([local[channel, block], remote[channel, block, 0]], axis=1)
                mix[low:high, channel * order:(channel + 1) * order] = product(coupling, rows).astype(BF16)
        for n in range(pieces):
            for load in beta_loads[i][n * channels:(n + 1) * channels]:
                load.wait()
            start_next()
            total = product_nt(beta[i, n], mix[...]).astype(BF16)
            stripe = out_buf.shape[4]
            for index in range(STRIPES):
                out_buf[i, n, index] = total[:, index * stripe:(index + 1) * stripe]
                target = out_refs[index].at[i, n]
                slot = (i * pieces + n) * STRIPES + index
                stores.append(pltpu.make_async_copy(out_buf.at[i, n, index], target, out_sems.at[slot]))
                stores[-1].start()
    for store in stores:
        store.wait()


def own_kernel(*refs):
    *in_refs, out_ref = refs
    stripe = in_refs[0].shape[3]
    for index, in_ref in enumerate(in_refs):
        out_ref[index * stripe:(index + 1) * stripe, :] = in_ref[0, 0].T


def collect_kernel(order_ref, *refs):
    *in_refs, out_ref, buf, in_sems, out_sems = refs
    loads = [pltpu.make_async_copy(ref, buf.at[at], in_sems.at[at]) for at, ref in enumerate(in_refs)]
    for load in loads:
        load.start()
    stores = []
    for at in range(len(in_refs)):
        loads[at].wait()
        stores.append(pltpu.make_async_copy(buf.at[at], out_ref.at[order_ref[at]], out_sems.at[at]))
        stores[-1].start()
    for store in stores:
        store.wait()


def pick_kernel(order_ref, in_ref, *refs):
    *out_refs, buf, in_sems, out_sems = refs
    count = len(out_refs)
    loads = [pltpu.make_async_copy(in_ref.at[order_ref[at]], buf.at[at], in_sems.at[at]) for at in range(count)]
    for load in loads:
        load.start()
    stores = []
    for at in range(count):
        loads[at].wait()
        stores.append(pltpu.make_async_copy(buf.at[at], out_refs[at], out_sems.at[at]))
        stores[-1].start()
    for store in stores:
        store.wait()


def final_kernel(turn_ref, *refs):
    own_buf, mirror_buf, out_buf, own_sems, mirror_sems, out_sems = refs[-6:]
    out_ref = refs[-7]
    chunks, row_count, width = own_buf.shape
    _, _, per_chunk, nc, piece, stripe = mirror_buf.shape
    own_refs, first_refs, second_ref = refs[:chunks], refs[chunks:chunks + STRIPES], refs[chunks + STRIPES]
    loads = []
    for chunk in (1, 0):
        for i in range(per_chunk):
            cols = slice(i * nc * piece, (i + 1) * nc * piece)
            source, target = own_refs[chunk].at[:, cols], own_buf.at[chunk, :, cols]
            group = [pltpu.make_async_copy(source, target, own_sems.at[chunk * per_chunk + i])]
            for j in range(STRIPES):
                if chunk:
                    z_flip = (turn_ref[6] + 1 + j // 2) & 1
                    source = second_ref.at[(turn_ref[5] + j) & (STRIPES - 1), (i + z_flip) & 1]
                else:
                    source = first_refs[j].at[i]
                slot = (chunk * per_chunk + i) * STRIPES + j
                group.append(pltpu.make_async_copy(source, mirror_buf.at[chunk, j, i], mirror_sems.at[slot]))
            for load in group:
                load.start()
            loads.append((chunk, i, group))
    stores = []
    for chunk, i, group in loads:
        for load in group:
            load.wait()
        for n in range(nc):
            slot = (chunk * per_chunk + i) * nc + n
            base = (i * nc + n) * piece
            for j in range(STRIPES):
                at = j if chunk else (2 * STRIPES + turn_ref[4] - j) & (STRIPES - 1)
                own_cols = pl.ds(pl.multiple_of(base + at * stripe, stripe), stripe)
                cols = pl.ds(pl.multiple_of(at * stripe, stripe), stripe)
                mirror = mirror_buf[chunk, j, i, n].astype(F32)
                out_buf[slot, :, cols] = (own_buf[chunk, :, own_cols].astype(F32) + mirror).astype(BF16)
            start = pl.multiple_of((turn_ref[chunk * per_chunk + i] * nc + n) * piece, piece)
            store = pltpu.make_async_copy(out_buf.at[slot], out_ref.at[:, pl.ds(start, piece)], out_sems.at[slot])
            store.start()
            stores.append(store)
    for store in stores:
        store.wait()


def params(mebibytes):
    return pltpu.CompilerParams(vmem_limit_bytes=mebibytes * 2**20)


def estimate(flops, mebibytes):
    return pl.CostEstimate(flops=flops, bytes_accessed=mebibytes * 2**20, transcendentals=0)


def device_pairs(sizes, move):
    nx, nz, nc, ny = sizes

    def at(x, z, core, y):
        return ((x % nx * nz + z % nz) * nc + core % nc) * ny + y % ny

    places = [(x, z, c, y) for x in range(nx) for z in range(nz) for c in range(nc) for y in range(ny)]
    return [(at(*place), at(*move(*place))) for place in places]


def prefetched(kernel, name, inputs, out_shape, scratch, flops, mebibytes):
    return pl.pallas_call(
        kernel,
        grid_spec=pltpu.PrefetchScalarGridSpec(
            num_scalar_prefetch=1,
            grid=(1,),
            in_specs=[pl.BlockSpec(memory_space=pl.ANY)] * inputs,
            out_specs=jax.tree.map(lambda _: pl.BlockSpec(memory_space=pl.ANY), out_shape),
            scratch_shapes=scratch,
        ),
        out_shape=out_shape,
        compiler_params=params(56),
        cost_estimate=estimate(flops, mebibytes),
        name=name,
    )


def on_device(sizes, coeffs, local_coupling, remote_coupling, beta_coupling, exc_rows):
    nx, nz, nc, ny = sizes
    owners = nx * nz * nc
    row_count, col_count = coeffs.shape
    channels, _, order, _ = beta_coupling.shape
    my_x, my_y, parity = lax.axis_index("x"), lax.axis_index("y"), lax.axis_index("zl")
    wanted = exc_rows.reshape(1, row_count)
    places = owners * CAP
    chunks, per_chunk = 2, nz // 2
    piece = order // nc
    stripe = row_count // STRIPES
    dma = pltpu.SemaphoreType.DMA

    table = pl.pallas_call(
        functools.partial(request_kernel, row_count, owners),
        out_shape=jax.ShapeDtypeStruct((owners, CAP), jnp.int32),
        name="requests",
    )(wanted)
    incoming = lax.all_to_all(table, ALPHA, split_axis=0, concat_axis=0, tiled=True)
    select = pl.pallas_call(
        functools.partial(select_kernel, row_count, owners),
        out_shape=jax.ShapeDtypeStruct((row_count, places), BF16),
        compiler_params=params(56),
        name="select",
    )(wanted)
    stripes = jnp.arange(STRIPES, dtype=jnp.int32)
    columns = [parity, 2 + parity, 1 - parity, 3 - parity]
    scalars = [*columns, (my_y - my_x) % STRIPES, (my_x + my_y) % STRIPES, parity]
    turn = jnp.stack(scalars).astype(jnp.int32)
    first_order = (my_y - stripes) % STRIPES
    second_order = (my_x - my_y - stripes) % STRIPES
    pick_order = (my_y + stripes) % STRIPES

    replies = []
    for chunk in range(chunks):
        outgoing = pl.pallas_call(
            functools.partial(outgoing_kernel, sizes, chunk),
            in_specs=[pl.BlockSpec(memory_space=pltpu.VMEM), pl.BlockSpec(memory_space=pl.ANY)],
            out_specs=pl.BlockSpec(memory_space=pl.ANY),
            out_shape=jax.ShapeDtypeStruct((nx, nz, nc, CAP, per_chunk * order), BF16),
            scratch_shapes=[
                pltpu.VMEM((places, row_count), BF16),
                pltpu.VMEM((nz, row_count, order), BF16),
                pltpu.VMEM((nz, 2, nx, nc, CAP, order), BF16),
                dma((nz,)),
                dma((nz * 2,)),
            ],
            compiler_params=params(56),
            cost_estimate=estimate(2 * 10**9, 10),
            name="outgoing",
        )(incoming, coeffs)
        outgoing = outgoing.reshape(owners, CAP, per_chunk * order)
        replies.append(lax.all_to_all(outgoing, ALPHA, split_axis=0, concat_axis=0, tiled=True))

    blocks_shape = jax.ShapeDtypeStruct((per_chunk, nc, piece, stripe), BF16)
    group_shape = jax.ShapeDtypeStruct((STRIPES, per_chunk, nc, piece, stripe), BF16)

    def half(chunk):
        scratch = [
            pltpu.VMEM((row_count, places), BF16),
            pltpu.VMEM(local_coupling.shape, BF16),
            pltpu.VMEM(remote_coupling.shape, BF16),
            pltpu.VMEM((per_chunk, row_count, order), BF16),
            pltpu.VMEM((per_chunk, owners, CAP, order), BF16),
            pltpu.VMEM((per_chunk, nc, piece, channels * order), BF16),
            pltpu.VMEM((row_count, channels * order), BF16),
            pltpu.VMEM((per_chunk, nc, STRIPES, piece, stripe), BF16),
            dma((3,)),
            dma((2 * per_chunk,)),
            dma((per_chunk, nc * channels)),
            dma((per_chunk * nc * STRIPES,)),
        ]
        call = prefetched(functools.partial(half_kernel, chunk), "half", 6, [blocks_shape] * STRIPES, scratch, 8 * 10**9, 18)
        return call(turn, select, local_coupling, remote_coupling, coeffs, replies[chunk], beta_coupling)

    def own(blocks_of):
        return pl.pallas_call(
            own_kernel,
            grid=(per_chunk, nc),
            in_specs=[pl.BlockSpec((1, 1, piece, stripe), lambda i, n: (i, n, 0, 0))] * STRIPES,
            out_specs=pl.BlockSpec((row_count, piece), lambda i, n: (0, i * nc + n)),
            out_shape=jax.ShapeDtypeStruct((row_count, per_chunk * order), BF16),
            compiler_params=params(56),
            cost_estimate=estimate(10**9, 4),
            name="own",
        )(*blocks_of)

    moving = [pltpu.VMEM(group_shape.shape, BF16), dma((STRIPES,)), dma((STRIPES,))]

    def exchange(arrays, to):
        grouped = prefetched(collect_kernel, "collect", STRIPES, group_shape, moving, 0, 4)(to, *arrays)
        return grouped

    def all_near(grouped):
        grouped = grouped.reshape(nx * per_chunk * nc, piece, stripe)
        return lax.all_to_all(grouped, NEAR, split_axis=0, concat_axis=0, tiled=True).reshape(group_shape.shape)

    def permute(block, move):
        return lax.ppermute(block, DEVICES, device_pairs(sizes, move))

    def along_y(arrays):
        moved = {0: arrays[0]}
        for j in (1, 3, 2):
            moved[j] = permute(arrays[j], lambda x, z, c, y: (x, z, c, y + j))
        return [moved[j] for j in range(STRIPES)]

    first = half(0)
    spread = along_y(first)
    first_grouped = exchange(spread, first_order)
    replies[1], first_grouped = lax.optimization_barrier((replies[1], first_grouped))
    first_mirror = all_near(first_grouped)
    second = half(1)
    swapped = {}
    for j in (0, 2, 1, 3):
        step = 1 if j < 2 else -1
        swapped[j] = permute(second[j], lambda x, z, c, y: (x + y + j, z + step, c, x))
    picked = prefetched(pick_kernel, "pick", 1, [blocks_shape] * STRIPES, moving, 0, 4)(pick_order, first_mirror)
    early = lax.optimization_barrier((swapped[0], swapped[2], *picked))
    swapped[0], swapped[2], picked = early[0], early[1], early[2:]
    second_mirror = all_near(exchange([swapped[j] for j in range(STRIPES)], second_order))

    arrived = along_y(picked)

    scratch = [
        pltpu.VMEM((chunks, row_count, per_chunk * order), BF16),
        pltpu.VMEM((chunks, STRIPES, per_chunk, nc, piece, stripe), BF16),
        pltpu.VMEM((nz * nc, row_count, piece), BF16),
        dma((nz,)),
        dma((nz * STRIPES,)),
        dma((nz * nc,)),
    ]
    out_shape = jax.ShapeDtypeStruct((row_count, col_count), BF16)
    final = prefetched(final_kernel, "final", chunks + STRIPES + 1, out_shape, scratch, 10**7, 12)
    return final(turn, own(first), own(second), *arrived, second_mirror)


def solution(mesh):
    sizes = (4, 4, 2, 4)
    cube = Mesh(mesh.devices.reshape(4, 2, 2, 2, 4), DEVICES)
    return jax.shard_map(
        functools.partial(on_device, sizes),
        mesh=cube,
        in_specs=(
            P(ALPHA, "y"),
            P(None, ALPHA, None, None),
            P(None, ALPHA, None, None, None),
            P(None, "y", None, None),
            P(ALPHA, None, None),
        ),
        out_specs=P(ALPHA, "y"),
        check_vma=False,
    )
```

```python
import functools

import jax
import jax.numpy as jnp
from jax import lax
from jax.experimental import pallas as pl
from jax.experimental.pallas import tpu as pltpu
from jax.sharding import Mesh, PartitionSpec as P

ABLK = 256
CAP = 32
ALPHA = ("x", "zh", "zl", "core")
NEAR = ("x", "zh", "core")
DEVICES = ("x", "zh", "zl", "core", "y")
F32 = jnp.float32
BF16 = jnp.bfloat16
STRIPES = 4


def iota(shape, axis):
    return lax.broadcasted_iota(jnp.int32, shape, axis)


def split(value, size):
    return lax.shift_right_logical(value, jnp.int32(size.bit_length() - 1))


def product(a, b):
    return jnp.dot(a, b, preferred_element_type=F32)


def product_nt(a, b):
    return lax.dot_general(a, b, (((1,), (1,)), ((), ())), preferred_element_type=F32)


def slots(wanted, row_count, owners):
    entries = wanted.shape[1]
    owner = split(wanted, row_count)
    source_row = wanted & (row_count - 1)
    owner_hot = (iota((owners, entries), 0) == owner).astype(F32)
    before = (iota((entries, entries), 0) < iota((entries, entries), 1)).astype(F32)
    earlier = product(owner_hot.astype(BF16), before.astype(BF16))
    slot = jnp.sum(owner_hot * earlier, axis=0, keepdims=True).astype(jnp.int32)
    return owner, owner_hot, slot, source_row


def request_kernel(row_count, owners, wanted_ref, table_ref):
    owner, owner_hot, slot, source_row = slots(wanted_ref[...], row_count, owners)
    slot_hot = (iota((CAP, slot.shape[1]), 0) == slot).astype(F32).astype(BF16)
    high, low = split(source_row, 32), source_row & 31
    table = 32.0 * product_nt((owner_hot * high.astype(F32)).astype(BF16), slot_hot)
    table = table + product_nt((owner_hot * low.astype(F32)).astype(BF16), slot_hot)
    table_ref[...] = table.astype(jnp.int32)


def select_kernel(row_count, owners, wanted_ref, select_ref):
    owner, _, slot, _ = slots(wanted_ref[...], row_count, owners)
    entries = slot.shape[1]
    flat = (owner * CAP + slot).astype(F32)
    diagonal = iota((entries, entries), 0) == iota((entries, entries), 1)
    column = jnp.sum(jnp.where(diagonal, flat, 0.0), axis=1, keepdims=True).astype(jnp.int32)
    select_ref[...] = (iota((entries, owners * CAP), 1) == column).astype(F32).astype(BF16)


def outgoing_kernel(sizes, chunk, incoming_ref, coeffs_ref, out_ref, hot_ref, coeffs_buf, out_buf, in_sems, out_sems):
    nx, nz, nc, _ = sizes
    owners = nx * nz * nc
    row_count = coeffs_ref.shape[0]
    group = nx * nc * CAP
    order = coeffs_buf.shape[2]
    loads = []
    for k in range(nz):
        loads.append(pltpu.make_async_copy(coeffs_ref.at[:, k * order:(k + 1) * order], coeffs_buf.at[k], in_sems.at[k]))
        loads[-1].start()

    places = owners * CAP
    table = incoming_ref[...]
    high, low = split(table, 32), table & 31
    place = iota((places, owners), 0)
    by_z, by_x, by_core = split(place, group), split(place & (group - 1), nc * CAP), split(place & (nc * CAP - 1), CAP)
    owner = by_x * (nz * nc) + ((by_z & 1) * 2 + split(by_z, 2)) * nc + by_core
    place_owner = (owner == iota((places, owners), 1)).astype(F32).astype(BF16)
    spread = 32.0 * product(place_owner, high.astype(F32).astype(BF16))
    spread = spread + product(place_owner, low.astype(F32).astype(BF16))
    mine = (iota((places, CAP), 0) & (CAP - 1)) == iota((places, CAP), 1)
    column = jnp.sum(jnp.where(mine, spread, 0.0), axis=1, keepdims=True).astype(jnp.int32)
    hot_ref[...] = (iota((places, row_count), 1) == column).astype(F32).astype(BF16)

    stores = []
    for k in range(nz):
        loads[k].wait()
        parity = k % 2 ^ chunk
        rows = product(hot_ref[parity * 2 * group:(parity + 1) * 2 * group, :], coeffs_buf[k]).astype(BF16)
        out_buf[k] = rows.reshape(out_buf.shape[1:])
        for near in range(2):
            slot = k * 2 + near
            target = out_ref.at[:, near * 2 + parity, :, :, k // 2 * order:(k // 2 + 1) * order]
            stores.append(pltpu.make_async_copy(out_buf.at[k, near], target, out_sems.at[slot]))
            stores[-1].start()
    for store in stores:
        store.wait()


def half_kernel(chunk, turn_ref, select_ref, local_ref, remote_ref, coeffs_ref, replies_ref, beta_ref, *refs):
    out_refs = refs[:STRIPES]
    select, local, remote, coeffs, replies, beta, mix, out_buf, base_sems, in_sems, beta_sems, out_sems = refs[STRIPES:]
    channels, blocks = local.shape[:2]
    count, _, order = coeffs.shape
    pieces = out_buf.shape[1]
    piece = order // pieces

    base = [
        pltpu.make_async_copy(source, target, base_sems.at[at])
        for at, (source, target) in enumerate([(select_ref, select), (local_ref, local), (remote_ref, remote)])
    ]
    rows_loads, reply_loads, beta_loads = [], [], []
    for i in range(count):
        column = turn_ref[chunk * count + i]
        source = replies_ref.at[:, :, i * order:(i + 1) * order]
        reply_loads.append(pltpu.make_async_copy(source, replies.at[i], in_sems.at[i]))
        source = coeffs_ref.at[:, pl.ds(pl.multiple_of(column * order, order), order)]
        rows_loads.append(pltpu.make_async_copy(source, coeffs.at[i], in_sems.at[count + i]))
        group = []
        for n in range(pieces):
            for channel in range(channels):
                source = beta_ref.at[channel, column, n * piece:(n + 1) * piece]
                target = beta.at[i, n, :, channel * order:(channel + 1) * order]
                group.append(pltpu.make_async_copy(source, target, beta_sems.at[i, n * channels + channel]))
        beta_loads.append(group)
    waves = [[base[0], reply_loads[0]], [rows_loads[0], *base[1:]]]
    for i in range(count):
        if i:
            waves.append([reply_loads[i], rows_loads[i]])
        waves += [beta_loads[i][n * channels:(n + 1) * channels] for n in range(pieces)]

    def start_next():
        for load in waves.pop(0) if waves else []:
            load.start()

    for _ in range(3):
        start_next()
    base[0].wait()
    stores = []
    for i in range(count):
        reply_loads[i].wait()
        start_next()
        far_rows = product(select[...], replies[i].reshape(-1, order)).astype(BF16)
        rows_loads[i].wait()
        if i == 0:
            base[1].wait()
            base[2].wait()
            start_next()
        for block in range(blocks):
            low, high = block * ABLK, (block + 1) * ABLK
            rows = jnp.concatenate([coeffs[i, low:high, :], far_rows[low:high]], axis=0)
            for channel in range(channels):
                coupling = jnp.concatenate([local[channel, block], remote[channel, block, 0]], axis=1)
                mix[low:high, channel * order:(channel + 1) * order] = product(coupling, rows).astype(BF16)
        for n in range(pieces):
            for load in beta_loads[i][n * channels:(n + 1) * channels]:
                load.wait()
            start_next()
            total = product_nt(beta[i, n], mix[...]).astype(BF16)
            stripe = out_buf.shape[4]
            for index in range(STRIPES):
                out_buf[i, n, index] = total[:, index * stripe:(index + 1) * stripe]
                target = out_refs[index].at[i, n]
                slot = (i * pieces + n) * STRIPES + index
                stores.append(pltpu.make_async_copy(out_buf.at[i, n, index], target, out_sems.at[slot]))
                stores[-1].start()
    for store in stores:
        store.wait()


def own_kernel(*refs):
    *in_refs, out_ref = refs
    stripe = in_refs[0].shape[3]
    for index, in_ref in enumerate(in_refs):
        out_ref[index * stripe:(index + 1) * stripe, :] = in_ref[0, 0].T


def collect_kernel(order_ref, *refs):
    *in_refs, out_ref, buf, in_sems, out_sems = refs
    in_refs = in_refs[:buf.shape[0]]
    loads = [pltpu.make_async_copy(ref, buf.at[at], in_sems.at[at]) for at, ref in enumerate(in_refs)]
    for load in loads:
        load.start()
    stores = []
    for at in range(len(in_refs)):
        loads[at].wait()
        stores.append(pltpu.make_async_copy(buf.at[at], out_ref.at[order_ref[at]], out_sems.at[at]))
        stores[-1].start()
    for store in stores:
        store.wait()


def pick_kernel(order_ref, in_ref, *refs):
    *out_refs, buf, in_sems, out_sems = refs
    count = len(out_refs)
    loads = [pltpu.make_async_copy(in_ref.at[order_ref[at]], buf.at[at], in_sems.at[at]) for at in range(count)]
    for load in loads:
        load.start()
    stores = []
    for at in range(count):
        loads[at].wait()
        stores.append(pltpu.make_async_copy(buf.at[at], out_refs[at], out_sems.at[at]))
        stores[-1].start()
    for store in stores:
        store.wait()


def final_kernel(turn_ref, *refs):
    own_buf, mirror_buf, out_buf, own_sems, mirror_sems, out_sems = refs[-6:]
    out_ref = refs[-7]
    chunks, row_count, width = own_buf.shape
    _, _, per_chunk, nc, piece, stripe = mirror_buf.shape
    own_refs, first_refs, second_ref = refs[:chunks], refs[chunks:chunks + STRIPES], refs[chunks + STRIPES]
    loads = []
    for chunk in (1, 0):
        for i in range(per_chunk):
            cols = slice(i * nc * piece, (i + 1) * nc * piece)
            source, target = own_refs[chunk].at[:, cols], own_buf.at[chunk, :, cols]
            group = [pltpu.make_async_copy(source, target, own_sems.at[chunk * per_chunk + i])]
            for j in range(STRIPES):
                if chunk:
                    z_flip = (turn_ref[6] + 1 + j // 2) & 1
                    source = second_ref.at[(turn_ref[5] + j) & (STRIPES - 1), (i + z_flip) & 1]
                else:
                    source = first_refs[j].at[i]
                slot = (chunk * per_chunk + i) * STRIPES + j
                group.append(pltpu.make_async_copy(source, mirror_buf.at[chunk, j, i], mirror_sems.at[slot]))
            for load in group:
                load.start()
            loads.append((chunk, i, group))
    stores = []
    for chunk, i, group in loads:
        for load in group:
            load.wait()
        for n in range(nc):
            slot = (chunk * per_chunk + i) * nc + n
            base = (i * nc + n) * piece
            for j in range(STRIPES):
                at = j if chunk else (2 * STRIPES + turn_ref[4] - j) & (STRIPES - 1)
                own_cols = pl.ds(pl.multiple_of(base + at * stripe, stripe), stripe)
                cols = pl.ds(pl.multiple_of(at * stripe, stripe), stripe)
                mirror = mirror_buf[chunk, j, i, n].astype(F32)
                out_buf[slot, :, cols] = (own_buf[chunk, :, own_cols].astype(F32) + mirror).astype(BF16)
            start = pl.multiple_of((turn_ref[chunk * per_chunk + i] * nc + n) * piece, piece)
            store = pltpu.make_async_copy(out_buf.at[slot], out_ref.at[:, pl.ds(start, piece)], out_sems.at[slot])
            store.start()
            stores.append(store)
    for store in stores:
        store.wait()


def params(mebibytes):
    return pltpu.CompilerParams(vmem_limit_bytes=mebibytes * 2**20)


def estimate(flops, mebibytes):
    return pl.CostEstimate(flops=flops, bytes_accessed=mebibytes * 2**20, transcendentals=0)


def device_pairs(sizes, move):
    nx, nz, nc, ny = sizes

    def at(x, z, core, y):
        return ((x % nx * nz + z % nz) * nc + core % nc) * ny + y % ny

    places = [(x, z, c, y) for x in range(nx) for z in range(nz) for c in range(nc) for y in range(ny)]
    return [(at(*place), at(*move(*place))) for place in places]


def prefetched(kernel, name, inputs, out_shape, scratch, flops, mebibytes, vmem=56, aliases={}):
    return pl.pallas_call(
        kernel,
        grid_spec=pltpu.PrefetchScalarGridSpec(
            num_scalar_prefetch=1,
            grid=(1,),
            in_specs=[pl.BlockSpec(memory_space=pl.ANY)] * inputs,
            out_specs=jax.tree.map(lambda _: pl.BlockSpec(memory_space=pl.ANY), out_shape),
            scratch_shapes=scratch,
        ),
        out_shape=out_shape,
        compiler_params=params(vmem),
        cost_estimate=estimate(flops, mebibytes),
        input_output_aliases=aliases,
        name=name,
    )


def on_device(sizes, coeffs, local_coupling, remote_coupling, beta_coupling, exc_rows):
    nx, nz, nc, ny = sizes
    owners = nx * nz * nc
    row_count, col_count = coeffs.shape
    channels, _, order, _ = beta_coupling.shape
    my_x, my_y, parity = lax.axis_index("x"), lax.axis_index("y"), lax.axis_index("zl")
    wanted = exc_rows.reshape(1, row_count)
    places = owners * CAP
    chunks, per_chunk = 2, nz // 2
    piece = order // nc
    stripe = row_count // STRIPES
    dma = pltpu.SemaphoreType.DMA

    table = pl.pallas_call(
        functools.partial(request_kernel, row_count, owners),
        out_shape=jax.ShapeDtypeStruct((owners, CAP), jnp.int32),
        name="requests",
    )(wanted)
    incoming = lax.all_to_all(table, ALPHA, split_axis=0, concat_axis=0, tiled=True)
    select = pl.pallas_call(
        functools.partial(select_kernel, row_count, owners),
        out_shape=jax.ShapeDtypeStruct((row_count, places), BF16),
        compiler_params=params(56),
        name="select",
    )(wanted)
    stripes = jnp.arange(STRIPES, dtype=jnp.int32)
    columns = [parity, 2 + parity, 1 - parity, 3 - parity]
    scalars = [*columns, (my_y - my_x) % STRIPES, (my_x + my_y) % STRIPES, parity]
    turn = jnp.stack(scalars).astype(jnp.int32)
    first_order = (my_y - stripes) % STRIPES
    second_order = (my_x - my_y - stripes) % STRIPES
    pick_order = (my_y + stripes) % STRIPES

    replies = []
    for chunk in range(chunks):
        outgoing = pl.pallas_call(
            functools.partial(outgoing_kernel, sizes, chunk),
            in_specs=[pl.BlockSpec(memory_space=pltpu.VMEM), pl.BlockSpec(memory_space=pl.ANY)],
            out_specs=pl.BlockSpec(memory_space=pl.ANY),
            out_shape=jax.ShapeDtypeStruct((nx, nz, nc, CAP, per_chunk * order), BF16),
            scratch_shapes=[
                pltpu.VMEM((places, row_count), BF16),
                pltpu.VMEM((nz, row_count, order), BF16),
                pltpu.VMEM((nz, 2, nx, nc, CAP, order), BF16),
                dma((nz,)),
                dma((nz * 2,)),
            ],
            compiler_params=params(56),
            cost_estimate=estimate(2 * 10**9, 10),
            name="outgoing",
        )(incoming, coeffs)
        outgoing = outgoing.reshape(owners, CAP, per_chunk * order)
        replies.append(lax.all_to_all(outgoing, ALPHA, split_axis=0, concat_axis=0, tiled=True))

    blocks_shape = jax.ShapeDtypeStruct((per_chunk, nc, piece, stripe), BF16)
    group_shape = jax.ShapeDtypeStruct((STRIPES, per_chunk, nc, piece, stripe), BF16)

    def half(chunk):
        scratch = [
            pltpu.VMEM((row_count, places), BF16),
            pltpu.VMEM(local_coupling.shape, BF16),
            pltpu.VMEM(remote_coupling.shape, BF16),
            pltpu.VMEM((per_chunk, row_count, order), BF16),
            pltpu.VMEM((per_chunk, owners, CAP, order), BF16),
            pltpu.VMEM((per_chunk, nc, piece, channels * order), BF16),
            pltpu.VMEM((row_count, channels * order), BF16),
            pltpu.VMEM((per_chunk, nc, STRIPES, piece, stripe), BF16),
            dma((3,)),
            dma((2 * per_chunk,)),
            dma((per_chunk, nc * channels)),
            dma((per_chunk * nc * STRIPES,)),
        ]
        call = prefetched(functools.partial(half_kernel, chunk), "half", 6, [blocks_shape] * STRIPES, scratch, 8 * 10**9, 18)
        return call(turn, select, local_coupling, remote_coupling, coeffs, replies[chunk], beta_coupling)

    def own(blocks_of):
        return pl.pallas_call(
            own_kernel,
            grid=(per_chunk, nc),
            in_specs=[pl.BlockSpec((1, 1, piece, stripe), lambda i, n: (i, n, 0, 0))] * STRIPES,
            out_specs=pl.BlockSpec((row_count, piece), lambda i, n: (0, i * nc + n)),
            out_shape=jax.ShapeDtypeStruct((row_count, per_chunk * order), BF16),
            compiler_params=params(56),
            cost_estimate=estimate(10**9, 4),
            name="own",
        )(*blocks_of)

    moving = [pltpu.VMEM(group_shape.shape, BF16), dma((STRIPES,)), dma((STRIPES,))]

    def exchange(arrays, to, base=None):
        count = len(arrays)
        scratch = [pltpu.VMEM((count, *group_shape.shape[1:]), BF16), dma((count,)), dma((count,))]
        if base is None:
            return prefetched(collect_kernel, "collect", count, group_shape, scratch, 0, count)(to, *arrays)
        call = prefetched(collect_kernel, "collect", count + 1, group_shape, scratch, 0, count, aliases={count + 1: 0})
        return call(to, *arrays, base)

    def all_near(grouped):
        grouped = grouped.reshape(nx * per_chunk * nc, piece, stripe)
        return lax.all_to_all(grouped, NEAR, split_axis=0, concat_axis=0, tiled=True).reshape(group_shape.shape)

    def permute(block, move):
        return lax.ppermute(block, DEVICES, device_pairs(sizes, move))

    def along_y(arrays):
        moved = {0: arrays[0]}
        for j in (1, 3, 2):
            moved[j] = permute(arrays[j], lambda x, z, c, y: (x, z, c, y + j))
        return [moved[j] for j in range(STRIPES)]

    first = half(0)
    spread = along_y(first)
    first_grouped = exchange(spread, first_order)
    replies[1], first_grouped = lax.optimization_barrier((replies[1], first_grouped))
    first_mirror = all_near(first_grouped)
    second = half(1)
    swapped = {}
    for j in (0, 2, 1, 3):
        step = 1 if j < 2 else -1
        swapped[j] = permute(second[j], lambda x, z, c, y: (x + y + j, z + step, c, x))
    picked = prefetched(pick_kernel, "pick", 1, [blocks_shape] * STRIPES, moving, 0, 4)(pick_order, first_mirror)
    early = lax.optimization_barrier((swapped[0], swapped[2], *picked))
    swapped[0], swapped[2], picked = early[0], early[1], early[2:]
    second_grouped = exchange([swapped[0], swapped[2]], second_order[0::2])
    second_grouped = exchange([swapped[1], swapped[3]], second_order[1::2], second_grouped)
    second_mirror = all_near(second_grouped)

    arrived = along_y(picked)

    scratch = [
        pltpu.VMEM((chunks, row_count, per_chunk * order), BF16),
        pltpu.VMEM((chunks, STRIPES, per_chunk, nc, piece, stripe), BF16),
        pltpu.VMEM((nz * nc, row_count, piece), BF16),
        dma((nz,)),
        dma((nz * STRIPES,)),
        dma((nz * nc,)),
    ]
    out_shape = jax.ShapeDtypeStruct((row_count, col_count), BF16)
    final = prefetched(final_kernel, "final", chunks + STRIPES + 1, out_shape, scratch, 10**7, 12, vmem=16)
    return final(turn, own(first), own(second), *arrived, second_mirror)


def solution(mesh):
    sizes = (4, 4, 2, 4)
    cube = Mesh(mesh.devices.reshape(4, 2, 2, 2, 4), DEVICES)
    return jax.shard_map(
        functools.partial(on_device, sizes),
        mesh=cube,
        in_specs=(
            P(ALPHA, "y"),
            P(None, ALPHA, None, None),
            P(None, ALPHA, None, None, None),
            P(None, "y", None, None),
            P(ALPHA, None, None),
        ),
        out_specs=P(ALPHA, "y"),
        check_vma=False,
    )
```

```python
import functools

import jax
import jax.numpy as jnp
from jax import lax
from jax.experimental import pallas as pl
from jax.experimental.pallas import tpu as pltpu
from jax.sharding import Mesh, PartitionSpec as P

ABLK = 256
CAP = 32
ALPHA = ("x", "zh", "zl", "core")
NEAR = ("x", "zh", "core")
DEVICES = ("x", "zh", "zl", "core", "y")
F32 = jnp.float32
BF16 = jnp.bfloat16
STRIPES = 4


def iota(shape, axis):
    return lax.broadcasted_iota(jnp.int32, shape, axis)


def split(value, size):
    return lax.shift_right_logical(value, jnp.int32(size.bit_length() - 1))


def product(a, b):
    return jnp.dot(a, b, preferred_element_type=F32)


def product_nt(a, b):
    return lax.dot_general(a, b, (((1,), (1,)), ((), ())), preferred_element_type=F32)


def slots(wanted, row_count, owners):
    entries = wanted.shape[1]
    owner = split(wanted, row_count)
    source_row = wanted & (row_count - 1)
    owner_hot = (iota((owners, entries), 0) == owner).astype(F32)
    before = (iota((entries, entries), 0) < iota((entries, entries), 1)).astype(F32)
    earlier = product(owner_hot.astype(BF16), before.astype(BF16))
    slot = jnp.sum(owner_hot * earlier, axis=0, keepdims=True).astype(jnp.int32)
    return owner, owner_hot, slot, source_row


def request_kernel(row_count, owners, wanted_ref, table_ref):
    owner, owner_hot, slot, source_row = slots(wanted_ref[...], row_count, owners)
    slot_hot = (iota((CAP, slot.shape[1]), 0) == slot).astype(F32).astype(BF16)
    high, low = split(source_row, 32), source_row & 31
    table = 32.0 * product_nt((owner_hot * high.astype(F32)).astype(BF16), slot_hot)
    table = table + product_nt((owner_hot * low.astype(F32)).astype(BF16), slot_hot)
    table_ref[...] = table.astype(jnp.int32)


def select_kernel(row_count, owners, wanted_ref, select_ref):
    owner, _, slot, _ = slots(wanted_ref[...], row_count, owners)
    entries = slot.shape[1]
    flat = (owner * CAP + slot).astype(F32)
    diagonal = iota((entries, entries), 0) == iota((entries, entries), 1)
    column = jnp.sum(jnp.where(diagonal, flat, 0.0), axis=1, keepdims=True).astype(jnp.int32)
    select_ref[...] = (iota((entries, owners * CAP), 1) == column).astype(F32).astype(BF16)


def outgoing_kernel(sizes, chunk, incoming_ref, coeffs_ref, out_ref, hot_ref, coeffs_buf, out_buf, in_sems, out_sems):
    nx, nz, nc, _ = sizes
    owners = nx * nz * nc
    row_count = coeffs_ref.shape[0]
    group = nx * nc * CAP
    order = coeffs_buf.shape[2]
    loads = []
    for k in range(nz):
        loads.append(pltpu.make_async_copy(coeffs_ref.at[:, k * order:(k + 1) * order], coeffs_buf.at[k], in_sems.at[k]))
    loads[0].start()
    loads[1].start()

    places = owners * CAP
    table = incoming_ref[...]
    high, low = split(table, 32), table & 31
    place = iota((places, owners), 0)
    by_z, by_x, by_core = split(place, group), split(place & (group - 1), nc * CAP), split(place & (nc * CAP - 1), CAP)
    owner = by_x * (nz * nc) + ((by_z & 1) * 2 + split(by_z, 2)) * nc + by_core
    place_owner = (owner == iota((places, owners), 1)).astype(F32).astype(BF16)
    spread = 32.0 * product(place_owner, high.astype(F32).astype(BF16))
    spread = spread + product(place_owner, low.astype(F32).astype(BF16))
    mine = (iota((places, CAP), 0) & (CAP - 1)) == iota((places, CAP), 1)
    column = jnp.sum(jnp.where(mine, spread, 0.0), axis=1, keepdims=True).astype(jnp.int32)
    hot_ref[...] = (iota((places, row_count), 1) == column).astype(F32).astype(BF16)

    stores = []
    for k in range(nz):
        loads[k].wait()
        if k + 2 < nz:
            loads[k + 2].start()
        parity = k % 2 ^ chunk
        rows = product(hot_ref[parity * 2 * group:(parity + 1) * 2 * group, :], coeffs_buf[k]).astype(BF16)
        out_buf[k] = rows.reshape(out_buf.shape[1:])
        for near in range(2):
            slot = k * 2 + near
            target = out_ref.at[:, near * 2 + parity, :, :, k // 2 * order:(k // 2 + 1) * order]
            stores.append(pltpu.make_async_copy(out_buf.at[k, near], target, out_sems.at[slot]))
            stores[-1].start()
    for store in stores:
        store.wait()


def half_kernel(chunk, turn_ref, select_ref, local_ref, remote_ref, coeffs_ref, replies_ref, beta_ref, *refs):
    out_refs = refs[:STRIPES]
    select, local, remote, coeffs, replies, beta, mix, out_buf, base_sems, in_sems, beta_sems, out_sems = refs[STRIPES:]
    channels, blocks = local.shape[:2]
    count, _, order = coeffs.shape
    pieces = out_buf.shape[1]
    piece = order // pieces

    base = [
        pltpu.make_async_copy(source, target, base_sems.at[at])
        for at, (source, target) in enumerate([(select_ref, select), (local_ref, local), (remote_ref, remote)])
    ]
    rows_loads, reply_loads, beta_loads = [], [], []
    for i in range(count):
        column = turn_ref[chunk * count + i]
        source = replies_ref.at[:, :, i * order:(i + 1) * order]
        reply_loads.append(pltpu.make_async_copy(source, replies.at[i], in_sems.at[i]))
        source = coeffs_ref.at[:, pl.ds(pl.multiple_of(column * order, order), order)]
        rows_loads.append(pltpu.make_async_copy(source, coeffs.at[i], in_sems.at[count + i]))
        group = []
        for n in range(pieces):
            for channel in range(channels):
                source = beta_ref.at[channel, column, n * piece:(n + 1) * piece]
                target = beta.at[i, n, :, channel * order:(channel + 1) * order]
                group.append(pltpu.make_async_copy(source, target, beta_sems.at[i, n * channels + channel]))
        beta_loads.append(group)
    waves = [[base[0], reply_loads[0]], [rows_loads[0], *base[1:]]]
    for i in range(count):
        if i:
            waves.append([reply_loads[i], rows_loads[i]])
        waves += [beta_loads[i][n * channels:(n + 1) * channels] for n in range(pieces)]

    def start_next():
        for load in waves.pop(0) if waves else []:
            load.start()

    for _ in range(3):
        start_next()
    base[0].wait()
    stores = []
    for i in range(count):
        reply_loads[i].wait()
        start_next()
        far_rows = product(select[...], replies[i].reshape(-1, order)).astype(BF16)
        rows_loads[i].wait()
        if i == 0:
            base[1].wait()
            base[2].wait()
            start_next()
        for block in range(blocks):
            low, high = block * ABLK, (block + 1) * ABLK
            rows = jnp.concatenate([coeffs[i, low:high, :], far_rows[low:high]], axis=0)
            for channel in range(channels):
                coupling = jnp.concatenate([local[channel, block], remote[channel, block, 0]], axis=1)
                mix[low:high, channel * order:(channel + 1) * order] = product(coupling, rows).astype(BF16)
        for n in range(pieces):
            for load in beta_loads[i][n * channels:(n + 1) * channels]:
                load.wait()
            start_next()
            total = product_nt(beta[i, n], mix[...]).astype(BF16)
            stripe = out_buf.shape[4]
            for index in range(STRIPES):
                out_buf[i, n, index] = total[:, index * stripe:(index + 1) * stripe]
                target = out_refs[index].at[i, n]
                slot = (i * pieces + n) * STRIPES + index
                stores.append(pltpu.make_async_copy(out_buf.at[i, n, index], target, out_sems.at[slot]))
                stores[-1].start()
    for store in stores:
        store.wait()


def own_kernel(*refs):
    *in_refs, out_ref = refs
    stripe = in_refs[0].shape[3]
    for index, in_ref in enumerate(in_refs):
        out_ref[index * stripe:(index + 1) * stripe, :] = in_ref[0, 0].T


def collect_kernel(order_ref, *refs):
    *in_refs, out_ref, buf, in_sems, out_sems = refs
    loads = [pltpu.make_async_copy(ref, buf.at[at], in_sems.at[at]) for at, ref in enumerate(in_refs)]
    for load in loads:
        load.start()
    stores = []
    for at in range(len(in_refs)):
        loads[at].wait()
        stores.append(pltpu.make_async_copy(buf.at[at], out_ref.at[order_ref[at]], out_sems.at[at]))
        stores[-1].start()
    for store in stores:
        store.wait()


def pick_kernel(order_ref, in_ref, *refs):
    *out_refs, buf, in_sems, out_sems = refs
    count = len(out_refs)
    loads = [pltpu.make_async_copy(in_ref.at[order_ref[at]], buf.at[at], in_sems.at[at]) for at in range(count)]
    for load in loads:
        load.start()
    stores = []
    for at in range(count):
        loads[at].wait()
        stores.append(pltpu.make_async_copy(buf.at[at], out_refs[at], out_sems.at[at]))
        stores[-1].start()
    for store in stores:
        store.wait()


def final_kernel(turn_ref, *refs):
    own_buf, mirror_buf, out_buf, own_sems, mirror_sems, out_sems = refs[-6:]
    out_ref = refs[-7]
    chunks, row_count, width = own_buf.shape
    _, _, per_chunk, nc, piece, stripe = mirror_buf.shape
    own_refs, first_refs, second_ref = refs[:chunks], refs[chunks:chunks + STRIPES], refs[chunks + STRIPES]
    loads = []
    for chunk in (1, 0):
        for i in range(per_chunk):
            cols = slice(i * nc * piece, (i + 1) * nc * piece)
            source, target = own_refs[chunk].at[:, cols], own_buf.at[chunk, :, cols]
            group = [pltpu.make_async_copy(source, target, own_sems.at[chunk * per_chunk + i])]
            for j in range(STRIPES):
                if chunk:
                    z_flip = (turn_ref[6] + 1 + j // 2) & 1
                    source = second_ref.at[(turn_ref[5] + j) & (STRIPES - 1), (i + z_flip) & 1]
                else:
                    source = first_refs[j].at[i]
                slot = (chunk * per_chunk + i) * STRIPES + j
                group.append(pltpu.make_async_copy(source, mirror_buf.at[chunk, j, i], mirror_sems.at[slot]))
            loads.append((chunk, i, group))
    for load in loads[0][2] + loads[1][2]:
        load.start()
    stores = []
    for at_load, (chunk, i, group) in enumerate(loads):
        for load in group:
            load.wait()
        for load in loads[at_load + 2][2] if at_load + 2 < len(loads) else []:
            load.start()
        for n in range(nc):
            slot = (chunk * per_chunk + i) * nc + n
            base = (i * nc + n) * piece
            for j in range(STRIPES):
                at = j if chunk else (2 * STRIPES + turn_ref[4] - j) & (STRIPES - 1)
                own_cols = pl.ds(pl.multiple_of(base + at * stripe, stripe), stripe)
                cols = pl.ds(pl.multiple_of(at * stripe, stripe), stripe)
                mirror = mirror_buf[chunk, j, i, n].astype(F32)
                out_buf[slot, :, cols] = (own_buf[chunk, :, own_cols].astype(F32) + mirror).astype(BF16)
            start = pl.multiple_of((turn_ref[chunk * per_chunk + i] * nc + n) * piece, piece)
            store = pltpu.make_async_copy(out_buf.at[slot], out_ref.at[:, pl.ds(start, piece)], out_sems.at[slot])
            store.start()
            stores.append(store)
    for store in stores:
        store.wait()


def params(mebibytes):
    return pltpu.CompilerParams(vmem_limit_bytes=mebibytes * 2**20)


def estimate(flops, mebibytes):
    return pl.CostEstimate(flops=flops, bytes_accessed=mebibytes * 2**20, transcendentals=0)


def device_pairs(sizes, move):
    nx, nz, nc, ny = sizes

    def at(x, z, core, y):
        return ((x % nx * nz + z % nz) * nc + core % nc) * ny + y % ny

    places = [(x, z, c, y) for x in range(nx) for z in range(nz) for c in range(nc) for y in range(ny)]
    return [(at(*place), at(*move(*place))) for place in places]


def prefetched(kernel, name, inputs, out_shape, scratch, flops, mebibytes, vmem=56, out_space=pl.ANY):
    return pl.pallas_call(
        kernel,
        grid_spec=pltpu.PrefetchScalarGridSpec(
            num_scalar_prefetch=1,
            grid=(1,),
            in_specs=[pl.BlockSpec(memory_space=pl.ANY)] * inputs,
            out_specs=jax.tree.map(lambda _: pl.BlockSpec(memory_space=out_space), out_shape),
            scratch_shapes=scratch,
        ),
        out_shape=out_shape,
        compiler_params=params(vmem),
        cost_estimate=estimate(flops, mebibytes),
        name=name,
    )


def on_device(sizes, coeffs, local_coupling, remote_coupling, beta_coupling, exc_rows):
    nx, nz, nc, ny = sizes
    owners = nx * nz * nc
    row_count, col_count = coeffs.shape
    channels, _, order, _ = beta_coupling.shape
    my_x, my_y, parity = lax.axis_index("x"), lax.axis_index("y"), lax.axis_index("zl")
    wanted = exc_rows.reshape(1, row_count)
    places = owners * CAP
    chunks, per_chunk = 2, nz // 2
    piece = order // nc
    stripe = row_count // STRIPES
    dma = pltpu.SemaphoreType.DMA

    table = pl.pallas_call(
        functools.partial(request_kernel, row_count, owners),
        out_shape=jax.ShapeDtypeStruct((owners, CAP), jnp.int32),
        name="requests",
    )(wanted)
    incoming = lax.all_to_all(table, ALPHA, split_axis=0, concat_axis=0, tiled=True)
    select = pl.pallas_call(
        functools.partial(select_kernel, row_count, owners),
        out_shape=jax.ShapeDtypeStruct((row_count, places), BF16),
        compiler_params=params(56),
        name="select",
    )(wanted)
    stripes = jnp.arange(STRIPES, dtype=jnp.int32)
    columns = [parity, 2 + parity, 1 - parity, 3 - parity]
    scalars = [*columns, (my_y - my_x) % STRIPES, (my_x + my_y) % STRIPES, parity]
    turn = jnp.stack(scalars).astype(jnp.int32)
    first_order = (my_y - stripes) % STRIPES
    second_order = (my_x - my_y - stripes) % STRIPES
    pick_order = (my_y + stripes) % STRIPES

    replies = []
    for chunk in range(chunks):
        outgoing = pl.pallas_call(
            functools.partial(outgoing_kernel, sizes, chunk),
            in_specs=[pl.BlockSpec(memory_space=pltpu.VMEM), pl.BlockSpec(memory_space=pl.ANY)],
            out_specs=pl.BlockSpec(memory_space=pl.ANY),
            out_shape=jax.ShapeDtypeStruct((nx, nz, nc, CAP, per_chunk * order), BF16),
            scratch_shapes=[
                pltpu.VMEM((places, row_count), BF16),
                pltpu.VMEM((nz, row_count, order), BF16),
                pltpu.VMEM((nz, 2, nx, nc, CAP, order), BF16),
                dma((nz,)),
                dma((nz * 2,)),
            ],
            compiler_params=params(56),
            cost_estimate=estimate(2 * 10**9, 10),
            name="outgoing",
        )(incoming, coeffs)
        outgoing = outgoing.reshape(owners, CAP, per_chunk * order)
        replies.append(lax.all_to_all(outgoing, ALPHA, split_axis=0, concat_axis=0, tiled=True))

    blocks_shape = jax.ShapeDtypeStruct((per_chunk, nc, piece, stripe), BF16)
    group_shape = jax.ShapeDtypeStruct((STRIPES, per_chunk, nc, piece, stripe), BF16)

    def half(chunk):
        scratch = [
            pltpu.VMEM((row_count, places), BF16),
            pltpu.VMEM(local_coupling.shape, BF16),
            pltpu.VMEM(remote_coupling.shape, BF16),
            pltpu.VMEM((per_chunk, row_count, order), BF16),
            pltpu.VMEM((per_chunk, owners, CAP, order), BF16),
            pltpu.VMEM((per_chunk, nc, piece, channels * order), BF16),
            pltpu.VMEM((row_count, channels * order), BF16),
            pltpu.VMEM((per_chunk, nc, STRIPES, piece, stripe), BF16),
            dma((3,)),
            dma((2 * per_chunk,)),
            dma((per_chunk, nc * channels)),
            dma((per_chunk * nc * STRIPES,)),
        ]
        call = prefetched(functools.partial(half_kernel, chunk), "half", 6, [blocks_shape] * STRIPES, scratch, 8 * 10**9, 18)
        return call(turn, select, local_coupling, remote_coupling, coeffs, replies[chunk], beta_coupling)

    def own(blocks_of):
        return pl.pallas_call(
            own_kernel,
            grid=(per_chunk, nc),
            in_specs=[pl.BlockSpec((1, 1, piece, stripe), lambda i, n: (i, n, 0, 0))] * STRIPES,
            out_specs=pl.BlockSpec((row_count, piece), lambda i, n: (0, i * nc + n)),
            out_shape=jax.ShapeDtypeStruct((row_count, per_chunk * order), BF16),
            compiler_params=params(56),
            cost_estimate=estimate(10**9, 4),
            name="own",
        )(*blocks_of)

    moving = [pltpu.VMEM(group_shape.shape, BF16), dma((STRIPES,)), dma((STRIPES,))]

    def exchange(arrays, to):
        grouped = prefetched(collect_kernel, "collect", STRIPES, group_shape, moving, 0, 4, 4, pltpu.HBM)(to, *arrays)
        return grouped

    def all_near(grouped):
        grouped = grouped.reshape(nx * per_chunk * nc, piece, stripe)
        return lax.all_to_all(grouped, NEAR, split_axis=0, concat_axis=0, tiled=True).reshape(group_shape.shape)

    def permute(block, move):
        return lax.ppermute(block, DEVICES, device_pairs(sizes, move))

    def along_y(arrays):
        moved = {0: arrays[0]}
        for j in (1, 3, 2):
            moved[j] = permute(arrays[j], lambda x, z, c, y: (x, z, c, y + j))
        return [moved[j] for j in range(STRIPES)]

    first = half(0)
    spread = along_y(first)
    first_grouped = exchange(spread, first_order)
    replies[1], first_grouped = lax.optimization_barrier((replies[1], first_grouped))
    first_mirror = all_near(first_grouped)
    second = half(1)
    swapped = {}
    for j in (0, 2, 1, 3):
        step = 1 if j < 2 else -1
        swapped[j] = permute(second[j], lambda x, z, c, y: (x + y + j, z + step, c, x))
    picked = prefetched(pick_kernel, "pick", 1, [blocks_shape] * STRIPES, moving, 0, 4, 4, pltpu.HBM)(pick_order, first_mirror)
    early = lax.optimization_barrier((swapped[0], swapped[2], *picked))
    swapped[0], swapped[2], picked = early[0], early[1], early[2:]
    second_mirror = all_near(exchange([swapped[j] for j in range(STRIPES)], second_order))

    arrived = along_y(picked)

    scratch = [
        pltpu.VMEM((chunks, row_count, per_chunk * order), BF16),
        pltpu.VMEM((chunks, STRIPES, per_chunk, nc, piece, stripe), BF16),
        pltpu.VMEM((nz * nc, row_count, piece), BF16),
        dma((nz,)),
        dma((nz * STRIPES,)),
        dma((nz * nc,)),
    ]
    out_shape = jax.ShapeDtypeStruct((row_count, col_count), BF16)
    final = prefetched(final_kernel, "final", chunks + STRIPES + 1, out_shape, scratch, 10**7, 12)
    return final(turn, own(first), own(second), *arrived, second_mirror)


def solution(mesh):
    sizes = (4, 4, 2, 4)
    cube = Mesh(mesh.devices.reshape(4, 2, 2, 2, 4), DEVICES)
    return jax.shard_map(
        functools.partial(on_device, sizes),
        mesh=cube,
        in_specs=(
            P(ALPHA, "y"),
            P(None, ALPHA, None, None),
            P(None, ALPHA, None, None, None),
            P(None, "y", None, None),
            P(ALPHA, None, None),
        ),
        out_specs=P(ALPHA, "y"),
        check_vma=False,
    )
```

```python
import functools

import jax
import jax.numpy as jnp
from jax import lax
from jax.experimental import pallas as pl
from jax.experimental.pallas import tpu as pltpu
from jax.sharding import Mesh, PartitionSpec as P

ABLK = 256
CAP = 32
ALPHA = ("x", "zh", "zl", "core")
NEAR = ("x", "zh", "core")
DEVICES = ("x", "zh", "zl", "core", "y")
F32 = jnp.float32
BF16 = jnp.bfloat16
STRIPES = 4


def iota(shape, axis):
    return lax.broadcasted_iota(jnp.int32, shape, axis)


def split(value, size):
    return lax.shift_right_logical(value, jnp.int32(size.bit_length() - 1))


def product(a, b):
    return jnp.dot(a, b, preferred_element_type=F32)


def product_nt(a, b):
    return lax.dot_general(a, b, (((1,), (1,)), ((), ())), preferred_element_type=F32)


def slots(wanted, row_count, owners):
    entries = wanted.shape[1]
    owner = split(wanted, row_count)
    source_row = wanted & (row_count - 1)
    owner_hot = (iota((owners, entries), 0) == owner).astype(F32)
    before = (iota((entries, entries), 0) < iota((entries, entries), 1)).astype(F32)
    earlier = product(owner_hot.astype(BF16), before.astype(BF16))
    slot = jnp.sum(owner_hot * earlier, axis=0, keepdims=True).astype(jnp.int32)
    return owner, owner_hot, slot, source_row


def request_kernel(row_count, owners, wanted_ref, table_ref):
    owner, owner_hot, slot, source_row = slots(wanted_ref[...], row_count, owners)
    slot_hot = (iota((CAP, slot.shape[1]), 0) == slot).astype(F32).astype(BF16)
    high, low = split(source_row, 32), source_row & 31
    table = 32.0 * product_nt((owner_hot * high.astype(F32)).astype(BF16), slot_hot)
    table = table + product_nt((owner_hot * low.astype(F32)).astype(BF16), slot_hot)
    table_ref[...] = table.astype(jnp.int32)


def select_kernel(row_count, owners, wanted_ref, select_ref):
    owner, _, slot, _ = slots(wanted_ref[...], row_count, owners)
    entries = slot.shape[1]
    flat = (owner * CAP + slot).astype(F32)
    diagonal = iota((entries, entries), 0) == iota((entries, entries), 1)
    column = jnp.sum(jnp.where(diagonal, flat, 0.0), axis=1, keepdims=True).astype(jnp.int32)
    select_ref[...] = (iota((entries, owners * CAP), 1) == column).astype(F32).astype(BF16)


def outgoing_kernel(sizes, chunk, incoming_ref, coeffs_ref, out_ref, hot_ref, coeffs_buf, out_buf, in_sems, out_sems):
    nx, nz, nc, _ = sizes
    owners = nx * nz * nc
    row_count = coeffs_ref.shape[0]
    group = nx * nc * CAP
    order = coeffs_buf.shape[2]
    loads = []
    for k in range(nz):
        loads.append(pltpu.make_async_copy(coeffs_ref.at[:, k * order:(k + 1) * order], coeffs_buf.at[k], in_sems.at[k]))
        loads[-1].start()

    places = owners * CAP
    table = incoming_ref[...]
    high, low = split(table, 32), table & 31
    place = iota((places, owners), 0)
    by_z, by_x, by_core = split(place, group), split(place & (group - 1), nc * CAP), split(place & (nc * CAP - 1), CAP)
    owner = by_x * (nz * nc) + ((by_z & 1) * 2 + split(by_z, 2)) * nc + by_core
    place_owner = (owner == iota((places, owners), 1)).astype(F32).astype(BF16)
    spread = 32.0 * product(place_owner, high.astype(F32).astype(BF16))
    spread = spread + product(place_owner, low.astype(F32).astype(BF16))
    mine = (iota((places, CAP), 0) & (CAP - 1)) == iota((places, CAP), 1)
    column = jnp.sum(jnp.where(mine, spread, 0.0), axis=1, keepdims=True).astype(jnp.int32)
    hot_ref[...] = (iota((places, row_count), 1) == column).astype(F32).astype(BF16)

    stores = []
    for k in range(nz):
        loads[k].wait()
        parity = k % 2 ^ chunk
        rows = product(hot_ref[parity * 2 * group:(parity + 1) * 2 * group, :], coeffs_buf[k]).astype(BF16)
        out_buf[k] = rows.reshape(out_buf.shape[1:])
        for near in range(2):
            slot = k * 2 + near
            target = out_ref.at[:, near * 2 + parity, :, :, k // 2 * order:(k // 2 + 1) * order]
            stores.append(pltpu.make_async_copy(out_buf.at[k, near], target, out_sems.at[slot]))
            stores[-1].start()
    for store in stores:
        store.wait()


def half_kernel(chunk, turn_ref, select_ref, local_ref, remote_ref, coeffs_ref, replies_ref, beta_ref, *refs):
    out_refs = refs[:STRIPES]
    select, local, remote, coeffs, replies, beta, mix, out_buf, base_sems, in_sems, beta_sems, out_sems = refs[STRIPES:]
    channels, blocks = local.shape[:2]
    count, _, order = coeffs.shape
    pieces = out_buf.shape[1]
    piece = order // pieces

    base = [
        pltpu.make_async_copy(source, target, base_sems.at[at])
        for at, (source, target) in enumerate([(select_ref, select), (local_ref, local), (remote_ref, remote)])
    ]
    rows_loads, reply_loads, beta_loads = [], [], []
    for i in range(count):
        column = turn_ref[chunk * count + i]
        source = replies_ref.at[:, :, i * order:(i + 1) * order]
        reply_loads.append(pltpu.make_async_copy(source, replies.at[i], in_sems.at[i]))
        source = coeffs_ref.at[:, pl.ds(pl.multiple_of(column * order, order), order)]
        rows_loads.append(pltpu.make_async_copy(source, coeffs.at[i], in_sems.at[count + i]))
        group = []
        for n in range(pieces):
            for channel in range(channels):
                source = beta_ref.at[channel, column, n * piece:(n + 1) * piece]
                target = beta.at[i, n, :, channel * order:(channel + 1) * order]
                group.append(pltpu.make_async_copy(source, target, beta_sems.at[i, n * channels + channel]))
        beta_loads.append(group)
    waves = [[base[0], reply_loads[0]], [rows_loads[0], *base[1:]]]
    for i in range(count):
        if i:
            waves.append([reply_loads[i], rows_loads[i]])
        waves += [beta_loads[i][n * channels:(n + 1) * channels] for n in range(pieces)]

    def start_next():
        for load in waves.pop(0) if waves else []:
            load.start()

    for _ in range(3):
        start_next()
    base[0].wait()
    stores = []
    for i in range(count):
        reply_loads[i].wait()
        start_next()
        far_rows = product(select[...], replies[i].reshape(-1, order)).astype(BF16)
        rows_loads[i].wait()
        if i == 0:
            base[1].wait()
            base[2].wait()
            start_next()
        for block in range(blocks):
            low, high = block * ABLK, (block + 1) * ABLK
            rows = jnp.concatenate([coeffs[i, low:high, :], far_rows[low:high]], axis=0)
            for channel in range(channels):
                coupling = jnp.concatenate([local[channel, block], remote[channel, block, 0]], axis=1)
                mix[low:high, channel * order:(channel + 1) * order] = product(coupling, rows).astype(BF16)
        for n in range(pieces):
            for load in beta_loads[i][n * channels:(n + 1) * channels]:
                load.wait()
            start_next()
            total = product_nt(beta[i, n], mix[...]).astype(BF16)
            stripe = out_buf.shape[4]
            for index in range(STRIPES):
                out_buf[i, n, index] = total[:, index * stripe:(index + 1) * stripe]
                target = out_refs[index].at[i, n]
                slot = (i * pieces + n) * STRIPES + index
                stores.append(pltpu.make_async_copy(out_buf.at[i, n, index], target, out_sems.at[slot]))
                stores[-1].start()
    for store in stores:
        store.wait()


def own_kernel(*refs):
    *in_refs, out_ref = refs
    stripe = in_refs[0].shape[3]
    for index, in_ref in enumerate(in_refs):
        out_ref[index * stripe:(index + 1) * stripe, :] = in_ref[0, 0].T


def collect_kernel(order_ref, *refs):
    *in_refs, out_ref, buf, in_sems, out_sems = refs
    loads = [pltpu.make_async_copy(ref, buf.at[at], in_sems.at[at]) for at, ref in enumerate(in_refs)]
    for load in loads:
        load.start()
    stores = []
    for at in range(len(in_refs)):
        loads[at].wait()
        stores.append(pltpu.make_async_copy(buf.at[at], out_ref.at[order_ref[at]], out_sems.at[at]))
        stores[-1].start()
    for store in stores:
        store.wait()


def pick_kernel(order_ref, in_ref, *refs):
    *out_refs, buf, in_sems, out_sems = refs
    count = len(out_refs)
    loads = [pltpu.make_async_copy(in_ref.at[order_ref[at]], buf.at[at], in_sems.at[at]) for at in range(count)]
    for load in loads:
        load.start()
    stores = []
    for at in range(count):
        loads[at].wait()
        stores.append(pltpu.make_async_copy(buf.at[at], out_refs[at], out_sems.at[at]))
        stores[-1].start()
    for store in stores:
        store.wait()


def final_kernel(turn_ref, *refs):
    own_buf, mirror_buf, out_buf, own_sems, mirror_sems, out_sems = refs[-6:]
    out_ref = refs[-7]
    chunks, row_count, width = own_buf.shape
    _, _, per_chunk, nc, piece, stripe = mirror_buf.shape
    own_refs, first_refs, second_ref = refs[:chunks], refs[chunks:chunks + STRIPES], refs[chunks + STRIPES]
    loads = []
    for chunk in (1, 0):
        for i in range(per_chunk):
            cols = slice(i * nc * piece, (i + 1) * nc * piece)
            source, target = own_refs[chunk].at[:, cols], own_buf.at[chunk, :, cols]
            group = [pltpu.make_async_copy(source, target, own_sems.at[chunk * per_chunk + i])]
            for j in range(STRIPES):
                if chunk:
                    z_flip = (turn_ref[6] + 1 + j // 2) & 1
                    source = second_ref.at[(turn_ref[5] + j) & (STRIPES - 1), (i + z_flip) & 1]
                else:
                    source = first_refs[j].at[i]
                slot = (chunk * per_chunk + i) * STRIPES + j
                group.append(pltpu.make_async_copy(source, mirror_buf.at[chunk, j, i], mirror_sems.at[slot]))
            for load in group:
                load.start()
            loads.append((chunk, i, group))
    stores = []
    for chunk, i, group in loads:
        for load in group:
            load.wait()
        for n in range(nc):
            slot = (chunk * per_chunk + i) * nc + n
            base = (i * nc + n) * piece
            for j in range(STRIPES):
                at = j if chunk else (2 * STRIPES + turn_ref[4] - j) & (STRIPES - 1)
                own_cols = pl.ds(pl.multiple_of(base + at * stripe, stripe), stripe)
                cols = pl.ds(pl.multiple_of(at * stripe, stripe), stripe)
                mirror = mirror_buf[chunk, j, i, n].astype(F32)
                out_buf[slot, :, cols] = (own_buf[chunk, :, own_cols].astype(F32) + mirror).astype(BF16)
            start = pl.multiple_of((turn_ref[chunk * per_chunk + i] * nc + n) * piece, piece)
            store = pltpu.make_async_copy(out_buf.at[slot], out_ref.at[:, pl.ds(start, piece)], out_sems.at[slot])
            store.start()
            stores.append(store)
    for store in stores:
        store.wait()


def params(mebibytes):
    return pltpu.CompilerParams(vmem_limit_bytes=mebibytes * 2**20)


def estimate(flops, mebibytes):
    return pl.CostEstimate(flops=flops, bytes_accessed=mebibytes * 2**20, transcendentals=0)


def device_pairs(sizes, move):
    nx, nz, nc, ny = sizes

    def at(x, z, core, y):
        return ((x % nx * nz + z % nz) * nc + core % nc) * ny + y % ny

    places = [(x, z, c, y) for x in range(nx) for z in range(nz) for c in range(nc) for y in range(ny)]
    return [(at(*place), at(*move(*place))) for place in places]


def prefetched(kernel, name, inputs, out_shape, scratch, flops, mebibytes, vmem=56):
    return pl.pallas_call(
        kernel,
        grid_spec=pltpu.PrefetchScalarGridSpec(
            num_scalar_prefetch=1,
            grid=(1,),
            in_specs=[pl.BlockSpec(memory_space=pl.ANY)] * inputs,
            out_specs=jax.tree.map(lambda _: pl.BlockSpec(memory_space=pl.ANY), out_shape),
            scratch_shapes=scratch,
        ),
        out_shape=out_shape,
        compiler_params=params(vmem),
        cost_estimate=estimate(flops, mebibytes),
        name=name,
    )


def on_device(sizes, coeffs, local_coupling, remote_coupling, beta_coupling, exc_rows):
    nx, nz, nc, ny = sizes
    owners = nx * nz * nc
    row_count, col_count = coeffs.shape
    channels, _, order, _ = beta_coupling.shape
    my_x, my_y, parity = lax.axis_index("x"), lax.axis_index("y"), lax.axis_index("zl")
    wanted = exc_rows.reshape(1, row_count)
    places = owners * CAP
    chunks, per_chunk = 2, nz // 2
    piece = order // nc
    stripe = row_count // STRIPES
    dma = pltpu.SemaphoreType.DMA

    table = pl.pallas_call(
        functools.partial(request_kernel, row_count, owners),
        out_shape=jax.ShapeDtypeStruct((owners, CAP), jnp.int32),
        name="requests",
    )(wanted)
    incoming = lax.all_to_all(table, ALPHA, split_axis=0, concat_axis=0, tiled=True)
    select = pl.pallas_call(
        functools.partial(select_kernel, row_count, owners),
        out_shape=jax.ShapeDtypeStruct((row_count, places), BF16),
        compiler_params=params(56),
        name="select",
    )(wanted)
    stripes = jnp.arange(STRIPES, dtype=jnp.int32)
    columns = [parity, 2 + parity, 1 - parity, 3 - parity]
    scalars = [*columns, (my_y - my_x) % STRIPES, (my_x + my_y) % STRIPES, parity]
    turn = jnp.stack(scalars).astype(jnp.int32)
    first_order = (my_y - stripes) % STRIPES
    second_order = (my_x - my_y - stripes) % STRIPES
    pick_order = (my_y + stripes) % STRIPES

    replies = []
    for chunk in range(chunks):
        outgoing = pl.pallas_call(
            functools.partial(outgoing_kernel, sizes, chunk),
            in_specs=[pl.BlockSpec(memory_space=pltpu.VMEM), pl.BlockSpec(memory_space=pl.ANY)],
            out_specs=pl.BlockSpec(memory_space=pl.ANY),
            out_shape=jax.ShapeDtypeStruct((nx, nz, nc, CAP, per_chunk * order), BF16),
            scratch_shapes=[
                pltpu.VMEM((places, row_count), BF16),
                pltpu.VMEM((nz, row_count, order), BF16),
                pltpu.VMEM((nz, 2, nx, nc, CAP, order), BF16),
                dma((nz,)),
                dma((nz * 2,)),
            ],
            compiler_params=params(56),
            cost_estimate=estimate(2 * 10**9, 10),
            name="outgoing",
        )(incoming, coeffs)
        outgoing = outgoing.reshape(owners, CAP, per_chunk * order)
        replies.append(lax.all_to_all(outgoing, ALPHA, split_axis=0, concat_axis=0, tiled=True))

    blocks_shape = jax.ShapeDtypeStruct((per_chunk, nc, piece, stripe), BF16)
    group_shape = jax.ShapeDtypeStruct((STRIPES, per_chunk, nc, piece, stripe), BF16)

    def half(chunk):
        scratch = [
            pltpu.VMEM((row_count, places), BF16),
            pltpu.VMEM(local_coupling.shape, BF16),
            pltpu.VMEM(remote_coupling.shape, BF16),
            pltpu.VMEM((per_chunk, row_count, order), BF16),
            pltpu.VMEM((per_chunk, owners, CAP, order), BF16),
            pltpu.VMEM((per_chunk, nc, piece, channels * order), BF16),
            pltpu.VMEM((row_count, channels * order), BF16),
            pltpu.VMEM((per_chunk, nc, STRIPES, piece, stripe), BF16),
            dma((3,)),
            dma((2 * per_chunk,)),
            dma((per_chunk, nc * channels)),
            dma((per_chunk * nc * STRIPES,)),
        ]
        call = prefetched(functools.partial(half_kernel, chunk), "half", 6, [blocks_shape] * STRIPES, scratch, 8 * 10**9, 18)
        return call(turn, select, local_coupling, remote_coupling, coeffs, replies[chunk], beta_coupling)

    def own(blocks_of):
        return pl.pallas_call(
            own_kernel,
            grid=(per_chunk, nc),
            in_specs=[pl.BlockSpec((1, 1, piece, stripe), lambda i, n: (i, n, 0, 0))] * STRIPES,
            out_specs=pl.BlockSpec((row_count, piece), lambda i, n: (0, i * nc + n)),
            out_shape=jax.ShapeDtypeStruct((row_count, per_chunk * order), BF16),
            compiler_params=params(56),
            cost_estimate=estimate(10**9, 4),
            name="own",
        )(*blocks_of)

    moving = [pltpu.VMEM(group_shape.shape, BF16), dma((STRIPES,)), dma((STRIPES,))]

    def exchange(arrays, to):
        grouped = prefetched(collect_kernel, "collect", STRIPES, group_shape, moving, 0, 4, 4)(to, *arrays)
        return grouped

    def all_near(grouped):
        grouped = grouped.reshape(nx * per_chunk * nc, piece, stripe)
        return lax.all_to_all(grouped, NEAR, split_axis=0, concat_axis=0, tiled=True).reshape(group_shape.shape)

    def permute(block, move):
        return lax.ppermute(block, DEVICES, device_pairs(sizes, move))

    def along_y(arrays):
        moved = {0: arrays[0]}
        for j in (1, 3, 2):
            moved[j] = permute(arrays[j], lambda x, z, c, y: (x, z, c, y + j))
        return [moved[j] for j in range(STRIPES)]

    first = half(0)
    spread = along_y(first)
    first_grouped = exchange(spread, first_order)
    replies[1], first_grouped = lax.optimization_barrier((replies[1], first_grouped))
    first_mirror = all_near(first_grouped)
    second = half(1)
    swapped = {}
    for j in (0, 2, 1, 3):
        step = 1 if j < 2 else -1
        swapped[j] = permute(second[j], lambda x, z, c, y: (x + y + j, z + step, c, x))
    picked = prefetched(pick_kernel, "pick", 1, [blocks_shape] * STRIPES, moving, 0, 4, 4)(pick_order, first_mirror)
    early = lax.optimization_barrier((swapped[0], swapped[2], *picked))
    swapped[0], swapped[2], picked = early[0], early[1], early[2:]
    second_mirror = all_near(exchange([swapped[j] for j in range(STRIPES)], second_order))

    arrived = along_y(picked)

    scratch = [
        pltpu.VMEM((chunks, row_count, per_chunk * order), BF16),
        pltpu.VMEM((chunks, STRIPES, per_chunk, nc, piece, stripe), BF16),
        pltpu.VMEM((nz * nc, row_count, piece), BF16),
        dma((nz,)),
        dma((nz * STRIPES,)),
        dma((nz * nc,)),
    ]
    out_shape = jax.ShapeDtypeStruct((row_count, col_count), BF16)
    final = prefetched(final_kernel, "final", chunks + STRIPES + 1, out_shape, scratch, 10**7, 12)
    return final(turn, own(first), own(second), *arrived, second_mirror)


def solution(mesh):
    sizes = (4, 4, 2, 4)
    cube = Mesh(mesh.devices.reshape(4, 2, 2, 2, 4), DEVICES)
    return jax.shard_map(
        functools.partial(on_device, sizes),
        mesh=cube,
        in_specs=(
            P(ALPHA, "y"),
            P(None, ALPHA, None, None),
            P(None, ALPHA, None, None, None),
            P(None, "y", None, None),
            P(ALPHA, None, None),
        ),
        out_specs=P(ALPHA, "y"),
        check_vma=False,
    )
```

```python
import functools

import jax
import jax.numpy as jnp
from jax import lax
from jax.experimental import pallas as pl
from jax.experimental.pallas import tpu as pltpu
from jax.sharding import Mesh, PartitionSpec as P

ABLK = 256
CAP = 32
ALPHA = ("x", "zh", "zl", "core")
NEAR = ("x", "zh", "core")
DEVICES = ("x", "zh", "zl", "core", "y")
F32 = jnp.float32
BF16 = jnp.bfloat16
STRIPES = 4


def iota(shape, axis):
    return lax.broadcasted_iota(jnp.int32, shape, axis)


def split(value, size):
    return lax.shift_right_logical(value, jnp.int32(size.bit_length() - 1))


def product(a, b):
    return jnp.dot(a, b, preferred_element_type=F32)


def product_nt(a, b):
    return lax.dot_general(a, b, (((1,), (1,)), ((), ())), preferred_element_type=F32)


def slots(wanted, row_count, owners):
    entries = wanted.shape[1]
    owner = split(wanted, row_count)
    source_row = wanted & (row_count - 1)
    owner_hot = (iota((owners, entries), 0) == owner).astype(F32)
    before = (iota((entries, entries), 0) < iota((entries, entries), 1)).astype(F32)
    earlier = product(owner_hot.astype(BF16), before.astype(BF16))
    slot = jnp.sum(owner_hot * earlier, axis=0, keepdims=True).astype(jnp.int32)
    return owner, owner_hot, slot, source_row


def request_kernel(row_count, owners, wanted_ref, table_ref):
    owner, owner_hot, slot, source_row = slots(wanted_ref[...], row_count, owners)
    slot_hot = (iota((CAP, slot.shape[1]), 0) == slot).astype(F32).astype(BF16)
    high, low = split(source_row, 32), source_row & 31
    table = 32.0 * product_nt((owner_hot * high.astype(F32)).astype(BF16), slot_hot)
    table = table + product_nt((owner_hot * low.astype(F32)).astype(BF16), slot_hot)
    table_ref[...] = table.astype(jnp.int32)


def select_kernel(row_count, owners, wanted_ref, select_ref):
    owner, _, slot, _ = slots(wanted_ref[...], row_count, owners)
    entries = slot.shape[1]
    flat = (owner * CAP + slot).astype(F32)
    diagonal = iota((entries, entries), 0) == iota((entries, entries), 1)
    column = jnp.sum(jnp.where(diagonal, flat, 0.0), axis=1, keepdims=True).astype(jnp.int32)
    select_ref[...] = (iota((entries, owners * CAP), 1) == column).astype(F32).astype(BF16)


def outgoing_kernel(sizes, chunk, incoming_ref, coeffs_ref, out_ref, hot_ref, coeffs_buf, out_buf, in_sems, out_sems):
    nx, nz, nc, _ = sizes
    owners = nx * nz * nc
    row_count = coeffs_ref.shape[0]
    group = nx * nc * CAP
    order = coeffs_buf.shape[2]
    loads = []
    for k in range(nz):
        loads.append(pltpu.make_async_copy(coeffs_ref.at[:, k * order:(k + 1) * order], coeffs_buf.at[k], in_sems.at[k]))
        loads[-1].start()

    places = owners * CAP
    table = incoming_ref[...]
    high, low = split(table, 32), table & 31
    place = iota((places, owners), 0)
    by_z, by_x, by_core = split(place, group), split(place & (group - 1), nc * CAP), split(place & (nc * CAP - 1), CAP)
    owner = by_x * (nz * nc) + ((by_z & 1) * 2 + split(by_z, 2)) * nc + by_core
    place_owner = (owner == iota((places, owners), 1)).astype(F32).astype(BF16)
    spread = 32.0 * product(place_owner, high.astype(F32).astype(BF16))
    spread = spread + product(place_owner, low.astype(F32).astype(BF16))
    mine = (iota((places, CAP), 0) & (CAP - 1)) == iota((places, CAP), 1)
    column = jnp.sum(jnp.where(mine, spread, 0.0), axis=1, keepdims=True).astype(jnp.int32)
    hot_ref[...] = (iota((places, row_count), 1) == column).astype(F32).astype(BF16)

    stores = []
    for k in range(nz):
        loads[k].wait()
        parity = k % 2 ^ chunk
        rows = product(hot_ref[parity * 2 * group:(parity + 1) * 2 * group, :], coeffs_buf[k]).astype(BF16)
        out_buf[k] = rows.reshape(out_buf.shape[1:])
        for near in range(2):
            slot = k * 2 + near
            target = out_ref.at[:, near * 2 + parity, :, :, k // 2 * order:(k // 2 + 1) * order]
            stores.append(pltpu.make_async_copy(out_buf.at[k, near], target, out_sems.at[slot]))
            stores[-1].start()
    for store in stores:
        store.wait()


def half_kernel(chunk, turn_ref, select_ref, local_ref, remote_ref, coeffs_ref, replies_ref, beta_ref, *refs):
    out_refs = refs[:STRIPES]
    select, local, remote, coeffs, replies, beta, mix, out_buf, base_sems, in_sems, beta_sems, out_sems = refs[STRIPES:]
    channels, blocks = local.shape[:2]
    count, _, order = coeffs.shape
    pieces = out_buf.shape[1]
    piece = order // pieces

    base = [
        pltpu.make_async_copy(source, target, base_sems.at[at])
        for at, (source, target) in enumerate([(select_ref, select), (local_ref, local), (remote_ref, remote)])
    ]
    rows_loads, reply_loads, beta_loads = [], [], []
    for i in range(count):
        column = turn_ref[chunk * count + i]
        source = replies_ref.at[:, :, i * order:(i + 1) * order]
        reply_loads.append(pltpu.make_async_copy(source, replies.at[i], in_sems.at[i]))
        source = coeffs_ref.at[:, pl.ds(pl.multiple_of(column * order, order), order)]
        rows_loads.append(pltpu.make_async_copy(source, coeffs.at[i], in_sems.at[count + i]))
        group = []
        for n in range(pieces):
            for channel in range(channels):
                source = beta_ref.at[channel, column, n * piece:(n + 1) * piece]
                target = beta.at[i, n, :, channel * order:(channel + 1) * order]
                group.append(pltpu.make_async_copy(source, target, beta_sems.at[i, n * channels + channel]))
        beta_loads.append(group)
    waves = [[base[0], reply_loads[0]], [rows_loads[0], *base[1:]]]
    for i in range(count):
        if i:
            waves.append([reply_loads[i], rows_loads[i]])
        waves += [beta_loads[i][n * channels:(n + 1) * channels] for n in range(pieces)]

    def start_next():
        for load in waves.pop(0) if waves else []:
            load.start()

    for _ in range(3):
        start_next()
    base[0].wait()
    stores = []
    for i in range(count):
        reply_loads[i].wait()
        start_next()
        far_rows = product(select[...], replies[i].reshape(-1, order)).astype(BF16)
        rows_loads[i].wait()
        if i == 0:
            base[1].wait()
            base[2].wait()
            start_next()
        for block in range(blocks):
            low, high = block * ABLK, (block + 1) * ABLK
            rows = jnp.concatenate([coeffs[i, low:high, :], far_rows[low:high]], axis=0)
            for channel in range(channels):
                coupling = jnp.concatenate([local[channel, block], remote[channel, block, 0]], axis=1)
                mix[low:high, channel * order:(channel + 1) * order] = product(coupling, rows).astype(BF16)
        for n in range(pieces):
            for load in beta_loads[i][n * channels:(n + 1) * channels]:
                load.wait()
            start_next()
            total = product_nt(beta[i, n], mix[...]).astype(BF16)
            stripe = out_buf.shape[4]
            for index in range(STRIPES):
                out_buf[i, n, index] = total[:, index * stripe:(index + 1) * stripe]
                target = out_refs[index].at[i, n]
                slot = (i * pieces + n) * STRIPES + index
                stores.append(pltpu.make_async_copy(out_buf.at[i, n, index], target, out_sems.at[slot]))
                stores[-1].start()
    for store in stores:
        store.wait()


def own_kernel(*refs):
    *in_refs, out_ref = refs
    stripe = in_refs[0].shape[3]
    for index, in_ref in enumerate(in_refs):
        out_ref[index * stripe:(index + 1) * stripe, :] = in_ref[0, 0].T


def collect_kernel(order_ref, *refs):
    *in_refs, out_ref, buf, in_sems, out_sems = refs
    loads = [pltpu.make_async_copy(ref, buf.at[at], in_sems.at[at]) for at, ref in enumerate(in_refs)]
    for load in loads:
        load.start()
    stores = []
    for at in range(len(in_refs)):
        loads[at].wait()
        stores.append(pltpu.make_async_copy(buf.at[at], out_ref.at[order_ref[at]], out_sems.at[at]))
        stores[-1].start()
    for store in stores:
        store.wait()


def pick_kernel(order_ref, in_ref, *refs):
    *out_refs, buf, in_sems, out_sems = refs
    count = len(out_refs)
    loads = [pltpu.make_async_copy(in_ref.at[order_ref[at]], buf.at[at], in_sems.at[at]) for at in range(count)]
    for load in loads:
        load.start()
    stores = []
    for at in range(count):
        loads[at].wait()
        stores.append(pltpu.make_async_copy(buf.at[at], out_refs[at], out_sems.at[at]))
        stores[-1].start()
    for store in stores:
        store.wait()


def final_kernel(turn_ref, *refs):
    own_buf, mirror_buf, out_buf, own_sems, mirror_sems, out_sems = refs[-6:]
    out_ref = refs[-7]
    chunks, row_count, width = own_buf.shape
    _, _, per_chunk, nc, piece, stripe = mirror_buf.shape
    own_refs, first_refs, second_ref = refs[:chunks], refs[chunks:chunks + STRIPES], refs[chunks + STRIPES]
    loads = []
    for chunk in (1, 0):
        for i in range(per_chunk):
            cols = slice(i * nc * piece, (i + 1) * nc * piece)
            source, target = own_refs[chunk].at[:, cols], own_buf.at[chunk, :, cols]
            group = [pltpu.make_async_copy(source, target, own_sems.at[chunk * per_chunk + i])]
            for j in range(STRIPES):
                if chunk:
                    z_flip = (turn_ref[6] + 1 + j // 2) & 1
                    source = second_ref.at[(turn_ref[5] + j) & (STRIPES - 1), (i + z_flip) & 1]
                else:
                    source = first_refs[j].at[i]
                slot = (chunk * per_chunk + i) * STRIPES + j
                group.append(pltpu.make_async_copy(source, mirror_buf.at[chunk, j, i], mirror_sems.at[slot]))
            for load in group:
                load.start()
            loads.append((chunk, i, group))
    stores = []
    for chunk, i, group in loads:
        for load in group:
            load.wait()
        for n in range(nc):
            slot = (chunk * per_chunk + i) * nc + n
            base = (i * nc + n) * piece
            for j in range(STRIPES):
                at = j if chunk else (2 * STRIPES + turn_ref[4] - j) & (STRIPES - 1)
                own_cols = pl.ds(pl.multiple_of(base + at * stripe, stripe), stripe)
                cols = pl.ds(pl.multiple_of(at * stripe, stripe), stripe)
                mirror = mirror_buf[chunk, j, i, n].astype(F32)
                out_buf[slot, :, cols] = (own_buf[chunk, :, own_cols].astype(F32) + mirror).astype(BF16)
            start = pl.multiple_of((turn_ref[chunk * per_chunk + i] * nc + n) * piece, piece)
            store = pltpu.make_async_copy(out_buf.at[slot], out_ref.at[:, pl.ds(start, piece)], out_sems.at[slot])
            store.start()
            stores.append(store)
    for store in stores:
        store.wait()


def params(mebibytes):
    return pltpu.CompilerParams(vmem_limit_bytes=mebibytes * 2**20)


def estimate(flops, mebibytes):
    return pl.CostEstimate(flops=flops, bytes_accessed=mebibytes * 2**20, transcendentals=0)


def device_pairs(sizes, move):
    nx, nz, nc, ny = sizes

    def at(x, z, core, y):
        return ((x % nx * nz + z % nz) * nc + core % nc) * ny + y % ny

    places = [(x, z, c, y) for x in range(nx) for z in range(nz) for c in range(nc) for y in range(ny)]
    return [(at(*place), at(*move(*place))) for place in places]


def prefetched(kernel, name, inputs, out_shape, scratch, flops, mebibytes, vmem=56):
    return pl.pallas_call(
        kernel,
        grid_spec=pltpu.PrefetchScalarGridSpec(
            num_scalar_prefetch=1,
            grid=(1,),
            in_specs=[pl.BlockSpec(memory_space=pl.ANY)] * inputs,
            out_specs=jax.tree.map(lambda _: pl.BlockSpec(memory_space=pl.ANY), out_shape),
            scratch_shapes=scratch,
        ),
        out_shape=out_shape,
        compiler_params=params(vmem),
        cost_estimate=estimate(flops, mebibytes),
        name=name,
    )


def on_device(sizes, coeffs, local_coupling, remote_coupling, beta_coupling, exc_rows):
    nx, nz, nc, ny = sizes
    owners = nx * nz * nc
    row_count, col_count = coeffs.shape
    channels, _, order, _ = beta_coupling.shape
    my_x, my_y, parity = lax.axis_index("x"), lax.axis_index("y"), lax.axis_index("zl")
    wanted = exc_rows.reshape(1, row_count)
    places = owners * CAP
    chunks, per_chunk = 2, nz // 2
    piece = order // nc
    stripe = row_count // STRIPES
    dma = pltpu.SemaphoreType.DMA

    table = pl.pallas_call(
        functools.partial(request_kernel, row_count, owners),
        out_shape=jax.ShapeDtypeStruct((owners, CAP), jnp.int32),
        name="requests",
    )(wanted)
    incoming = lax.all_to_all(table, ALPHA, split_axis=0, concat_axis=0, tiled=True)
    select = pl.pallas_call(
        functools.partial(select_kernel, row_count, owners),
        out_shape=jax.ShapeDtypeStruct((row_count, places), BF16),
        compiler_params=params(56),
        name="select",
    )(wanted)
    stripes = jnp.arange(STRIPES, dtype=jnp.int32)
    columns = [parity, 2 + parity, 1 - parity, 3 - parity]
    scalars = [*columns, (my_y - my_x) % STRIPES, (my_x + my_y) % STRIPES, parity]
    turn = jnp.stack(scalars).astype(jnp.int32)
    first_order = (my_y - stripes) % STRIPES
    second_order = (my_x - my_y - stripes) % STRIPES
    pick_order = (my_y + stripes) % STRIPES

    replies = []
    for chunk in range(chunks):
        outgoing = pl.pallas_call(
            functools.partial(outgoing_kernel, sizes, chunk),
            in_specs=[pl.BlockSpec(memory_space=pltpu.VMEM), pl.BlockSpec(memory_space=pl.ANY)],
            out_specs=pl.BlockSpec(memory_space=pl.ANY),
            out_shape=jax.ShapeDtypeStruct((nx, nz, nc, CAP, per_chunk * order), BF16),
            scratch_shapes=[
                pltpu.VMEM((places, row_count), BF16),
                pltpu.VMEM((nz, row_count, order), BF16),
                pltpu.VMEM((nz, 2, nx, nc, CAP, order), BF16),
                dma((nz,)),
                dma((nz * 2,)),
            ],
            compiler_params=params(56),
            cost_estimate=estimate(2 * 10**9, 10),
            name="outgoing",
        )(incoming, coeffs)
        outgoing = outgoing.reshape(owners, CAP, per_chunk * order)
        replies.append(lax.all_to_all(outgoing, ALPHA, split_axis=0, concat_axis=0, tiled=True))

    blocks_shape = jax.ShapeDtypeStruct((per_chunk, nc, piece, stripe), BF16)
    group_shape = jax.ShapeDtypeStruct((STRIPES, per_chunk, nc, piece, stripe), BF16)

    def half(chunk):
        scratch = [
            pltpu.VMEM((row_count, places), BF16),
            pltpu.VMEM(local_coupling.shape, BF16),
            pltpu.VMEM(remote_coupling.shape, BF16),
            pltpu.VMEM((per_chunk, row_count, order), BF16),
            pltpu.VMEM((per_chunk, owners, CAP, order), BF16),
            pltpu.VMEM((per_chunk, nc, piece, channels * order), BF16),
            pltpu.VMEM((row_count, channels * order), BF16),
            pltpu.VMEM((per_chunk, nc, STRIPES, piece, stripe), BF16),
            dma((3,)),
            dma((2 * per_chunk,)),
            dma((per_chunk, nc * channels)),
            dma((per_chunk * nc * STRIPES,)),
        ]
        call = prefetched(functools.partial(half_kernel, chunk), "half", 6, [blocks_shape] * STRIPES, scratch, 8 * 10**9, 18)
        return call(turn, select, local_coupling, remote_coupling, coeffs, replies[chunk], beta_coupling)

    def own(blocks_of):
        return pl.pallas_call(
            own_kernel,
            grid=(per_chunk, nc),
            in_specs=[pl.BlockSpec((1, 1, piece, stripe), lambda i, n: (i, n, 0, 0))] * STRIPES,
            out_specs=pl.BlockSpec((row_count, piece), lambda i, n: (0, i * nc + n)),
            out_shape=jax.ShapeDtypeStruct((row_count, per_chunk * order), BF16),
            compiler_params=params(56),
            cost_estimate=estimate(10**9, 4),
            name="own",
        )(*blocks_of)

    moving = [pltpu.VMEM(group_shape.shape, BF16), dma((STRIPES,)), dma((STRIPES,))]

    def exchange(arrays, to):
        grouped = prefetched(collect_kernel, "collect", STRIPES, group_shape, moving, 0, 4, 4)(to, *arrays)
        return grouped

    def all_near(grouped):
        grouped = grouped.reshape(nx * per_chunk * nc, piece, stripe)
        return lax.all_to_all(grouped, NEAR, split_axis=0, concat_axis=0, tiled=True).reshape(group_shape.shape)

    def permute(block, move):
        return lax.ppermute(block, DEVICES, device_pairs(sizes, move))

    def along_y(arrays):
        moved = {0: arrays[0]}
        for j in (1, 3, 2):
            moved[j] = permute(arrays[j], lambda x, z, c, y: (x, z, c, y + j))
        return [moved[j] for j in range(STRIPES)]

    first = half(0)
    spread = along_y(first)
    first_grouped = exchange(spread, first_order)
    replies[1], first_grouped = lax.optimization_barrier((replies[1], first_grouped))
    first_mirror = all_near(first_grouped)
    second = half(1)
    swapped = {}
    for j in (0, 2, 1, 3):
        step = 1 if j < 2 else -1
        swapped[j] = permute(second[j], lambda x, z, c, y: (x + y + j, z + step, c, x))
    picked = prefetched(pick_kernel, "pick", 1, [blocks_shape] * STRIPES, moving, 0, 4, 4)(pick_order, first_mirror)
    early = lax.optimization_barrier((swapped[0], swapped[2], *picked))
    swapped[0], swapped[2] = early[0], early[1]
    second_mirror = all_near(exchange([swapped[j] for j in range(STRIPES)], second_order))

    arrived = along_y(picked)

    scratch = [
        pltpu.VMEM((chunks, row_count, per_chunk * order), BF16),
        pltpu.VMEM((chunks, STRIPES, per_chunk, nc, piece, stripe), BF16),
        pltpu.VMEM((nz * nc, row_count, piece), BF16),
        dma((nz,)),
        dma((nz * STRIPES,)),
        dma((nz * nc,)),
    ]
    out_shape = jax.ShapeDtypeStruct((row_count, col_count), BF16)
    final = prefetched(final_kernel, "final", chunks + STRIPES + 1, out_shape, scratch, 10**7, 12)
    return final(turn, own(first), own(second), *arrived, second_mirror)


def solution(mesh):
    sizes = (4, 4, 2, 4)
    cube = Mesh(mesh.devices.reshape(4, 2, 2, 2, 4), DEVICES)
    return jax.shard_map(
        functools.partial(on_device, sizes),
        mesh=cube,
        in_specs=(
            P(ALPHA, "y"),
            P(None, ALPHA, None, None),
            P(None, ALPHA, None, None, None),
            P(None, "y", None, None),
            P(ALPHA, None, None),
        ),
        out_specs=P(ALPHA, "y"),
        check_vma=False,
    )
```
